128 devices in a mesh: row: 8 (over y_lo, x), col: 16 (over y_hi, z, core).
Axes of the slice: x: 4, y: 4 (y_hi: 2, y_lo: 2; y = y_hi * 2 + y_lo), z: 4, core: 2. Of those that a mesh axis runs over, the one named last changes fastest.
Arguments:
- pair_tensor: bfloat16 [2048, 2048, 128], P('row', 'col'), may hold values from -6 to 6
- token_single: bfloat16 [2048, 768], P('row'), may hold values from -6 to 6
- atom_single: bfloat16 [16384, 128], P(('row', 'col')), may hold values from -6 to 6
- atom_token: int32 [16384], replicated, may hold values from 0 to 2047, as said below
- chain_index: int32 [2048], replicated, may hold values from 0 to 15, never falling along the last dimension, each value on 1 to 512 neighbouring positions
- pair_up: bfloat16 [128, 512], replicated, may hold values from -0.5 to 0.5
- pair_down: bfloat16 [256, 128], replicated, may hold values from -0.75 to 0.75
- bias_heads: bfloat16 [128, 20], replicated, may hold values from -0.5 to 0.5
- atom_gain: float32 [128], replicated, may hold values from 0.1 to 1.9
- atom_proj: bfloat16 [128, 512], replicated, may hold values from -0.5 to 0.5
- atom_exit: bfloat16 [128, 128], replicated, may hold values from -0.5 to 0.5
- atom_pool: bfloat16 [128, 768], replicated, may hold values from -0.5 to 0.5
- token_gain: float32 [768], replicated, may hold values from 0.1 to 1.9
- token_proj: bfloat16 [768, 3072], replicated, may hold values from -0.21875 to 0.21875
- token_exit: bfloat16 [768, 768], replicated, may hold values from -0.21875 to 0.21875
- chain_bias: float32 [16], replicated, may hold values from -2 to 115
- token_back: bfloat16 [768, 128], replicated, may hold values from -0.21875 to 0.21875
Outputs:
- token_update: bfloat16 [2048, 768], P('row')
- atom_update: bfloat16 [16384, 128], P(('row', 'col'))
The draws below stay inside these ranges and needn't reach their ends.
Inputs may be any that keep to these rules, and one draw needn't show every extreme that they name: `atom_token`: Non-decreasing. For every r, the atoms r * 8 * 256 to (r + 1) * 8 * 256 - 1 belong to the tokens r * 256 to (r + 1) * 256 - 1, and every token has one atom or more.
All inputs are finite; a program needn't handle non-finite values.
Results may differ from the reference program's by a relative error of at most 0.0085.
Values may be sent and summed in bfloat16 or wider, within the bound.
No kernel may reach another device: no remote copies, remote signals or barrier semaphores. Data moves between devices by JAX's collectives and lax.ppermute only.
A program may use at most 128 MiB of HBM per device.

```python
import math
import jax
import jax.numpy as jnp
import numpy as np
from jax import lax

CZ = 128
CS = 768
CA = 128
HT = 16
HA = 4
PH = 256
QB = 32
KW = 128
APT = 8
CHAINS = 16
TOK_R = 256
TOKENS = 2048
ATOMS = 16384
EDGE = 48
HDA = 32
HDT = 48
HB = 20


def draw_atom_token(key, part):
    key = jax.random.fold_in(key, 11)
    groups = TOKENS // TOK_R
    spare = APT * TOK_R - TOK_R
    key_one, key_two, key_three = jax.random.split(key, 3)
    first_pick = jax.random.randint(key_one, (groups, spare), 0, TOK_R)
    second_pick = jax.random.randint(key_two, (groups, spare), 0, TOK_R)
    coin_flip = jax.random.randint(key_three, (groups, spare), 0, 2)
    extra = jnp.where(coin_flip == 1, jnp.minimum(first_pick, second_pick), first_pick).astype(jnp.int32)
    base_tokens = jnp.broadcast_to(jnp.arange(TOK_R, dtype=jnp.int32)[None, :], (groups, TOK_R))
    local_tokens = jnp.sort(jnp.concatenate([base_tokens, extra], axis=1), axis=1)
    offsets = (jnp.arange(groups, dtype=jnp.int32) * TOK_R)[:, None]
    return (local_tokens + offsets).reshape(-1).astype(jnp.int32)


def chain_values(key, big_lo, big_hi):
    key_order, key_small, key_big = jax.random.split(key, 3)
    order = jax.random.permutation(key_order, HT)
    strong = order < HT // 2
    small_part = jax.random.uniform(key_small, (HT,), jnp.float32, -2.0, 2.0)
    big_part = jax.random.uniform(key_big, (HT,), jnp.float32, big_lo, big_hi)
    return jnp.where(strong, big_part, small_part).astype(jnp.float32)


def draw_chain_bias(key, part):
    key = jax.random.fold_in(key, 23)
    return chain_values(key, 96.0, 110.0)


def shard_levels(rng, dims, cuts, low, largest):
    factor_of = 1.0
    for position, shards_of in cuts:
        draws = jax.random.uniform(jax.random.fold_in(jax.random.fold_in(rng, 6), position), (shards_of,), jnp.float32, low / len(cuts), largest / len(cuts))
        factor_of = factor_of * jnp.repeat(jnp.exp(draws), dims[position] // shards_of).reshape((-1,) + (1,) * (len(dims) - 1 - position))
    return factor_of


def split_up(amount, total, limit, slope):
    portions = [(1 << 20) // math.isqrt(standing ** slope) + 1 for standing in range(2, amount + 1)]
    rest, given = total - limit - (amount - 1), [1] * (amount - 1)
    while rest > 0:
        free = [i for i in range(amount - 1) if given[i] < limit]
        mass, left = sum([portions[i] for i in free]), rest
        for i in free:
            addition = min(limit - given[i], max(1, left * portions[i] // mass), rest)
            given[i] = given[i] + addition
            rest = rest - addition
    return np.array([limit] + given)


def ragged_sizes(own_key, count, total, bound, lean):
    if count == 2:
        one = jax.random.randint(own_key, (), max(1, total - bound), min(bound, total - 1) + 1)
        return jnp.stack([one, total - one])
    tallies = jnp.asarray(split_up(count, total, bound, lean), jnp.int32)
    pairs = (count - 1) // 2
    giver, taker = tallies[1:1 + 2 * pairs:2], tallies[2:2 + 2 * pairs:2]
    room = jnp.minimum(giver - 1, bound - taker)
    shifted = jax.random.randint(jax.random.fold_in(own_key, 1), (pairs,), 0, 1 << 20) % (room + 1)
    tallies = tallies.at[1:1 + 2 * pairs:2].set(giver - shifted).at[2:2 + 2 * pairs:2].set(taker + shifted)
    return tallies[jax.random.permutation(jax.random.fold_in(own_key, 2), count)]


def gaussian(key, shape, scale, reach, cuts=(), kind=jnp.bfloat16):
    drawn = scale * jax.random.normal(key, shape, jnp.float32)
    if cuts:
        drawn = drawn * shard_levels(key, shape, cuts, -0.22, 0.18)
    return jnp.clip(drawn, -reach, reach).astype(kind)


def setup_inputs(seed: int = 0) -> dict:
    arg_keys = jax.random.split(jax.random.key(seed), 18)
    return {
        "pair_tensor": gaussian(arg_keys[0], (TOKENS, TOKENS, CZ), 1.0, 6.0, ((0, 8), (1, 16))),
        "token_single": gaussian(arg_keys[1], (TOKENS, CS), 1.0, 6.0, ((0, 8),)),
        "atom_single": gaussian(arg_keys[2], (ATOMS, CA), 1.0, 6.0, ((0, 128),)),
        "atom_token": draw_atom_token(jax.random.fold_in(arg_keys[17], 71), 0),
        "chain_index": jnp.searchsorted(jnp.cumsum(ragged_sizes(arg_keys[4], CHAINS, TOKENS, TOKENS // 4, 1)), jnp.arange(TOKENS), side="right").astype(jnp.int32),
        "pair_up": gaussian(arg_keys[5], (CZ, 2 * PH), CZ ** -0.5, 0.5),
        "pair_down": gaussian(arg_keys[6], (PH, CZ), (PH // 4) ** -0.5, 0.75),
        "bias_heads": gaussian(arg_keys[7], (CZ, HB), CZ ** -0.5, 0.5),
        "atom_gain": jnp.clip(1.0 + 0.18 * jax.random.normal(arg_keys[8], (CA,), jnp.float32), 0.1, 1.9),
        "atom_proj": gaussian(arg_keys[9], (CA, 4 * CA), CA ** -0.5, 0.5),
        "atom_exit": gaussian(arg_keys[10], (CA, CA), CA ** -0.5, 0.5),
        "atom_pool": gaussian(arg_keys[11], (CA, CS), CA ** -0.5, 0.5),
        "token_gain": jnp.clip(1.0 + 0.18 * jax.random.normal(arg_keys[12], (CS,), jnp.float32), 0.1, 1.9),
        "token_proj": gaussian(arg_keys[13], (CS, 4 * CS), CS ** -0.5, 0.21875),
        "token_exit": gaussian(arg_keys[14], (CS, CS), CS ** -0.5, 0.21875),
        "chain_bias": draw_chain_bias(jax.random.fold_in(arg_keys[17], 71), 0),
        "token_back": gaussian(arg_keys[16], (CS, CA), CS ** -0.5, 0.21875),
    }


EPS = 1e-05

def standardize(features):
    features = features.astype(jnp.float32)
    center = features - lax.optimization_barrier(jnp.mean(features, axis=-1, keepdims=True))
    spread = lax.optimization_barrier(jnp.mean(center * center, axis=-1, keepdims=True))
    return center * lax.rsqrt(spread + EPS)

def normalize(features, gain_vec):
    return standardize(features) * gain_vec.astype(jnp.float32)

def rounded(features):
    return lax.optimization_barrier(features.astype(jnp.bfloat16)).astype(jnp.float32)

def pair_part(pair_rows_in, pair_up, pair_down, bias_heads):
    normed = rounded(standardize(pair_rows_in))
    mixed_up = jnp.einsum('ijc,cf->ijf', normed, pair_up.astype(jnp.float32))
    hidden = rounded(jax.nn.silu(mixed_up[..., :PH]) * mixed_up[..., PH:])
    updated = pair_rows_in.astype(jnp.float32) + jnp.einsum('ijf,fc->ijc', hidden, pair_down.astype(jnp.float32))
    normed_two = rounded(standardize(updated))
    return jnp.einsum('ijc,ch->hij', normed_two, bias_heads.astype(jnp.float32)).astype(jnp.bfloat16)

def reference(pair_tensor, token_single, atom_single, atom_token, chain_index, pair_up, pair_down, bias_heads, atom_gain, atom_proj, atom_exit, atom_pool, token_gain, token_proj, token_exit, chain_bias, token_back):
    row_block = TOK_R // 4
    stacked = pair_tensor.reshape(TOKENS // row_block, row_block, TOKENS, CZ)
    mapped = lax.map(lambda part_rows: pair_part(part_rows, pair_up, pair_down, bias_heads), stacked)
    pair_bias = jnp.transpose(mapped, (1, 0, 2, 3)).reshape(HB, TOKENS, TOKENS)
    atom_normed = normalize(atom_single, atom_gain).astype(jnp.bfloat16)
    atom_projected = jnp.dot(atom_normed, atom_proj, preferred_element_type=jnp.float32)
    atom_qkv = atom_projected[:, :3 * CA].astype(jnp.bfloat16)
    atom_gate = atom_projected[:, 3 * CA:]
    blocks = ATOMS // QB
    starts = QB * jnp.arange(blocks, dtype=jnp.int32)
    positions = starts[:, None] - EDGE + jnp.arange(KW, dtype=jnp.int32)[None, :]
    in_range = (positions >= 0) & (positions < ATOMS)
    clipped = jnp.clip(positions, 0, ATOMS - 1).astype(jnp.int32)
    query_heads = atom_qkv[:, :CA].reshape(blocks, QB, HA, HDA).astype(jnp.float32)
    keys_win = atom_qkv[clipped, CA:2 * CA].reshape(blocks, KW, HA, HDA).astype(jnp.float32)
    vals_win = atom_qkv[clipped, 2 * CA:].reshape(blocks, KW, HA, HDA).astype(jnp.float32)
    query_tok = atom_token.reshape(blocks, QB)
    key_tok = atom_token[clipped]
    bias_tile = pair_bias[:HA][:, query_tok[:, :, None], key_tok[:, None, :]]
    bias_tile = jnp.transpose(bias_tile, (1, 0, 2, 3)).astype(jnp.float32)
    scores = jnp.einsum('bihd,bjhd->bhij', query_heads, keys_win) * HDA ** (-0.5) + bias_tile
    scores = jnp.where(in_range[:, None, None, :], scores, -1e+30)
    row_top = lax.optimization_barrier(jnp.max(scores, axis=-1, keepdims=True))
    weights_full = jnp.exp(scores - row_top)
    denominator = lax.optimization_barrier(jnp.sum(weights_full, axis=-1))
    attended = jnp.einsum('bhij,bjhd->bihd', rounded(weights_full), vals_win)
    attended = attended / jnp.transpose(denominator, (0, 2, 1))[..., None]
    attended = attended.reshape(ATOMS, CA)
    atom_gated = (attended * jax.nn.sigmoid(atom_gate)).astype(jnp.bfloat16)
    atom_mid = (atom_single.astype(jnp.float32) + jnp.dot(atom_gated, atom_exit, preferred_element_type=jnp.float32)).astype(jnp.bfloat16)
    atom_pooled = jax.nn.relu(jnp.dot(atom_mid, atom_pool, preferred_element_type=jnp.float32)).astype(jnp.bfloat16)
    sums = jax.ops.segment_sum(atom_pooled.astype(jnp.float32), atom_token, num_segments=TOKENS)
    counts = jax.ops.segment_sum(jnp.ones((ATOMS,), jnp.float32), atom_token, num_segments=TOKENS)
    token_mid = (token_single.astype(jnp.float32) + sums / counts[:, None]).astype(jnp.bfloat16)
    token_normed = normalize(token_mid, token_gain).astype(jnp.bfloat16)
    token_projected = jnp.dot(token_normed, token_proj, preferred_element_type=jnp.float32)
    queries = token_projected[:, :CS].astype(jnp.bfloat16)
    token_gate = token_projected[:, CS:2 * CS]
    keys_all = token_projected[:, 2 * CS:3 * CS].astype(jnp.bfloat16)
    values_all = token_projected[:, 3 * CS:].astype(jnp.bfloat16)
    same_chain = (chain_index[:, None] == chain_index[None, :]).astype(jnp.float32)

    def one_head(head_items):
        query_h, key_h, value_h, bias_h, chain_h = head_items
        head_scores = jnp.dot(query_h, key_h.T, preferred_element_type=jnp.float32) * HDT ** (-0.5) + bias_h.astype(jnp.float32) + chain_h * same_chain
        head_top = lax.optimization_barrier(jnp.max(head_scores, axis=-1, keepdims=True))
        head_exp = jnp.exp(head_scores - head_top)
        head_den = lax.optimization_barrier(jnp.sum(head_exp, axis=-1))
        return jnp.dot(head_exp.astype(jnp.bfloat16), value_h, preferred_element_type=jnp.float32) / head_den[:, None]
    heads_out = lax.map(one_head, (jnp.transpose(queries.reshape(TOKENS, HT, HDT), (1, 0, 2)), jnp.transpose(keys_all.reshape(TOKENS, HT, HDT), (1, 0, 2)), jnp.transpose(values_all.reshape(TOKENS, HT, HDT), (1, 0, 2)), pair_bias[HA:], chain_bias.astype(jnp.float32)))
    token_attended = jnp.transpose(heads_out, (1, 0, 2)).reshape(TOKENS, CS)
    token_gated = (token_attended * jax.nn.sigmoid(token_gate)).astype(jnp.bfloat16)
    token_update = (token_mid.astype(jnp.float32) + jnp.dot(token_gated, token_exit, preferred_element_type=jnp.float32)).astype(jnp.bfloat16)
    token_sent = jnp.dot(token_update, token_back, preferred_element_type=jnp.float32).astype(jnp.bfloat16)
    atom_update = (atom_mid.astype(jnp.float32) + token_sent[atom_token].astype(jnp.float32)).astype(jnp.bfloat16)
    return (token_update, atom_update)
```

```python
import functools

import jax
import jax.numpy as jnp
from jax import lax
from jax.experimental import pallas as pl
from jax.experimental.pallas import tpu as pltpu
from jax.sharding import PartitionSpec as P

CZ = 128
CS = 768
CA = 128
HT = 16
HA = 4
PH = 256
QB = 32
KW = 128
HDA = 32
HDT = 48
HB = 20
HALO = 64
CHUNK = 64
GROUP = 256
EPS = 1e-05

bf16 = jnp.bfloat16
f32 = jnp.float32


def dot(left, right):
    return jnp.dot(left, right, preferred_element_type=f32)


def dot_nt(left, right):
    return lax.dot_general(left, right, (((1,), (1,)), ((), ())), preferred_element_type=f32)


def dot_tn(left, right):
    return lax.dot_general(left, right, (((0,), (0,)), ((), ())), preferred_element_type=f32)


def centered(features):
    return features - jnp.mean(features, axis=-1, keepdims=True)


def scaled(center):
    spread = jnp.mean(center * center, axis=-1, keepdims=True)
    return center * lax.rsqrt(spread + EPS)


def sigmoid(value):
    return 0.5 + 0.5 * jnp.tanh(0.5 * value)


VMEM = pl.BlockSpec(memory_space=pltpu.VMEM)
SMEM = pl.BlockSpec(memory_space=pltpu.SMEM)


def pair_body(place, pair_ref, up_ref, down_ref, heads_ref, center_ref, *refs):
    refs = refs[-3:] if len(refs) in (3, 5) else refs[-2:]
    pair_part = pair_ref[...].reshape(-1, CZ)
    normed = scaled(dot(pair_part, center_ref[...])).astype(bf16)
    mixed = dot(normed, up_ref[...])
    gate, value = mixed[:, :PH], mixed[:, PH:]
    hidden = ((gate + gate * jnp.tanh(gate)) * value).astype(bf16)
    updated = pair_part.astype(f32) + dot(hidden, down_ref[...])
    normed_two = scaled(centered(updated)).astype(bf16)
    biases = dot_nt(heads_ref[...], normed_two)
    rows = pair_ref.shape[0]
    stacked = jnp.stack([biases[:, i * CZ : (i + 1) * CZ] for i in range(rows)], axis=0)
    stacked = jnp.swapaxes(stacked, 0, 1).astype(bf16)
    refs[0][...] = stacked[:HA]
    refs[1][...] = stacked[HA:HB]
    if len(refs) == 3:
        refs[2][...] = stacked[:HA]


def pair_chunks(place, pair, weights, before, count, where):
    rows, cols = pair.shape[:2]
    whole = lambda array: pl.BlockSpec(array.shape, lambda i, place: (0,) * array.ndim)
    out_shape = [
        jax.ShapeDtypeStruct((HA, rows, cols), bf16),
        jax.ShapeDtypeStruct((HT, rows, cols), bf16),
    ]
    out_specs = [
        pl.BlockSpec((HA, CHUNK, cols), lambda i, place: (0, where(i, place), 0)),
        pl.BlockSpec((HT, CHUNK, cols), lambda i, place: (0, where(i, place), 0)),
    ]
    in_specs = [pl.BlockSpec((CHUNK, cols, CZ), lambda i, place: (where(i, place), 0, 0))]
    in_specs += [whole(array) for array in weights]
    aliases = {}
    if before:
        aliases = {2 + len(weights): 0, 3 + len(weights): 1}
        in_specs += [pl.BlockSpec(memory_space=pl.ANY)] * 2
    else:
        out_shape.append(jax.ShapeDtypeStruct((HA, CHUNK, cols), bf16))
        out_specs.append(pl.BlockSpec((HA, CHUNK, cols), lambda i, place: (0, 0, 0)))
    cells = count * CHUNK * cols
    return pl.pallas_call(
        pair_body,
        grid_spec=pltpu.PrefetchScalarGridSpec(
            num_scalar_prefetch=1, grid=(count,), in_specs=in_specs, out_specs=out_specs
        ),
        out_shape=out_shape,
        input_output_aliases=aliases,
        compiler_params=pltpu.CompilerParams(vmem_limit_bytes=56 * 2**20),
        cost_estimate=pl.CostEstimate(
            flops=cells * 250000, bytes_accessed=cells * 300, transcendentals=cells * PH
        ),
        name="pair",
    )(place, pair, *weights, *before)


def project_body(ext_ref, gain_ref, proj_ref, query_ref, key_ref, value_ref, gate_ref):
    ext = ext_ref[...].astype(f32)
    normed = (scaled(centered(ext)) * gain_ref[...]).astype(bf16)
    atoms = query_ref.shape[0]
    own = normed[HALO : HALO + atoms]
    query_ref[...] = (dot(own, proj_ref[:, :CA]) * HDA ** (-0.5)).astype(bf16)
    key_ref[...] = dot(normed, proj_ref[:, CA : 2 * CA]).astype(bf16)
    value_ref[...] = dot(normed, proj_ref[:, 2 * CA : 3 * CA]).astype(bf16)
    gate_ref[...] = sigmoid(dot(own, proj_ref[:, 3 * CA :]))


def project_atoms(ext, gain, proj):
    total = ext.shape[0]
    atoms = total - 2 * HALO
    return pl.pallas_call(
        project_body,
        in_specs=[VMEM] * 3,
        out_specs=[VMEM] * 4,
        out_shape=[
            jax.ShapeDtypeStruct((atoms, CA), bf16),
            jax.ShapeDtypeStruct((total, CA), bf16),
            jax.ShapeDtypeStruct((total, CA), bf16),
            jax.ShapeDtypeStruct((atoms, CA), f32),
        ],
        compiler_params=pltpu.CompilerParams(vmem_limit_bytes=48 * 2**20),
        cost_estimate=pl.CostEstimate(flops=10**9, bytes_accessed=2**22, transcendentals=2**18),
        name="atom_projections",
    )(ext, gain, proj)


def atoms_body(
    place,
    half_ref,
    other_ref,
    query_ref,
    key_ref,
    value_ref,
    gate_ref,
    ext_ref,
    tokens_ref,
    exit_ref,
    pool_ref,
    single_ref,
    gain_ref,
    tproj_ref,
    mid_ref,
    tmid_ref,
    tquery_ref,
    tgate_ref,
    tkv_ref,
    bias_ref,
    look_ref,
    sums_ref,
):
    row, col, row_count = place[0], place[1], place[2]
    total = ext_ref.shape[0]
    atoms = query_ref.shape[0]
    rows = single_ref.shape[0]
    even = lax.rem(col, 2) == 0
    for h in range(HA):
        mine, theirs = half_ref[h], other_ref[h]
        first = jnp.where(even, mine, theirs)
        second = jnp.where(even, theirs, mine)
        base = h * 3 * KW
        bias_ref[:, base : base + KW] = first[:rows]
        bias_ref[:, base + KW : base + 2 * KW] = second[:rows]
        bias_ref[:, base + 2 * KW : base + 3 * KW] = jnp.concatenate(
            [first[rows:], jnp.zeros((rows - 2 * HALO, KW), bf16), second[rows:]], axis=0
        )
    lane = lax.broadcasted_iota(jnp.int32, (KW, 3 * KW), 1)
    for t in range(total // KW):
        at = slice(t * KW, (t + 1) * KW)
        tokens = jnp.broadcast_to(tokens_ref[:, at], (KW, KW)).astype(f32).T.astype(jnp.int32)
        tokens = jnp.concatenate([tokens] * 3, axis=1)
        tokens = jnp.where(tokens < 0, tokens + 3 * KW, tokens)
        look_ref[at, :CA] = key_ref[at, :]
        look_ref[at, CA:] = (tokens == lane).astype(f32).astype(bf16)
    head_of = lax.broadcasted_iota(jnp.int32, (QB, CA), 1) // HDA
    sums_ref[...] = jnp.zeros_like(sums_ref)
    row_lane = lax.broadcasted_iota(jnp.int32, (1, KW), 1)

    def group(g, counts):
        start = pl.multiple_of(g * GROUP, GROUP)
        own = pl.ds(start, GROUP)
        onehot = look_ref[pl.ds(pl.multiple_of(start + HALO, HALO), GROUP), CA : CA + 2 * KW]
        picked = dot(onehot, bias_ref[...]).astype(bf16)
        queries = query_ref[own, :]
        scores = []
        for b in range(GROUP // QB):
            part = slice(b * QB, (b + 1) * QB)
            left = jnp.concatenate(
                [
                    jnp.concatenate(
                        [
                            jnp.where(head_of == h, queries[part].astype(f32), 0.0).astype(bf16),
                            picked[part, h * 3 * KW : (h + 1) * 3 * KW],
                        ],
                        axis=1,
                    )
                    for h in range(HA)
                ],
                axis=0,
            )
            first = start + b * QB + HALO - (KW - QB) // 2
            window = look_ref[pl.ds(pl.multiple_of(first, 16), KW), :]
            at = row_lane + first
            inside = ((at >= HALO) | (row > 0)) & ((at < total - HALO) | (row < row_count - 1))
            scores.append(dot_nt(left, window) + jnp.where(inside, 0.0, -1e30))
        scores = jnp.concatenate(scores, axis=0)
        exps = jnp.exp(scores - jnp.max(scores, axis=-1, keepdims=True))
        inverse = 1.0 / jnp.sum(exps, axis=-1, keepdims=True)
        weights = exps.astype(bf16)
        attended = []
        for b in range(GROUP // QB):
            first = start + b * QB + HALO - (KW - QB) // 2
            part = slice(b * HA * QB, (b + 1) * HA * QB)
            out = dot(weights[part], value_ref[pl.ds(pl.multiple_of(first, 16), KW), :])
            out = out * inverse[part]
            merged = out[:QB]
            for h in range(1, HA):
                merged = jnp.where(head_of == h, out[h * QB : (h + 1) * QB], merged)
            attended.append(merged)
        attended = jnp.concatenate(attended, axis=0)
        gated = (attended * gate_ref[own, :]).astype(bf16)
        single = ext_ref[pl.ds(pl.multiple_of(start + HALO, HALO), GROUP), :].astype(f32)
        mid = (single + dot(gated, exit_ref[...])).astype(bf16)
        mid_ref[own, :] = mid
        pooled = jnp.maximum(dot(mid, pool_ref[...]), 0.0).astype(bf16)
        sums_ref[...] += dot_tn(onehot, pooled)
        return counts + jnp.sum(onehot.astype(f32).T, axis=1, keepdims=True)

    counts = lax.fori_loop(0, atoms // GROUP, group, jnp.zeros((rows, 1), f32))
    token_mid = (single_ref[...].astype(f32) + sums_ref[...] / counts).astype(bf16)
    tmid_ref[...] = token_mid
    normed = (scaled(centered(token_mid.astype(f32))) * gain_ref[...]).astype(bf16)

    def head_part(part):
        start = part * CS + col * HDT
        base = jnp.minimum(start // KW * KW, 4 * CS - 2 * KW)
        base = pl.multiple_of(base, KW)
        wide = dot(normed, tproj_ref[:, pl.ds(base, 2 * KW)])
        return pltpu.roll(wide, lax.rem(2 * KW - (start - base), 2 * KW), 1)[:, :KW]

    tquery_ref[...] = head_part(0)[:, :HDT].astype(bf16)
    tgate_ref[...] = sigmoid(head_part(1)[:, :HDT])
    tkv_ref[:HDT, :] = head_part(2).T[:HDT].astype(bf16)
    tkv_ref[HDT:, :] = head_part(3).T[:HDT].astype(bf16)


def atom_attention(place, half, other, parts, ext, tokens, exit_w, pool, single, gain, tproj):
    total = ext.shape[0]
    atoms = total - 2 * HALO
    rows = single.shape[0]
    return pl.pallas_call(
        atoms_body,
        in_specs=[SMEM] + [VMEM] * 13,
        out_specs=[VMEM] * 5,
        out_shape=[
            jax.ShapeDtypeStruct((atoms, CA), bf16),
            jax.ShapeDtypeStruct((rows, CS), bf16),
            jax.ShapeDtypeStruct((rows, HDT), bf16),
            jax.ShapeDtypeStruct((rows, HDT), f32),
            jax.ShapeDtypeStruct((2 * HDT, rows), bf16),
        ],
        scratch_shapes=[
            pltpu.VMEM((rows, HA * 3 * KW), bf16),
            pltpu.VMEM((total, CA + 3 * KW), bf16),
            pltpu.VMEM((rows, CS), f32),
        ],
        compiler_params=pltpu.CompilerParams(vmem_limit_bytes=48 * 2**20),
        cost_estimate=pl.CostEstimate(
            flops=10**10, bytes_accessed=2**24, transcendentals=2**22
        ),
        name="atoms",
    )(place, half, other, *parts, ext, tokens, exit_w, pool, single, gain, tproj)


def tokens_body(place, query_ref, gate_ref, kv_ref, bias_ref, mine_ref, chain_ref, strength, out_ref):
    col = place[1]
    rows = query_ref.shape[0]
    shards, cols = bias_ref.shape[0], bias_ref.shape[2]
    query = query_ref[...]
    strong = strength[col]
    scores = []
    for r in range(kv_ref.shape[0]):
        raw = dot(query, kv_ref[r, :HDT, :]) * HDT ** (-0.5)
        per = rows // cols
        bias = jnp.concatenate([bias_ref[r * per + k].astype(f32) for k in range(per)], axis=1)
        same = mine_ref[...] == chain_ref[:, r * rows : (r + 1) * rows]
        scores.append(raw + bias + jnp.where(same, strong, 0.0))
    top = scores[0]
    for part in scores[1:]:
        top = jnp.maximum(top, part)
    top = jnp.max(top, axis=-1, keepdims=True)
    exps = [jnp.exp(part - top) for part in scores]
    total = exps[0]
    for part in exps[1:]:
        total = total + part
    total = jnp.sum(total, axis=-1, keepdims=True)
    out = jnp.zeros((rows, HDT), f32)
    for r in range(kv_ref.shape[0]):
        out = out + dot_nt(exps[r].astype(bf16), kv_ref[r, HDT:, :])
    gated = out / total * gate_ref[...]
    wide = jnp.concatenate([gated, jnp.zeros((rows, KW - HDT), f32)], axis=1)
    gated = wide.T[:HDT].astype(bf16)
    for k in range(out_ref.shape[0]):
        out_ref[k] = gated


def token_attention(place, query, gate, kv, bias, mine, chain, strength):
    rows = query.shape[0]
    shards = bias.shape[0]
    return pl.pallas_call(
        tokens_body,
        in_specs=[SMEM] + [VMEM] * 6 + [SMEM],
        out_specs=VMEM,
        out_shape=jax.ShapeDtypeStruct((shards, HDT, rows), bf16),
        compiler_params=pltpu.CompilerParams(vmem_limit_bytes=48 * 2**20),
        cost_estimate=pl.CostEstimate(flops=10**9, bytes_accessed=2**22, transcendentals=2**19),
        name="tokens",
    )(place, query, gate, kv, bias, mine, chain, strength)


def update_body(place, gated_ref, exit_ref, tmid_ref, back_ref, mid_ref, tokens_ref, tout_ref, aout_ref):
    col = place[1]
    atoms, rows = aout_ref.shape[0], tmid_ref.shape[0]
    added = dot_tn(gated_ref[...], exit_ref[...])
    update = (tmid_ref[...].astype(f32) + added).astype(bf16)
    tout_ref[...] = update
    sent = dot(update, back_ref[...]).astype(bf16)
    own = tokens_ref[...]
    onehot = (lax.broadcasted_iota(jnp.int32, (rows, atoms), 0) == own).astype(f32).astype(bf16)
    at = pl.multiple_of(col * atoms, atoms)
    mid = mid_ref[pl.ds(at, atoms), :].astype(f32)
    aout_ref[...] = (mid + dot_tn(onehot, sent)).astype(bf16)


def updates(place, gated, exit_w, tmid, back, mid, tokens, atoms):
    rows = tmid.shape[0]
    return pl.pallas_call(
        update_body,
        in_specs=[SMEM] + [VMEM] * 6,
        out_specs=[VMEM] * 2,
        out_shape=[
            jax.ShapeDtypeStruct((rows, CS), bf16),
            jax.ShapeDtypeStruct((atoms, CA), bf16),
        ],
        compiler_params=pltpu.CompilerParams(vmem_limit_bytes=48 * 2**20),
        name="updates",
    )(place, gated, exit_w, tmid, back, mid, tokens)


def local(
    pair_tensor,
    token_single,
    atom_single,
    atom_token,
    chain_index,
    pair_up,
    pair_down,
    bias_heads,
    atom_gain,
    atom_proj,
    atom_exit,
    atom_pool,
    token_gain,
    token_proj,
    token_exit,
    chain_bias,
    token_back,
):
    rows, cols = pair_tensor.shape[:2]
    atom_rows = atom_single.shape[0]
    row_count = lax.axis_size("row")
    col_count = lax.axis_size("col")
    row = lax.axis_index("row")
    col = lax.axis_index("col")
    chips = col_count // 2
    row_atoms = atom_rows * col_count

    spread = lambda part, count: jnp.broadcast_to(part[None], (count,) + part.shape)
    atoms = lax.all_to_all(spread(atom_single, col_count), "col", 0, 0).reshape(row_atoms, CA)
    up = [(i, i + 1) for i in range(row_count - 1)]
    down = [(i + 1, i) for i in range(row_count - 1)]
    before = lax.ppermute(atoms[-HALO:], "row", up)
    after = lax.ppermute(atoms[:HALO], "row", down)
    ext = jnp.concatenate([before, atoms, after], axis=0)
    ext_tokens = lax.dynamic_slice_in_dim(
        jnp.pad(atom_token, (HALO, HALO)), row * row_atoms, row_atoms + 2 * HALO
    )
    ext_tokens = (ext_tokens - row * rows)[None, :]
    own_tokens = lax.dynamic_slice_in_dim(
        atom_token, row * row_atoms + col * atom_rows, atom_rows
    )
    own_tokens = (own_tokens - row * rows)[None, :]

    flip = ((col == 2 * row + 1) | (col == 2 * row + 2)).astype(jnp.int32)
    place = jnp.stack([row, col, jnp.int32(row_count), flip]).astype(jnp.int32)
    halved = jnp.concatenate([pair_up[:, :PH] * bf16(0.5), pair_up[:, PH:]], axis=1)
    heads = jnp.pad(bias_heads.T, ((0, 32 - HB), (0, 0)))
    center = (jnp.eye(CZ, dtype=f32) - 1.0 / CZ).astype(bf16)
    weights = (halved, pair_down, heads, center)
    chunks = rows // CHUNK
    atom_bias, token_bias, edge = pair_chunks(
        place, pair_tensor, weights, (), 1, lambda i, place: (chunks - 1) * place[3]
    )
    halo_pairs = [
        (r * col_count + 2 * r - 1, r * col_count + 2 * r) for r in range(1, row_count)
    ] + [(r * col_count + 2 * r + 2, r * col_count + 2 * r + 1) for r in range(row_count - 1)]
    edge = lax.ppermute(edge, ("row", "col"), halo_pairs)
    atom_bias, token_bias = pair_chunks(
        place,
        pair_tensor,
        weights,
        (atom_bias, token_bias),
        chunks - 1,
        lambda i, place: i + 1 - place[3],
    )
    head_bias = lax.all_to_all(token_bias, "col", 0, 0)

    half = jnp.concatenate([atom_bias, edge], axis=1)
    gathered = jnp.where(col // 2 == row, half, jnp.zeros_like(half))
    for step in range(1, chips):
        pairs = [
            (r * col_count + 2 * r + core, r * col_count + 2 * ((r + step) % chips) + core)
            for r in range(row_count)
            for core in range(2)
        ]
        gathered = gathered + lax.ppermute(half, ("row", "col"), pairs)
    other = lax.ppermute(gathered, "col", [(i, i ^ 1) for i in range(col_count)])

    parts = project_atoms(ext, atom_gain[None], atom_proj)
    atom_mid, token_mid, query, gate, keyvals = atom_attention(
        place,
        gathered,
        other,
        parts,
        ext,
        ext_tokens,
        atom_exit,
        atom_pool,
        token_single,
        token_gain[None],
        token_proj,
    )
    keyvals = lax.all_to_all(spread(keyvals, row_count), "row", 0, 0)
    mine = lax.dynamic_slice_in_dim(chain_index, row * rows, rows)
    gated = token_attention(
        place, query, gate, keyvals, head_bias, mine[:, None], chain_index[None], chain_bias
    )
    gated = lax.all_to_all(gated, "col", 0, 0).reshape(CS, rows)
    return tuple(
        updates(
            place, gated, token_exit, token_mid, token_back, atom_mid, own_tokens, atom_rows
        )
    )


def solution(mesh):
    placed = (
        P("row", "col", None),
        P("row", None),
        P(("row", "col"), None),
    ) + (P(),) * 14
    return jax.shard_map(
        local,
        mesh=mesh,
        in_specs=placed,
        out_specs=(P("row", None), P(("row", "col"), None)),
        check_vma=False,
    )
```

```python
import functools

import jax
import jax.numpy as jnp
import numpy as np
from jax import lax
from jax.experimental import pallas as pl
from jax.experimental.pallas import tpu as pltpu
from jax.sharding import PartitionSpec as P

CZ = 128
CS = 768
CA = 128
HT = 16
HA = 4
PH = 256
QB = 32
KW = 128
HDA = 32
HDT = 48
HB = 20
HALO = 64
BANDS = (64, 80, 64)
GROUP = 256
EPS = 1e-05

bf16 = jnp.bfloat16
f32 = jnp.float32


def dot(left, right):
    return jnp.dot(left, right, preferred_element_type=f32)


def dot_nt(left, right):
    return lax.dot_general(left, right, (((1,), (1,)), ((), ())), preferred_element_type=f32)


def dot_tn(left, right):
    return lax.dot_general(left, right, (((0,), (0,)), ((), ())), preferred_element_type=f32)


def centered(features):
    return features - jnp.mean(features, axis=-1, keepdims=True)


def scaled(center):
    spread = jnp.mean(center * center, axis=-1, keepdims=True)
    return center * lax.rsqrt(spread + EPS)


def sigmoid(value):
    return 0.5 + 0.5 * jnp.tanh(0.5 * value)


SMEM = pl.BlockSpec(memory_space=pltpu.SMEM)


def full(array):
    return pl.BlockSpec(array.shape, lambda *_: (0,) * len(array.shape))


def pair_body(place, pair_ref, up_ref, down_ref, heads_ref, center_ref, *refs, edges):
    outs = refs[-2:] if edges else refs[-1:]
    pair_part = pair_ref[...].reshape(-1, CZ)
    normed = scaled(dot(pair_part, center_ref[...])).astype(bf16)
    gate = dot(normed, up_ref[:, :PH] * bf16(0.5))
    value = dot(normed, up_ref[:, PH:])
    hidden = ((gate + gate * jnp.tanh(gate)) * value).astype(bf16)
    updated = pair_part.astype(f32) + dot(hidden, down_ref[...])
    normed_two = scaled(centered(updated)).astype(bf16)
    heads = jnp.concatenate([heads_ref[...].astype(f32), jnp.zeros((CZ, CZ - HB), f32)], axis=1)
    biases = dot_nt(heads.T[:32].astype(bf16), normed_two)
    rows = pair_ref.shape[0]
    stacked = jnp.stack([biases[:, i * CZ : (i + 1) * CZ] for i in range(rows)], axis=0)
    stacked = jnp.swapaxes(stacked, 0, 1).astype(bf16)
    outs[0][...] = stacked[HA:HB]
    if edges:
        outs[1][...] = stacked[:HA]


def pair_chunk(place, pair, weights, before, first, count, edges):
    rows, cols = pair.shape[:2]

    def start(place):
        return pl.multiple_of(first + place[3] * (rows - 2 * first - count), 16)

    in_specs = [
        pl.BlockSpec(
            (pl.Element(count), pl.Element(cols), pl.Element(CZ)),
            lambda i, place: (start(place), 0, 0),
        )
    ]
    in_specs += [full(array) for array in weights]
    out_shape = [jax.ShapeDtypeStruct((HT, rows, cols), bf16)]
    out_specs = [
        pl.BlockSpec(
            (pl.Element(HT), pl.Element(count), pl.Element(cols)),
            lambda i, place: (0, start(place), 0),
        )
    ]
    if edges:
        out_shape.append(jax.ShapeDtypeStruct((HA, count, cols), bf16))
        out_specs.append(full(out_shape[-1]))
    aliases = {}
    if before:
        aliases = {2 + len(weights): 0}
        in_specs += [pl.BlockSpec(memory_space=pl.ANY)]
    cells = count * cols
    return pl.pallas_call(
        functools.partial(pair_body, edges=edges),
        grid_spec=pltpu.PrefetchScalarGridSpec(
            num_scalar_prefetch=1, grid=(1,), in_specs=in_specs, out_specs=out_specs
        ),
        out_shape=out_shape,
        input_output_aliases=aliases,
        compiler_params=pltpu.CompilerParams(vmem_limit_bytes=56 * 2**20),
        cost_estimate=pl.CostEstimate(
            flops=cells * 500000, bytes_accessed=cells * 300, transcendentals=cells * PH
        ),
        name="pair",
    )(place, pair, *weights, *before)


def project_body(shards_ref, gain_ref, proj_ref, ext_ref, query_ref, key_ref, value_ref, gate_ref):
    shards = shards_ref.shape[0]
    atoms = query_ref.shape[0]
    per = atoms // shards
    ext_ref[:HALO] = shards_ref[0, per : per + HALO]
    for k in range(shards):
        ext_ref[HALO + k * per : HALO + (k + 1) * per] = shards_ref[k, :per]
    ext_ref[HALO + atoms :] = shards_ref[shards - 1, per : per + HALO]
    normed = (scaled(centered(ext_ref[...].astype(f32))) * gain_ref[...]).astype(bf16)
    own = normed[HALO : HALO + atoms]
    query_ref[...] = (dot(own, proj_ref[:, :CA]) * HDA ** (-0.5)).astype(bf16)
    key_ref[...] = dot(normed, proj_ref[:, CA : 2 * CA]).astype(bf16)
    value_ref[...] = dot(normed, proj_ref[:, 2 * CA : 3 * CA]).astype(bf16)
    gate_ref[...] = sigmoid(dot(own, proj_ref[:, 3 * CA :]))


def project_atoms(shards, gain, proj, atoms):
    total = atoms + 2 * HALO
    out_shape = [
        jax.ShapeDtypeStruct((total, CA), bf16),
        jax.ShapeDtypeStruct((atoms, CA), bf16),
        jax.ShapeDtypeStruct((total, CA), bf16),
        jax.ShapeDtypeStruct((total, CA), bf16),
        jax.ShapeDtypeStruct((atoms, CA), f32),
    ]
    return pl.pallas_call(
        project_body,
        grid=(1,),
        in_specs=[full(shards), full(gain), full(proj)],
        out_specs=[full(shape) for shape in out_shape],
        out_shape=out_shape,
        compiler_params=pltpu.CompilerParams(vmem_limit_bytes=48 * 2**20),
        cost_estimate=pl.CostEstimate(flops=10**9, bytes_accessed=2**22, transcendentals=2**18),
        name="atom_projections",
    )(shards, gain, proj)


def atoms_body(
    place,
    half_ref,
    other_ref,
    half_two_ref,
    other_two_ref,
    ext_ref,
    query_ref,
    key_ref,
    value_ref,
    gate_ref,
    tokens_ref,
    exit_ref,
    pool_ref,
    single_ref,
    gain_ref,
    tproj_hbm,
    mid_ref,
    tmid_ref,
    tquery_ref,
    tgate_ref,
    tkv_ref,
    bias_ref,
    look_ref,
    sums_ref,
    tproj_ref,
    sem,
):
    row, col, row_count = place[0], place[1], place[2]
    total = ext_ref.shape[0]
    atoms = query_ref.shape[0]
    rows = single_ref.shape[0]
    even = lax.rem(col, 2) == 0
    copy = pltpu.make_async_copy(tproj_hbm, tproj_ref, sem)
    copy.start()
    near, mid, far = BANDS
    for h in range(HA):
        mine, theirs = half_ref[h], other_ref[h]
        first = jnp.where(even, mine, theirs)
        second = jnp.where(even, theirs, mine)
        mine, theirs = half_two_ref[h], other_two_ref[h]
        first_two = jnp.where(even, mine, theirs)
        second_two = jnp.where(even, theirs, mine)
        base = h * 3 * KW
        rest = jnp.zeros((rows - near - mid - far, KW), bf16)
        bias_ref[:, base : base + KW] = jnp.concatenate([first[: near + mid], first_two, rest], axis=0)
        bias_ref[:, base + KW : base + 2 * KW] = jnp.concatenate(
            [rest, second_two, second[near : near + mid], second[:near]], axis=0
        )
        bias_ref[:, base + 2 * KW : base + 3 * KW] = jnp.concatenate(
            [first[near + mid :], jnp.zeros((rows - 2 * near, KW), bf16), second[near + mid :]],
            axis=0,
        )
    lane = lax.broadcasted_iota(jnp.int32, (KW, 3 * KW), 1)
    for t in range(total // KW):
        at = slice(t * KW, (t + 1) * KW)
        tokens = jnp.broadcast_to(tokens_ref[:, at], (KW, KW)).astype(f32).T.astype(jnp.int32)
        tokens = jnp.concatenate([tokens] * 3, axis=1)
        tokens = jnp.where(tokens < 0, tokens + 3 * KW, tokens)
        look_ref[at, :CA] = key_ref[at, :]
        look_ref[at, CA:] = (tokens == lane).astype(f32).astype(bf16)
    head_of = lax.broadcasted_iota(jnp.int32, (QB, CA), 1) // HDA
    sums_ref[...] = jnp.zeros_like(sums_ref)
    row_lane = lax.broadcasted_iota(jnp.int32, (1, KW), 1)

    def group(g, counts):
        start = pl.multiple_of(g * GROUP, GROUP)
        own = pl.ds(start, GROUP)
        onehot = look_ref[pl.ds(pl.multiple_of(start + HALO, HALO), GROUP), CA : CA + 2 * KW]
        picked = dot(onehot, bias_ref[...]).astype(bf16)
        queries = query_ref[own, :]
        scores = []
        for b in range(GROUP // QB):
            part = slice(b * QB, (b + 1) * QB)
            left = jnp.concatenate(
                [
                    jnp.concatenate(
                        [
                            jnp.where(head_of == h, queries[part].astype(f32), 0.0).astype(bf16),
                            picked[part, h * 3 * KW : (h + 1) * 3 * KW],
                        ],
                        axis=1,
                    )
                    for h in range(HA)
                ],
                axis=0,
            )
            first = start + b * QB + HALO - (KW - QB) // 2
            window = look_ref[pl.ds(pl.multiple_of(first, 16), KW), :]
            at = row_lane + first
            inside = ((at >= HALO) | (row > 0)) & ((at < total - HALO) | (row < row_count - 1))
            scores.append(dot_nt(left, window) + jnp.where(inside, 0.0, -1e30))
        scores = jnp.concatenate(scores, axis=0)
        exps = jnp.exp(scores - jnp.max(scores, axis=-1, keepdims=True))
        inverse = 1.0 / jnp.sum(exps, axis=-1, keepdims=True)
        weights = exps.astype(bf16)
        attended = []
        for b in range(GROUP // QB):
            first = start + b * QB + HALO - (KW - QB) // 2
            part = slice(b * HA * QB, (b + 1) * HA * QB)
            out = dot(weights[part], value_ref[pl.ds(pl.multiple_of(first, 16), KW), :])
            out = out * inverse[part]
            merged = out[:QB]
            for h in range(1, HA):
                merged = jnp.where(head_of == h, out[h * QB : (h + 1) * QB], merged)
            attended.append(merged)
        attended = jnp.concatenate(attended, axis=0)
        gated = (attended * gate_ref[own, :]).astype(bf16)
        single = ext_ref[pl.ds(pl.multiple_of(start + HALO, HALO), GROUP), :].astype(f32)
        mid = (single + dot(gated, exit_ref[...])).astype(bf16)
        mid_ref[own, :] = mid
        pooled = jnp.maximum(dot(mid, pool_ref[...]), 0.0).astype(bf16)
        sums_ref[...] += dot_tn(onehot, pooled)
        return counts + jnp.sum(onehot.astype(f32).T, axis=1, keepdims=True)

    counts = lax.fori_loop(0, atoms // GROUP, group, jnp.zeros((rows, 1), f32))
    token_mid = (single_ref[...].astype(f32) + sums_ref[...] / counts).astype(bf16)
    tmid_ref[...] = token_mid
    normed = (scaled(centered(token_mid.astype(f32))) * gain_ref[...]).astype(bf16)

    copy.wait()

    def head_part(part):
        start = part * CS + col * HDT
        base = jnp.minimum(start // KW * KW, 4 * CS - 2 * KW)
        base = pl.multiple_of(base, KW)
        wide = dot(normed, tproj_ref[:, pl.ds(base, 2 * KW)])
        return pltpu.roll(wide, lax.rem(2 * KW - (start - base), 2 * KW), 1)[:, :KW]

    tquery_ref[...] = head_part(0)[:, :HDT].astype(bf16)
    tgate_ref[...] = sigmoid(head_part(1)[:, :HDT])
    tkv_ref[:HDT, :] = head_part(2).T[:HDT].astype(bf16)
    tkv_ref[HDT:, :] = head_part(3).T[:HDT].astype(bf16)


def atom_attention(place, bands, parts, tokens, exit_w, pool, single, gain, tproj):
    total = parts[0].shape[0]
    atoms = total - 2 * HALO
    rows = single.shape[0]
    operands = (*bands, *parts, tokens, exit_w, pool, single, gain)
    out_shape = [
        jax.ShapeDtypeStruct((atoms, CA), bf16),
        jax.ShapeDtypeStruct((rows, CS), bf16),
        jax.ShapeDtypeStruct((rows, HDT), bf16),
        jax.ShapeDtypeStruct((rows, HDT), f32),
        jax.ShapeDtypeStruct((2 * HDT, rows), bf16),
    ]
    return pl.pallas_call(
        atoms_body,
        grid=(1,),
        in_specs=[SMEM] + [full(array) for array in operands] + [pl.BlockSpec(memory_space=pl.ANY)],
        out_specs=[full(shape) for shape in out_shape],
        out_shape=out_shape,
        scratch_shapes=[
            pltpu.VMEM((rows, HA * 3 * KW), bf16),
            pltpu.VMEM((total, CA + 3 * KW), bf16),
            pltpu.VMEM((rows, CS), f32),
            pltpu.VMEM(tproj.shape, bf16),
            pltpu.SemaphoreType.DMA,
        ],
        compiler_params=pltpu.CompilerParams(vmem_limit_bytes=56 * 2**20),
        cost_estimate=pl.CostEstimate(
            flops=10**10, bytes_accessed=2**24, transcendentals=2**22
        ),
        name="atoms",
    )(place, *operands, tproj)


def tokens_body(place, query_ref, gate_ref, kv_ref, bias_ref, mine_ref, chain_ref, strength, out_ref):
    col = place[1]
    rows = query_ref.shape[0]
    shards, cols = bias_ref.shape[0], bias_ref.shape[2]
    query = query_ref[...]
    strong = strength[col]
    scores = []
    for r in range(kv_ref.shape[0]):
        raw = dot(query, kv_ref[r, :HDT, :]) * HDT ** (-0.5)
        per = rows // cols
        bias = jnp.concatenate([bias_ref[r * per + k].astype(f32) for k in range(per)], axis=1)
        same = mine_ref[...] == chain_ref[:, r * rows : (r + 1) * rows]
        scores.append(raw + bias + jnp.where(same, strong, 0.0))
    top = scores[0]
    for part in scores[1:]:
        top = jnp.maximum(top, part)
    top = jnp.max(top, axis=-1, keepdims=True)
    exps = [jnp.exp(part - top) for part in scores]
    total = exps[0]
    for part in exps[1:]:
        total = total + part
    total = jnp.sum(total, axis=-1, keepdims=True)
    out = jnp.zeros((rows, HDT), f32)
    for r in range(kv_ref.shape[0]):
        out = out + dot_nt(exps[r].astype(bf16), kv_ref[r, HDT:, :])
    gated = out / total * gate_ref[...]
    wide = jnp.concatenate([gated, jnp.zeros((rows, KW - HDT), f32)], axis=1)
    gated = wide.T[:HDT].astype(bf16)
    for k in range(out_ref.shape[0]):
        out_ref[k] = gated


def token_attention(place, query, gate, kv, bias, mine, chain, strength):
    rows = query.shape[0]
    shards = bias.shape[0]
    out_shape = jax.ShapeDtypeStruct((shards, HDT, rows), bf16)
    return pl.pallas_call(
        tokens_body,
        grid=(1,),
        in_specs=[SMEM] + [full(a) for a in (query, gate, kv, bias, mine, chain)] + [SMEM],
        out_specs=full(out_shape),
        out_shape=out_shape,
        compiler_params=pltpu.CompilerParams(vmem_limit_bytes=48 * 2**20),
        cost_estimate=pl.CostEstimate(flops=10**9, bytes_accessed=2**22, transcendentals=2**19),
        name="tokens",
    )(place, query, gate, kv, bias, mine, chain, strength)


def update_body(place, gated_ref, exit_ref, tmid_ref, back_ref, mid_ref, tokens_ref, tout_ref, aout_ref):
    col = place[1]
    atoms, rows = aout_ref.shape[0], tmid_ref.shape[0]
    added = dot_tn(gated_ref[...], exit_ref[...])
    update = (tmid_ref[...].astype(f32) + added).astype(bf16)
    tout_ref[...] = update
    sent = dot(update, back_ref[...]).astype(bf16)
    own = tokens_ref[...]
    onehot = (lax.broadcasted_iota(jnp.int32, (rows, atoms), 0) == own).astype(f32).astype(bf16)
    at = pl.multiple_of(col * atoms, atoms)
    mid = mid_ref[pl.ds(at, atoms), :].astype(f32)
    aout_ref[...] = (mid + dot_tn(onehot, sent)).astype(bf16)


def updates(place, gated, exit_w, tmid, back, mid, tokens, atoms):
    rows = tmid.shape[0]
    out_shape = [
        jax.ShapeDtypeStruct((rows, CS), bf16),
        jax.ShapeDtypeStruct((atoms, CA), bf16),
    ]
    return pl.pallas_call(
        update_body,
        grid=(1,),
        in_specs=[SMEM] + [full(a) for a in (gated, exit_w, tmid, back, mid, tokens)],
        out_specs=[full(shape) for shape in out_shape],
        out_shape=out_shape,
        compiler_params=pltpu.CompilerParams(vmem_limit_bytes=48 * 2**20),
        name="updates",
    )(place, gated, exit_w, tmid, back, mid, tokens)


def local(
    pair_tensor,
    token_single,
    atom_single,
    atom_token,
    chain_index,
    pair_up,
    pair_down,
    bias_heads,
    atom_gain,
    atom_proj,
    atom_exit,
    atom_pool,
    token_gain,
    token_proj,
    token_exit,
    chain_bias,
    token_back,
):
    rows, cols = pair_tensor.shape[:2]
    atom_rows = atom_single.shape[0]
    row_count = lax.axis_size("row")
    col_count = lax.axis_size("col")
    row = lax.axis_index("row")
    col = lax.axis_index("col")
    chips = col_count // 2
    row_atoms = atom_rows * col_count

    spread = lambda part, count: jnp.broadcast_to(part[None], (count,) + part.shape)
    both = ("row", "col")
    at = lambda r, k, core: r * col_count + 2 * k + core
    last = col_count - 1

    halo = lax.ppermute(
        jnp.where(col == last, atom_single[-HALO:], atom_single[:HALO]),
        both,
        [(r * col_count + last, (r + 1) * col_count) for r in range(row_count - 1)]
        + [((r + 1) * col_count, r * col_count + last) for r in range(row_count - 1)],
    )
    shards = lax.all_gather(
        jnp.concatenate([atom_single, halo, jnp.zeros_like(halo)], axis=0), "col", axis=0
    )
    ext_tokens = lax.dynamic_slice_in_dim(
        jnp.pad(atom_token, (HALO, HALO)), row * row_atoms, row_atoms + 2 * HALO
    )
    ext_tokens = (ext_tokens - row * rows)[None, :]
    own_tokens = lax.dynamic_slice_in_dim(
        atom_token, row * row_atoms + col * atom_rows, atom_rows
    )
    own_tokens = (own_tokens - row * rows)[None, :]

    flip = ((col == 2 * row + 1) | (col == 2 * row + 2)).astype(jnp.int32)
    place = jnp.stack([row, col, jnp.int32(row_count), flip]).astype(jnp.int32)
    center = jnp.asarray((np.eye(CZ) - 1.0 / CZ).astype(bf16))
    weights = (pair_up, pair_down, bias_heads, center)
    near, mid, far = BANDS
    token_bias, band_near = pair_chunk(place, pair_tensor, weights, (), 0, near, True)
    edge = lax.ppermute(
        band_near,
        both,
        [(at(r, r - 1, 1), at(r, r, 0)) for r in range(1, row_count)]
        + [(at(r, r + 1, 0), at(r, r, 1)) for r in range(row_count - 1)],
    )
    token_bias, band_mid = pair_chunk(
        place, pair_tensor, weights, (token_bias,), near, mid, True
    )

    here = col // 2 == row
    ring = chips // 2
    flat = lambda k, step: k // ring * ring + (k + step) % ring
    across = lambda k: (k + ring) % chips

    def over_y(band):
        band = jnp.where(here, band, jnp.zeros_like(band))
        return band + lax.ppermute(
            band,
            both,
            [(at(r, r, core), at(r, across(r), core)) for r in range(row_count) for core in range(2)],
        )

    def over_z(band):
        total = band
        for step in range(1, ring):
            total = total + lax.ppermute(
                band,
                both,
                [
                    (at(r, k, core), at(r, flat(k, step), core))
                    for r in range(row_count)
                    for k in (r, across(r))
                    for core in range(2)
                ],
            )
        return total, lax.ppermute(total, "col", [(i, i ^ 1) for i in range(col_count)])

    part_one = over_y(jnp.concatenate([band_near, band_mid, edge], axis=1))
    token_bias, band_far = pair_chunk(
        place, pair_tensor, weights, (token_bias,), near + mid, far, True
    )
    part_two = over_y(band_far)
    part_one, token_bias = lax.optimization_barrier((part_one, token_bias))
    bands_one = over_z(part_one)
    rest = near + mid + far
    (token_bias,) = pair_chunk(
        place, pair_tensor, weights, (token_bias,), rest, rows - rest, False
    )
    bands_two = over_z(part_two)
    token_bias, bands_one, bands_two = lax.optimization_barrier((token_bias, bands_one, bands_two))
    head_bias = lax.all_to_all(token_bias, "col", 0, 0)

    parts = project_atoms(shards, atom_gain[None], atom_proj, row_atoms)
    atom_mid, token_mid, query, gate, keyvals = atom_attention(
        place,
        (*bands_one, *bands_two),
        parts,
        ext_tokens,
        atom_exit,
        atom_pool,
        token_single,
        token_gain[None],
        token_proj,
    )
    keyvals = lax.all_to_all(spread(keyvals, row_count), "row", 0, 0)
    mine = lax.dynamic_slice_in_dim(chain_index, row * rows, rows)
    gated = token_attention(
        place, query, gate, keyvals, head_bias, mine[:, None], chain_index[None], chain_bias
    )
    gated = lax.all_to_all(gated, "col", 0, 0).reshape(CS, rows)
    return tuple(
        updates(
            place, gated, token_exit, token_mid, token_back, atom_mid, own_tokens, atom_rows
        )
    )


def solution(mesh):
    placed = (
        P("row", "col", None),
        P("row", None),
        P(("row", "col"), None),
    ) + (P(),) * 14
    return jax.shard_map(
        local,
        mesh=mesh,
        in_specs=placed,
        out_specs=(P("row", None), P(("row", "col"), None)),
        check_vma=False,
    )
```

```python
import functools

import jax
import jax.numpy as jnp
import numpy as np
from jax import lax
from jax.experimental import pallas as pl
from jax.experimental.pallas import tpu as pltpu
from jax.sharding import PartitionSpec as P

CZ = 128
CS = 768
CA = 128
HT = 16
HA = 4
PH = 256
QB = 32
KW = 128
HDA = 32
HDT = 48
HB = 20
HALO = 64
PART = 112
REACH = 208
GROUP = 1024
EPS = 1e-05

bf16 = jnp.bfloat16
f32 = jnp.float32


def dot(left, right):
    return jnp.dot(left, right, preferred_element_type=f32)


def dot_nt(left, right):
    return lax.dot_general(left, right, (((1,), (1,)), ((), ())), preferred_element_type=f32)


def dot_tn(left, right):
    return lax.dot_general(left, right, (((0,), (0,)), ((), ())), preferred_element_type=f32)


def centered(features):
    return features - jnp.mean(features, axis=-1, keepdims=True)


def scaled(center):
    spread = jnp.mean(center * center, axis=-1, keepdims=True)
    return center * lax.rsqrt(spread + EPS)


def sigmoid(value):
    return 0.5 + 0.5 * jnp.tanh(0.5 * value)


SMEM = pl.BlockSpec(memory_space=pltpu.SMEM)
ANY = pl.BlockSpec(memory_space=pl.ANY)


def full(array):
    return pl.BlockSpec(array.shape, lambda *_: (0,) * len(array.shape))


def held(arrays):
    return [pltpu.VMEM(a.shape, a.dtype) for a in arrays] + [
        pltpu.SemaphoreType.DMA((len(arrays),))
    ]


def fetch(sources, targets, sems):
    copies = [
        pltpu.make_async_copy(source, target, sems.at[i])
        for i, (source, target) in enumerate(zip(sources, targets))
    ]
    for copy in copies:
        copy.start()
    return copies


def pair_body(place, pair_ref, up_ref, down_ref, heads_ref, center_ref, *refs, bands):
    padded = refs[-1]
    outs = refs[-4:-1] if bands else refs[-2:-1]
    pair_part = pair_ref[...].reshape(-1, CZ)
    normed = scaled(dot(pair_part, center_ref[...])).astype(bf16)
    gate = dot(normed, up_ref[:, :PH] * bf16(0.5))
    value = dot(normed, up_ref[:, PH:])
    hidden = ((gate + gate * jnp.tanh(gate)) * value).astype(bf16)
    updated = pair_part.astype(f32) + dot(hidden, down_ref[...])
    normed_two = scaled(centered(updated)).astype(bf16)
    padded[...] = jnp.zeros_like(padded)
    padded[:HB, :] = heads_ref[...].astype(f32)
    biases = dot_nt(padded[...].astype(bf16), normed_two)
    rows = pair_ref.shape[0]
    stacked = jnp.stack([biases[:, i * CZ : (i + 1) * CZ] for i in range(rows)], axis=0)
    stacked = jnp.swapaxes(stacked, 0, 1)
    outs[0][...] = stacked[HA:HB].astype(bf16)
    if bands:
        outs[1][...] = stacked[:HA].astype(bf16)

        @pl.when(pl.program_id(0) == 0)
        def _():
            edge = jnp.where(place[3] == 1, stacked[:HA, rows - HALO :], stacked[:HA, :HALO])
            edge = pltpu.roll(edge.reshape(HA * HALO, CZ), HALO, 1)
            outs[2][...] = edge.reshape(HA, HALO, CZ).astype(bf16)


def pair_rows(place, pair, weights, before, first, size, count, bands):
    rows, cols = pair.shape[:2]

    def start(i, place):
        at = first + i * size
        return pl.multiple_of(at + place[3] * (rows - 2 * at - size), 16)

    in_specs = [
        pl.BlockSpec(
            (pl.Element(size), pl.Element(cols), pl.Element(CZ)),
            lambda i, place: (start(i, place), 0, 0),
        )
    ]
    in_specs += [full(array) for array in weights]
    out_shape = [jax.ShapeDtypeStruct((HT, rows, cols), bf16)]
    out_specs = [
        pl.BlockSpec(
            (pl.Element(HT), pl.Element(size), pl.Element(cols)),
            lambda i, place: (0, start(i, place), 0),
        )
    ]
    if bands:
        out_shape.append(jax.ShapeDtypeStruct((HA, size * count, cols), bf16))
        out_specs.append(
            pl.BlockSpec(
                (HA, size, cols),
                lambda i, place: (0, i + place[3] * (count - 1 - 2 * i), 0),
            )
        )
        out_shape.append(jax.ShapeDtypeStruct((HA, HALO, cols), bf16))
        out_specs.append(full(out_shape[-1]))
    aliases = {}
    if before:
        aliases = {2 + len(weights): 0}
        in_specs += [ANY]
    cells = size * count * cols
    return pl.pallas_call(
        functools.partial(pair_body, bands=bands),
        grid_spec=pltpu.PrefetchScalarGridSpec(
            num_scalar_prefetch=1,
            grid=(count,),
            in_specs=in_specs,
            out_specs=out_specs,
            scratch_shapes=[pltpu.VMEM((32, CZ), f32)],
        ),
        out_shape=out_shape,
        input_output_aliases=aliases,
        compiler_params=pltpu.CompilerParams(vmem_limit_bytes=56 * 2**20),
        cost_estimate=pl.CostEstimate(
            flops=cells * 500000, bytes_accessed=cells * 300, transcendentals=cells * PH
        ),
        name="pair",
    )(place, pair, *weights, *before)


def project_body(
    atoms_ref, before_ref, after_ref, gain_ref, proj_ref, ext_ref, query_ref, key_ref, value_ref, gate_ref
):
    atoms = atoms_ref.shape[0]
    ext_ref[:HALO] = before_ref[...]
    ext_ref[HALO : HALO + atoms] = atoms_ref[...]
    ext_ref[HALO + atoms :] = after_ref[...]
    normed = (scaled(centered(ext_ref[...].astype(f32))) * gain_ref[...]).astype(bf16)
    own = normed[HALO : HALO + atoms]
    query_ref[...] = (dot(own, proj_ref[:, :CA]) * HDA ** (-0.5)).astype(bf16)
    key_ref[...] = dot(normed, proj_ref[:, CA : 2 * CA]).astype(bf16)
    value_ref[...] = dot(normed, proj_ref[:, 2 * CA : 3 * CA]).astype(bf16)
    gate_ref[...] = sigmoid(dot(own, proj_ref[:, 3 * CA :]))


def project_atoms(atoms, before, after, gain, proj):
    count = atoms.shape[0]
    total = count + 2 * HALO
    operands = (atoms, before, after, gain, proj)
    out_shape = [
        jax.ShapeDtypeStruct((total, CA), bf16),
        jax.ShapeDtypeStruct((count, CA), bf16),
        jax.ShapeDtypeStruct((total, CA), bf16),
        jax.ShapeDtypeStruct((total, CA), bf16),
        jax.ShapeDtypeStruct((count, CA), f32),
    ]
    return pl.pallas_call(
        project_body,
        grid=(1,),
        in_specs=[full(array) for array in operands],
        out_specs=[full(shape) for shape in out_shape],
        out_shape=out_shape,
        compiler_params=pltpu.CompilerParams(vmem_limit_bytes=48 * 2**20),
        cost_estimate=pl.CostEstimate(flops=10**9, bytes_accessed=2**22, transcendentals=2**18),
        name="atom_projections",
    )(*operands)


def atoms_body(
    place,
    tokens_ref,
    exit_ref,
    pool_ref,
    single_ref,
    gain_ref,
    half_hbm,
    other_hbm,
    ext_hbm,
    query_hbm,
    key_hbm,
    value_hbm,
    gate_hbm,
    tproj_hbm,
    mid_ref,
    tmid_ref,
    tquery_ref,
    tgate_ref,
    tkv_ref,
    bias_ref,
    look_ref,
    sums_ref,
    half_ref,
    other_ref,
    ext_ref,
    query_ref,
    key_ref,
    value_ref,
    gate_ref,
    tproj_ref,
    sems,
):
    copies = fetch(
        (half_hbm, other_hbm, ext_hbm, query_hbm, key_hbm, value_hbm, gate_hbm, tproj_hbm),
        (half_ref, other_ref, ext_ref, query_ref, key_ref, value_ref, gate_ref, tproj_ref),
        sems,
    )
    for copy in copies[:-1]:
        copy.wait()
    row, col, row_count = place[0], place[1], place[2]
    total = ext_ref.shape[0]
    atoms = query_ref.shape[0]
    rows = single_ref.shape[0]
    even = lax.rem(col, 2) == 0
    rest = jnp.zeros((rows - REACH, KW), bf16)
    for h in range(HA):
        mine, theirs = half_ref[h], other_ref[h]
        first = jnp.where(even, mine, theirs)
        second = jnp.where(even, theirs, mine)
        base = h * 3 * KW
        bias_ref[:, base : base + KW] = jnp.concatenate([first, rest], axis=0)
        bias_ref[:, base + KW : base + 2 * KW] = jnp.concatenate([rest, second], axis=0)
        bias_ref[:, base + 2 * KW : base + 3 * KW] = jnp.concatenate(
            [first[REACH - HALO :], jnp.zeros((rows - 2 * HALO, KW), bf16), second[:HALO]], axis=0
        )
    lane = lax.broadcasted_iota(jnp.int32, (KW, 3 * KW), 1)
    for t in range(total // KW):
        at = slice(t * KW, (t + 1) * KW)
        tokens = jnp.broadcast_to(tokens_ref[:, at], (KW, KW)).astype(f32).T.astype(jnp.int32)
        tokens = jnp.concatenate([tokens] * 3, axis=1)
        tokens = jnp.where(
            tokens < 0,
            tokens + 2 * KW + HALO,
            jnp.where(tokens < 2 * KW, tokens, tokens + HALO),
        )
        look_ref[at, :CA] = key_ref[at, :]
        look_ref[at, CA:] = (tokens == lane).astype(f32).astype(bf16)
    head_of = lax.broadcasted_iota(jnp.int32, (QB, CA), 1) // HDA
    sums_ref[...] = jnp.zeros_like(sums_ref)
    row_lane = lax.broadcasted_iota(jnp.int32, (1, KW), 1)

    def group(g, counts):
        start = pl.multiple_of(g * GROUP, GROUP)
        own = pl.ds(start, GROUP)
        onehot = look_ref[pl.ds(pl.multiple_of(start + HALO, HALO), GROUP), CA : CA + 2 * KW]
        picked = dot(onehot, bias_ref[...]).astype(bf16)
        queries = query_ref[own, :]
        scores = []
        for b in range(GROUP // QB):
            part = slice(b * QB, (b + 1) * QB)
            left = jnp.concatenate(
                [
                    jnp.concatenate(
                        [
                            jnp.where(head_of == h, queries[part].astype(f32), 0.0).astype(bf16),
                            picked[part, h * 3 * KW : (h + 1) * 3 * KW],
                        ],
                        axis=1,
                    )
                    for h in range(HA)
                ],
                axis=0,
            )
            first = start + b * QB + HALO - (KW - QB) // 2
            window = look_ref[pl.ds(pl.multiple_of(first, 16), KW), :]
            at = row_lane + first
            inside = ((at >= HALO) | (row > 0)) & ((at < total - HALO) | (row < row_count - 1))
            scores.append(dot_nt(left, window) + jnp.where(inside, 0.0, -1e30))
        scores = jnp.concatenate(scores, axis=0)
        exps = jnp.exp(scores - jnp.max(scores, axis=-1, keepdims=True))
        inverse = 1.0 / jnp.sum(exps, axis=-1, keepdims=True)
        weights = exps.astype(bf16)
        attended = []
        for b in range(GROUP // QB):
            first = start + b * QB + HALO - (KW - QB) // 2
            part = slice(b * HA * QB, (b + 1) * HA * QB)
            out = dot(weights[part], value_ref[pl.ds(pl.multiple_of(first, 16), KW), :])
            out = out * inverse[part]
            merged = out[:QB]
            for h in range(1, HA):
                merged = jnp.where(head_of == h, out[h * QB : (h + 1) * QB], merged)
            attended.append(merged)
        attended = jnp.concatenate(attended, axis=0)
        gated = (attended * gate_ref[own, :]).astype(bf16)
        single = ext_ref[pl.ds(pl.multiple_of(start + HALO, HALO), GROUP), :].astype(f32)
        mid = (single + dot(gated, exit_ref[...])).astype(bf16)
        mid_ref[own, :] = mid
        pooled = jnp.maximum(dot(mid, pool_ref[...]), 0.0).astype(bf16)
        sums_ref[...] += dot_tn(onehot, pooled)
        return counts + jnp.sum(onehot.astype(f32).T, axis=1, keepdims=True)

    counts = lax.fori_loop(0, atoms // GROUP, group, jnp.zeros((rows, 1), f32))
    token_mid = (single_ref[...].astype(f32) + sums_ref[...] / counts).astype(bf16)
    tmid_ref[...] = token_mid
    normed = (scaled(centered(token_mid.astype(f32))) * gain_ref[...]).astype(bf16)

    copies[-1].wait()

    def head_part(part):
        start = part * CS + col * HDT
        base = jnp.minimum(start // KW * KW, 4 * CS - 2 * KW)
        base = pl.multiple_of(base, KW)
        wide = dot(normed, tproj_ref[:, pl.ds(base, 2 * KW)])
        return pltpu.roll(wide, lax.rem(2 * KW - (start - base), 2 * KW), 1)[:, :KW]

    tquery_ref[...] = head_part(0)[:, :HDT].astype(bf16)
    tgate_ref[...] = sigmoid(head_part(1)[:, :HDT])
    keyvals = jnp.concatenate([head_part(2).T[:HDT], head_part(3).T[:HDT]], axis=0).astype(bf16)
    for k in range(tkv_ref.shape[0]):
        tkv_ref[k] = keyvals


def atom_attention(place, bands, parts, tokens, exit_w, pool, single, gain, tproj, copies):
    total = parts[0].shape[0]
    atoms = total - 2 * HALO
    rows = single.shape[0]
    operands = (tokens, exit_w, pool, single, gain)
    fetched = (*bands, *parts, tproj)
    out_shape = [
        jax.ShapeDtypeStruct((atoms, CA), bf16),
        jax.ShapeDtypeStruct((rows, CS), bf16),
        jax.ShapeDtypeStruct((rows, HDT), bf16),
        jax.ShapeDtypeStruct((rows, HDT), f32),
        jax.ShapeDtypeStruct((copies, 2 * HDT, rows), bf16),
    ]
    return pl.pallas_call(
        atoms_body,
        grid=(1,),
        in_specs=[SMEM] + [full(array) for array in operands] + [ANY] * len(fetched),
        out_specs=[full(shape) for shape in out_shape],
        out_shape=out_shape,
        scratch_shapes=[
            pltpu.VMEM((rows, HA * 3 * KW), bf16),
            pltpu.VMEM((total, CA + 3 * KW), bf16),
            pltpu.VMEM((rows, CS), f32),
        ]
        + held(fetched),
        compiler_params=pltpu.CompilerParams(vmem_limit_bytes=56 * 2**20),
        cost_estimate=pl.CostEstimate(
            flops=10**10, bytes_accessed=2**24, transcendentals=2**22
        ),
        name="atoms",
    )(place, *operands, *fetched)


def tokens_body(
    place,
    strength,
    mine_ref,
    chain_ref,
    query_hbm,
    gate_hbm,
    kv_hbm,
    bias_hbm,
    out_ref,
    query_ref,
    gate_ref,
    kv_ref,
    bias_ref,
    sems,
):
    copies = fetch(
        (query_hbm, gate_hbm, kv_hbm, bias_hbm), (query_ref, gate_ref, kv_ref, bias_ref), sems
    )
    for copy in copies:
        copy.wait()
    col = place[1]
    rows = query_ref.shape[0]
    shards, cols = bias_ref.shape[0], bias_ref.shape[2]
    query = query_ref[...]
    strong = strength[col]
    scores = []
    for r in range(kv_ref.shape[0]):
        raw = dot(query, kv_ref[r, :HDT, :]) * HDT ** (-0.5)
        per = rows // cols
        bias = jnp.concatenate([bias_ref[r * per + k].astype(f32) for k in range(per)], axis=1)
        same = mine_ref[...] == chain_ref[:, r * rows : (r + 1) * rows]
        scores.append(raw + bias + jnp.where(same, strong, 0.0))
    top = scores[0]
    for part in scores[1:]:
        top = jnp.maximum(top, part)
    top = jnp.max(top, axis=-1, keepdims=True)
    exps = [jnp.exp(part - top) for part in scores]
    total = exps[0]
    for part in exps[1:]:
        total = total + part
    total = jnp.sum(total, axis=-1, keepdims=True)
    out = jnp.zeros((rows, HDT), f32)
    for r in range(kv_ref.shape[0]):
        out = out + dot_nt(exps[r].astype(bf16), kv_ref[r, HDT:, :])
    gated = out / total * gate_ref[...]
    wide = jnp.concatenate([gated, jnp.zeros((rows, KW - HDT), f32)], axis=1)
    gated = wide.T[:HDT].astype(bf16)
    for k in range(out_ref.shape[0]):
        out_ref[k] = gated


def token_attention(place, query, gate, kv, bias, mine, chain, strength):
    rows = query.shape[0]
    shards = bias.shape[0]
    out_shape = jax.ShapeDtypeStruct((shards, HDT, rows), bf16)
    return pl.pallas_call(
        tokens_body,
        grid=(1,),
        in_specs=[SMEM] * 2 + [full(mine), full(chain)] + [ANY] * 4,
        out_specs=full(out_shape),
        out_shape=out_shape,
        scratch_shapes=held((query, gate, kv, bias)),
        compiler_params=pltpu.CompilerParams(vmem_limit_bytes=48 * 2**20),
        cost_estimate=pl.CostEstimate(flops=10**9, bytes_accessed=2**22, transcendentals=2**19),
        name="tokens",
    )(place, strength, mine, chain, query, gate, kv, bias)


def update_body(
    place,
    exit_ref,
    back_ref,
    tokens_ref,
    gated_hbm,
    tmid_hbm,
    mid_hbm,
    tout_ref,
    aout_ref,
    gated_ref,
    tmid_ref,
    mid_ref,
    sems,
):
    col = place[1]
    atoms, rows = aout_ref.shape[0], tmid_ref.shape[0]
    at = pl.multiple_of(col * atoms, atoms)
    copies = fetch(
        (gated_hbm, tmid_hbm, mid_hbm.at[pl.ds(at, atoms)]), (gated_ref, tmid_ref, mid_ref), sems
    )
    for copy in copies:
        copy.wait()
    added = dot_tn(gated_ref[...], exit_ref[...])
    update = (tmid_ref[...].astype(f32) + added).astype(bf16)
    tout_ref[...] = update
    sent = dot(update, back_ref[...]).astype(bf16)
    own = tokens_ref[...]
    onehot = (lax.broadcasted_iota(jnp.int32, (rows, atoms), 0) == own).astype(f32).astype(bf16)
    aout_ref[...] = (mid_ref[...].astype(f32) + dot_tn(onehot, sent)).astype(bf16)


def updates(place, gated, exit_w, tmid, back, mid, tokens, atoms):
    rows = tmid.shape[0]
    out_shape = [
        jax.ShapeDtypeStruct((rows, CS), bf16),
        jax.ShapeDtypeStruct((atoms, CA), bf16),
    ]
    return pl.pallas_call(
        update_body,
        grid=(1,),
        in_specs=[SMEM] + [full(a) for a in (exit_w, back, tokens)] + [ANY] * 3,
        out_specs=[full(shape) for shape in out_shape],
        out_shape=out_shape,
        scratch_shapes=held((gated, tmid, jax.ShapeDtypeStruct((atoms, CA), bf16))),
        compiler_params=pltpu.CompilerParams(vmem_limit_bytes=48 * 2**20),
        name="updates",
    )(place, exit_w, back, tokens, gated, tmid, mid)


def local(
    pair_tensor,
    token_single,
    atom_single,
    atom_token,
    chain_index,
    pair_up,
    pair_down,
    bias_heads,
    atom_gain,
    atom_proj,
    atom_exit,
    atom_pool,
    token_gain,
    token_proj,
    token_exit,
    chain_bias,
    token_back,
):
    rows, cols = pair_tensor.shape[:2]
    atom_rows = atom_single.shape[0]
    row_count = lax.axis_size("row")
    col_count = lax.axis_size("col")
    row = lax.axis_index("row")
    col = lax.axis_index("col")
    chips = col_count // 2
    row_atoms = atom_rows * col_count

    both = ("row", "col")
    at = lambda r, k, core: r * col_count + 2 * k + core
    last = col_count - 1

    spread = jnp.broadcast_to(atom_single[None], (col_count,) + atom_single.shape)
    atoms = lax.all_to_all(spread, "col", 0, 0).reshape(row_atoms, CA)
    ext_tokens = lax.dynamic_slice_in_dim(
        jnp.pad(atom_token, (HALO, HALO)), row * row_atoms, row_atoms + 2 * HALO
    )
    ext_tokens = (ext_tokens - row * rows)[None, :]
    own_tokens = lax.dynamic_slice_in_dim(
        atom_token, row * row_atoms + col * atom_rows, atom_rows
    )
    own_tokens = (own_tokens - row * rows)[None, :]

    flip = ((col == 2 * row + 1) | (col == 2 * row + 2)).astype(jnp.int32)
    place = jnp.stack([row, col, jnp.int32(row_count), flip]).astype(jnp.int32)
    center = jnp.asarray((np.eye(CZ) - 1.0 / CZ).astype(bf16))
    weights = (pair_up, pair_down, bias_heads.T, center)
    token_bias, band, edge = pair_rows(place, pair_tensor, weights, (), 0, PART, 2, True)
    atoms, band, edge, token_bias = lax.optimization_barrier((atoms, band, edge, token_bias))

    up = [(i, i + 1) for i in range(row_count - 1)]
    down = [(i + 1, i) for i in range(row_count - 1)]
    before = lax.ppermute(atoms[-HALO:], "row", up)
    after = lax.ppermute(atoms[:HALO], "row", down)

    here = col // 2 == row
    even = col % 2 == 0
    ring = chips // 2
    flat = lambda k, step: k // ring * ring + (k + step) % ring
    across = lambda k: (k + ring) % chips
    band = jnp.where(
        here & even,
        band[:, :REACH],
        jnp.where(here, band[:, 2 * PART - REACH :], jnp.zeros_like(band[:, :REACH])),
    )
    band_y = lax.ppermute(
        band,
        both,
        [(at(r, r, core), at(r, across(r), core)) for r in range(row_count) for core in range(2)],
    )
    edges = [
        lax.ppermute(
            edge,
            both,
            [(at(r, r - 1, 1), at(r, to(r), 0)) for r in range(1, row_count)]
            + [(at(r, r + 1, 0), at(r, to(r), 1)) for r in range(row_count - 1)],
        )
        for to in (lambda r: r, across)
    ]
    (token_bias,) = pair_rows(
        place, pair_tensor, weights, (token_bias,), 2 * PART, rows - 2 * PART, 1, False
    )
    band_y, edges, before, after, token_bias = lax.optimization_barrier(
        (band_y, edges, before, after, token_bias)
    )
    edge = edges[0] + edges[1]
    blank = jnp.zeros((HA, REACH - HALO, cols), bf16)
    edge = jnp.where(
        even, jnp.concatenate([blank, edge], axis=1), jnp.concatenate([edge, blank], axis=1)
    )
    place_in = lax.broadcasted_iota(jnp.int32, band.shape, 1)
    lane = lax.broadcasted_iota(jnp.int32, band.shape, 2)
    spare = jnp.where(
        even, (place_in >= REACH - HALO) & (lane < HALO), (place_in < HALO) & (lane >= HALO)
    )
    band = jnp.where(spare, edge, band + band_y)
    sent = [
        lax.ppermute(
            band,
            both,
            [
                (at(r, k, core), at(r, flat(k, step), core))
                for r in range(row_count)
                for k in (r, across(r))
                for core in range(2)
            ],
        )
        for step in range(1, ring)
    ]
    parts = project_atoms(atoms, before, after, atom_gain[None], atom_proj)
    sent, parts = lax.optimization_barrier((sent, parts))
    band = band + sent[0] + sent[1] + sent[2]
    other = lax.ppermute(band, "col", [(i, i ^ 1) for i in range(col_count)])
    token_bias, band = lax.optimization_barrier((token_bias, band))
    head_bias = lax.all_to_all(token_bias, "col", 0, 0)

    atom_mid, token_mid, query, gate, keyvals = atom_attention(
        place,
        (band, other),
        parts,
        ext_tokens,
        atom_exit,
        atom_pool,
        token_single,
        token_gain[None],
        token_proj,
        row_count,
    )
    keyvals = lax.all_to_all(keyvals, "row", 0, 0)
    mine = lax.dynamic_slice_in_dim(chain_index, row * rows, rows)
    gated = token_attention(
        place, query, gate, keyvals, head_bias, mine[:, None], chain_index[None], chain_bias
    )
    gated = lax.all_to_all(gated, "col", 0, 0).reshape(CS, rows)
    return tuple(
        updates(
            place, gated, token_exit, token_mid, token_back, atom_mid, own_tokens, atom_rows
        )
    )


def solution(mesh):
    placed = (
        P("row", "col", None),
        P("row", None),
        P(("row", "col"), None),
    ) + (P(),) * 14
    return jax.shard_map(
        local,
        mesh=mesh,
        in_specs=placed,
        out_specs=(P("row", None), P(("row", "col"), None)),
        check_vma=False,
    )
```

```python
import functools

import jax
import jax.numpy as jnp
import numpy as np
from jax import lax
from jax.experimental import pallas as pl
from jax.experimental.pallas import tpu as pltpu
from jax.sharding import PartitionSpec as P

CZ = 128
CS = 768
CA = 128
HT = 16
HA = 4
PH = 256
QB = 32
KW = 128
HDA = 32
HDT = 48
HB = 20
HALO = 64
PART = 112
REACH = 208
GROUP = 1024
EPS = 1e-05

bf16 = jnp.bfloat16
f32 = jnp.float32


def dot(left, right):
    return jnp.dot(left, right, preferred_element_type=f32)


def dot_nt(left, right):
    return lax.dot_general(left, right, (((1,), (1,)), ((), ())), preferred_element_type=f32)


def dot_tn(left, right):
    return lax.dot_general(left, right, (((0,), (0,)), ((), ())), preferred_element_type=f32)


def centered(features):
    return features - jnp.mean(features, axis=-1, keepdims=True)


def scaled(center):
    spread = jnp.mean(center * center, axis=-1, keepdims=True)
    return center * lax.rsqrt(spread + EPS)


def sigmoid(value):
    return 0.5 + 0.5 * jnp.tanh(0.5 * value)


SMEM = pl.BlockSpec(memory_space=pltpu.SMEM)
ANY = pl.BlockSpec(memory_space=pl.ANY)
HBM = pl.BlockSpec(memory_space=pltpu.HBM)


def full(array):
    return pl.BlockSpec(array.shape, lambda *_: (0,) * len(array.shape))


def held(arrays):
    return [pltpu.VMEM(a.shape, a.dtype) for a in arrays] + [
        pltpu.SemaphoreType.DMA((len(arrays),))
    ]


def fetch(sources, targets, sems):
    copies = [
        pltpu.make_async_copy(source, target, sems.at[i])
        for i, (source, target) in enumerate(zip(sources, targets))
    ]
    for copy in copies:
        copy.start()
    return copies


def pair_body(place, pair_ref, up_ref, down_ref, heads_ref, center_ref, *refs, bands):
    padded = refs[-1]
    outs = refs[-4:-1] if bands else refs[-2:-1]
    pair_part = pair_ref[...].reshape(-1, CZ)
    normed = scaled(dot(pair_part, center_ref[...])).astype(bf16)
    gate = dot(normed, up_ref[:, :PH] * bf16(0.5))
    value = dot(normed, up_ref[:, PH:])
    hidden = ((gate + gate * jnp.tanh(gate)) * value).astype(bf16)
    updated = pair_part.astype(f32) + dot(hidden, down_ref[...])
    normed_two = scaled(centered(updated)).astype(bf16)
    padded[...] = jnp.zeros_like(padded)
    padded[:HB, :] = heads_ref[...].astype(f32)
    biases = dot_nt(padded[...].astype(bf16), normed_two)
    rows = pair_ref.shape[0]
    stacked = jnp.stack([biases[:, i * CZ : (i + 1) * CZ] for i in range(rows)], axis=0)
    stacked = jnp.swapaxes(stacked, 0, 1)
    outs[0][...] = stacked[HA:HB].astype(bf16)
    if bands:
        outs[1][...] = stacked[:HA].astype(bf16)

        @pl.when(pl.program_id(0) == 0)
        def _():
            edge = jnp.where(place[3] == 1, stacked[:HA, rows - HALO :], stacked[:HA, :HALO])
            edge = pltpu.roll(edge.reshape(HA * HALO, CZ), HALO, 1)
            outs[2][...] = edge.reshape(HA, HALO, CZ).astype(bf16)


def pair_rows(place, pair, weights, before, first, size, count, bands):
    rows, cols = pair.shape[:2]

    def start(i, place):
        at = first + i * size
        return pl.multiple_of(at + place[3] * (rows - 2 * at - size), 16)

    in_specs = [
        pl.BlockSpec(
            (pl.Element(size), pl.Element(cols), pl.Element(CZ)),
            lambda i, place: (start(i, place), 0, 0),
        )
    ]
    in_specs += [full(array) for array in weights]
    out_shape = [jax.ShapeDtypeStruct((HT, rows, cols), bf16)]
    out_specs = [
        pl.BlockSpec(
            (pl.Element(HT), pl.Element(size), pl.Element(cols)),
            lambda i, place: (0, start(i, place), 0),
        )
    ]
    if bands:
        out_shape.append(jax.ShapeDtypeStruct((HA, size * count, cols), bf16))
        out_specs.append(
            pl.BlockSpec(
                (HA, size, cols),
                lambda i, place: (0, i + place[3] * (count - 1 - 2 * i), 0),
            )
        )
        out_shape.append(jax.ShapeDtypeStruct((HA, HALO, cols), bf16))
        out_specs.append(full(out_shape[-1]))
    aliases = {}
    if before:
        aliases = {2 + len(weights): 0}
        in_specs += [ANY]
    cells = size * count * cols
    return pl.pallas_call(
        functools.partial(pair_body, bands=bands),
        grid_spec=pltpu.PrefetchScalarGridSpec(
            num_scalar_prefetch=1,
            grid=(count,),
            in_specs=in_specs,
            out_specs=out_specs,
            scratch_shapes=[pltpu.VMEM((32, CZ), f32)],
        ),
        out_shape=out_shape,
        input_output_aliases=aliases,
        compiler_params=pltpu.CompilerParams(vmem_limit_bytes=56 * 2**20),
        cost_estimate=pl.CostEstimate(
            flops=cells * 500000, bytes_accessed=cells * 300, transcendentals=cells * PH
        ),
        name="pair",
    )(place, pair, *weights, *before)


def project_body(shards_ref, gain_ref, proj_ref, ext_ref, query_ref, key_ref, value_ref, gate_ref):
    shards = shards_ref.shape[0]
    atoms = query_ref.shape[0]
    per = atoms // shards
    ext_ref[:HALO] = shards_ref[0, per:]
    for k in range(shards):
        ext_ref[HALO + k * per : HALO + (k + 1) * per] = shards_ref[k, :per]
    ext_ref[HALO + atoms :] = shards_ref[shards - 1, per:]
    normed = (scaled(centered(ext_ref[...].astype(f32))) * gain_ref[...]).astype(bf16)
    own = normed[HALO : HALO + atoms]
    query_ref[...] = (dot(own, proj_ref[:, :CA]) * HDA ** (-0.5)).astype(bf16)
    key_ref[...] = dot(normed, proj_ref[:, CA : 2 * CA]).astype(bf16)
    value_ref[...] = dot(normed, proj_ref[:, 2 * CA : 3 * CA]).astype(bf16)
    gate_ref[...] = sigmoid(dot(own, proj_ref[:, 3 * CA :]))


def project_atoms(shards, gain, proj):
    count = shards.shape[0] * (shards.shape[1] - HALO)
    total = count + 2 * HALO
    operands = (shards, gain, proj)
    out_shape = [
        jax.ShapeDtypeStruct((total, CA), bf16),
        jax.ShapeDtypeStruct((count, CA), bf16),
        jax.ShapeDtypeStruct((total, CA), bf16),
        jax.ShapeDtypeStruct((total, CA), bf16),
        jax.ShapeDtypeStruct((count, CA), f32),
    ]
    return pl.pallas_call(
        project_body,
        grid=(1,),
        in_specs=[full(array) for array in operands],
        out_specs=[full(shape) for shape in out_shape],
        out_shape=out_shape,
        compiler_params=pltpu.CompilerParams(vmem_limit_bytes=20 * 2**20),
        cost_estimate=pl.CostEstimate(flops=10**9, bytes_accessed=2**22, transcendentals=2**18),
        name="atom_projections",
    )(*operands)


def atoms_body(
    place,
    tokens_ref,
    exit_ref,
    pool_ref,
    single_ref,
    gain_ref,
    half_hbm,
    other_hbm,
    ext_hbm,
    query_hbm,
    key_hbm,
    value_hbm,
    gate_hbm,
    tproj_hbm,
    mid_ref,
    tmid_ref,
    state_ref,
    tkv_ref,
    bias_ref,
    look_ref,
    sums_ref,
    half_ref,
    other_ref,
    ext_ref,
    query_ref,
    key_ref,
    value_ref,
    gate_ref,
    tproj_ref,
    sems,
):
    copies = fetch(
        (half_hbm, other_hbm, ext_hbm, query_hbm, key_hbm, value_hbm, gate_hbm, tproj_hbm),
        (half_ref, other_ref, ext_ref, query_ref, key_ref, value_ref, gate_ref, tproj_ref),
        sems,
    )
    for copy in copies[:-1]:
        copy.wait()
    row, col, row_count = place[0], place[1], place[2]
    total = ext_ref.shape[0]
    atoms = query_ref.shape[0]
    rows = single_ref.shape[0]
    even = lax.rem(col, 2) == 0
    rest = jnp.zeros((rows - REACH, KW), bf16)
    for h in range(HA):
        mine, theirs = half_ref[h], other_ref[h]
        first = jnp.where(even, mine, theirs)
        second = jnp.where(even, theirs, mine)
        base = h * 3 * KW
        bias_ref[:, base : base + KW] = jnp.concatenate([first, rest], axis=0)
        bias_ref[:, base + KW : base + 2 * KW] = jnp.concatenate([rest, second], axis=0)
        bias_ref[:, base + 2 * KW : base + 3 * KW] = jnp.concatenate(
            [first[REACH - HALO :], jnp.zeros((rows - 2 * HALO, KW), bf16), second[:HALO]], axis=0
        )
    lane = lax.broadcasted_iota(jnp.int32, (KW, 3 * KW), 1)
    for t in range(total // KW):
        at = slice(t * KW, (t + 1) * KW)
        tokens = jnp.broadcast_to(tokens_ref[:, at], (KW, KW)).astype(f32).T.astype(jnp.int32)
        tokens = jnp.concatenate([tokens] * 3, axis=1)
        tokens = jnp.where(
            tokens < 0,
            tokens + 2 * KW + HALO,
            jnp.where(tokens < 2 * KW, tokens, tokens + HALO),
        )
        look_ref[at, :CA] = key_ref[at, :]
        look_ref[at, CA:] = (tokens == lane).astype(f32).astype(bf16)
    head_of = lax.broadcasted_iota(jnp.int32, (QB, CA), 1) // HDA
    sums_ref[...] = jnp.zeros_like(sums_ref)
    row_lane = lax.broadcasted_iota(jnp.int32, (1, KW), 1)

    def group(g, counts):
        start = pl.multiple_of(g * GROUP, GROUP)
        own = pl.ds(start, GROUP)
        onehot = look_ref[pl.ds(pl.multiple_of(start + HALO, HALO), GROUP), CA : CA + 2 * KW]
        picked = dot(onehot, bias_ref[...]).astype(bf16)
        queries = query_ref[own, :]
        scores = []
        for b in range(GROUP // QB):
            part = slice(b * QB, (b + 1) * QB)
            left = jnp.concatenate(
                [
                    jnp.concatenate(
                        [
                            jnp.where(head_of == h, queries[part].astype(f32), 0.0).astype(bf16),
                            picked[part, h * 3 * KW : (h + 1) * 3 * KW],
                        ],
                        axis=1,
                    )
                    for h in range(HA)
                ],
                axis=0,
            )
            first = start + b * QB + HALO - (KW - QB) // 2
            window = look_ref[pl.ds(pl.multiple_of(first, 16), KW), :]
            at = row_lane + first
            inside = ((at >= HALO) | (row > 0)) & ((at < total - HALO) | (row < row_count - 1))
            scores.append(dot_nt(left, window) + jnp.where(inside, 0.0, -1e30))
        scores = jnp.concatenate(scores, axis=0)
        exps = jnp.exp(scores - jnp.max(scores, axis=-1, keepdims=True))
        inverse = 1.0 / jnp.sum(exps, axis=-1, keepdims=True)
        weights = exps.astype(bf16)
        attended = []
        for b in range(GROUP // QB):
            first = start + b * QB + HALO - (KW - QB) // 2
            part = slice(b * HA * QB, (b + 1) * HA * QB)
            out = dot(weights[part], value_ref[pl.ds(pl.multiple_of(first, 16), KW), :])
            out = out * inverse[part]
            merged = out[:QB]
            for h in range(1, HA):
                merged = jnp.where(head_of == h, out[h * QB : (h + 1) * QB], merged)
            attended.append(merged)
        attended = jnp.concatenate(attended, axis=0)
        gated = (attended * gate_ref[own, :]).astype(bf16)
        single = ext_ref[pl.ds(pl.multiple_of(start + HALO, HALO), GROUP), :].astype(f32)
        mid = (single + dot(gated, exit_ref[...])).astype(bf16)
        mid_ref[own, :] = mid
        pooled = jnp.maximum(dot(mid, pool_ref[...]), 0.0).astype(bf16)
        sums_ref[...] += dot_tn(onehot, pooled)
        return counts + jnp.sum(onehot.astype(f32).T, axis=1, keepdims=True)

    counts = lax.fori_loop(0, atoms // GROUP, group, jnp.zeros((rows, 1), f32))
    token_mid = (single_ref[...].astype(f32) + sums_ref[...] / counts).astype(bf16)
    tmid_ref[...] = token_mid
    normed = (scaled(centered(token_mid.astype(f32))) * gain_ref[...]).astype(bf16)

    copies[-1].wait()

    def head_part(part):
        start = part * CS + col * HDT
        base = jnp.minimum(start // KW * KW, 4 * CS - 2 * KW)
        base = pl.multiple_of(base, KW)
        wide = dot(normed, tproj_ref[:, pl.ds(base, 2 * KW)])
        return pltpu.roll(wide, lax.rem(2 * KW - (start - base), 2 * KW), 1)[:, :KW]

    state_ref[...] = jnp.concatenate([head_part(0), sigmoid(head_part(1))], axis=1)
    keyvals = jnp.concatenate([head_part(2).T[:HDT], head_part(3).T[:HDT]], axis=0).astype(bf16)
    for k in range(tkv_ref.shape[0]):
        tkv_ref[k] = keyvals


def atom_attention(place, bands, parts, tokens, exit_w, pool, single, gain, tproj, copies):
    total = parts[0].shape[0]
    atoms = total - 2 * HALO
    rows = single.shape[0]
    operands = (tokens, exit_w, pool, single, gain)
    fetched = (*bands, *parts, tproj)
    out_shape = [
        jax.ShapeDtypeStruct((atoms, CA), bf16),
        jax.ShapeDtypeStruct((rows, CS), bf16),
        jax.ShapeDtypeStruct((rows, 2 * KW), f32),
        jax.ShapeDtypeStruct((copies, 2 * HDT, rows), bf16),
    ]
    return pl.pallas_call(
        atoms_body,
        grid=(1,),
        in_specs=[SMEM] + [full(array) for array in operands] + [ANY] * len(fetched),
        out_specs=[full(shape) for shape in out_shape],
        out_shape=out_shape,
        scratch_shapes=[
            pltpu.VMEM((rows, HA * 3 * KW), bf16),
            pltpu.VMEM((total, CA + 3 * KW), bf16),
            pltpu.VMEM((rows, CS), f32),
        ]
        + held(fetched),
        compiler_params=pltpu.CompilerParams(vmem_limit_bytes=44 * 2**20),
        cost_estimate=pl.CostEstimate(
            flops=10**10, bytes_accessed=2**24, transcendentals=2**22
        ),
        name="atoms",
    )(place, *operands, *fetched)


def tokens_body(
    place, strength, chain_ref, state_hbm, kv_hbm, bias_hbm, out_ref, state_ref, kv_ref, bias_ref, sems
):
    copies = fetch((state_hbm, kv_hbm, bias_hbm), (state_ref, kv_ref, bias_ref), sems)
    col = place[1]
    rows = state_ref.shape[0]
    own = pl.multiple_of(place[0] * rows, rows)
    mine = chain_ref[:, pl.ds(own, rows)].astype(f32)
    mine = jnp.broadcast_to(mine, (KW, rows)).T
    mine = jnp.concatenate([mine] * (rows // KW), axis=1).astype(jnp.int32)
    for copy in copies:
        copy.wait()
    query = state_ref[:, :HDT].astype(bf16)
    shards, cols = bias_ref.shape[0], bias_ref.shape[2]
    strong = strength[col]
    scores = []
    for r in range(kv_ref.shape[0]):
        raw = dot(query, kv_ref[r, :HDT, :]) * HDT ** (-0.5)
        per = rows // cols
        bias = jnp.concatenate([bias_ref[r * per + k].astype(f32) for k in range(per)], axis=1)
        same = mine == chain_ref[:, r * rows : (r + 1) * rows]
        scores.append(raw + bias + jnp.where(same, strong, 0.0))
    top = scores[0]
    for part in scores[1:]:
        top = jnp.maximum(top, part)
    top = jnp.max(top, axis=-1, keepdims=True)
    exps = [jnp.exp(part - top) for part in scores]
    total = exps[0]
    for part in exps[1:]:
        total = total + part
    total = jnp.sum(total, axis=-1, keepdims=True)
    out = jnp.zeros((rows, HDT), f32)
    for r in range(kv_ref.shape[0]):
        out = out + dot_nt(exps[r].astype(bf16), kv_ref[r, HDT:, :])
    gated = out / total * state_ref[:, KW : KW + HDT]
    wide = jnp.concatenate([gated, jnp.zeros((rows, KW - HDT), f32)], axis=1)
    gated = wide.T[:HDT].astype(bf16)
    for k in range(out_ref.shape[0]):
        out_ref[k] = gated


def token_attention(place, state, kv, bias, chain, strength):
    rows = state.shape[0]
    out_shape = jax.ShapeDtypeStruct((bias.shape[0], HDT, rows), bf16)
    return pl.pallas_call(
        tokens_body,
        grid=(1,),
        in_specs=[SMEM] * 2 + [full(chain)] + [HBM] * 3,
        out_specs=full(out_shape),
        out_shape=out_shape,
        scratch_shapes=held((state, kv, bias)),
        compiler_params=pltpu.CompilerParams(vmem_limit_bytes=24 * 2**20),
        cost_estimate=pl.CostEstimate(flops=10**9, bytes_accessed=2**22, transcendentals=2**19),
        name="tokens",
    )(place, strength, chain, state, kv, bias)


def update_body(
    place,
    tokens_ref,
    gated_hbm,
    exit_hbm,
    tmid_hbm,
    back_hbm,
    mid_hbm,
    tout_ref,
    aout_ref,
    gated_ref,
    exit_ref,
    tmid_ref,
    back_ref,
    mid_ref,
    sems,
):
    col = place[1]
    atoms, rows = aout_ref.shape[0], tmid_ref.shape[0]
    at = pl.multiple_of(col * atoms, atoms)
    copies = fetch(
        (gated_hbm, exit_hbm, tmid_hbm, back_hbm, mid_hbm.at[pl.ds(at, atoms)]),
        (gated_ref, exit_ref, tmid_ref, back_ref, mid_ref),
        sems,
    )
    for copy in copies:
        copy.wait()
    added = dot_tn(gated_ref[...], exit_ref[...])
    update = (tmid_ref[...].astype(f32) + added).astype(bf16)
    tout_ref[...] = update
    sent = dot(update, back_ref[...]).astype(bf16)
    own = tokens_ref[...]
    onehot = (lax.broadcasted_iota(jnp.int32, (rows, atoms), 0) == own).astype(f32).astype(bf16)
    aout_ref[...] = (mid_ref[...].astype(f32) + dot_tn(onehot, sent)).astype(bf16)


def updates(place, gated, exit_w, tmid, back, mid, tokens, atoms):
    rows = tmid.shape[0]
    out_shape = [
        jax.ShapeDtypeStruct((rows, CS), bf16),
        jax.ShapeDtypeStruct((atoms, CA), bf16),
    ]
    return pl.pallas_call(
        update_body,
        grid=(1,),
        in_specs=[SMEM, full(tokens)] + [HBM] * 5,
        out_specs=[full(shape) for shape in out_shape],
        out_shape=out_shape,
        scratch_shapes=held((gated, exit_w, tmid, back, jax.ShapeDtypeStruct((atoms, CA), bf16))),
        compiler_params=pltpu.CompilerParams(vmem_limit_bytes=24 * 2**20),
        name="updates",
    )(place, tokens, gated, exit_w, tmid, back, mid)


def local(
    pair_tensor,
    token_single,
    atom_single,
    atom_token,
    chain_index,
    pair_up,
    pair_down,
    bias_heads,
    atom_gain,
    atom_proj,
    atom_exit,
    atom_pool,
    token_gain,
    token_proj,
    token_exit,
    chain_bias,
    token_back,
):
    rows, cols = pair_tensor.shape[:2]
    atom_rows = atom_single.shape[0]
    row_count = lax.axis_size("row")
    col_count = lax.axis_size("col")
    row = lax.axis_index("row")
    col = lax.axis_index("col")
    chips = col_count // 2
    row_atoms = atom_rows * col_count

    both = ("row", "col")
    at = lambda r, k, core: r * col_count + 2 * k + core
    last = col_count - 1

    last = col_count - 1
    halo = lax.ppermute(
        jnp.where(col == last, atom_single[-HALO:], atom_single[:HALO]),
        both,
        [(r * col_count + last, (r + 1) * col_count) for r in range(row_count - 1)]
        + [((r + 1) * col_count, r * col_count + last) for r in range(row_count - 1)],
    )
    packed = jnp.concatenate([atom_single, halo], axis=0)
    spread = jnp.broadcast_to(packed[None], (col_count,) + packed.shape)
    ext_tokens = lax.dynamic_slice_in_dim(
        jnp.pad(atom_token, (HALO, HALO)), row * row_atoms, row_atoms + 2 * HALO
    )
    ext_tokens = (ext_tokens - row * rows)[None, :]
    own_tokens = lax.dynamic_slice_in_dim(
        atom_token, row * row_atoms + col * atom_rows, atom_rows
    )
    own_tokens = (own_tokens - row * rows)[None, :]

    flip = ((col == 2 * row + 1) | (col == 2 * row + 2)).astype(jnp.int32)
    place = jnp.stack([row, col, jnp.int32(row_count), flip]).astype(jnp.int32)
    spread, place = lax.optimization_barrier((spread, place))
    shards = lax.all_to_all(spread, "col", 0, 0)
    center = jnp.asarray((np.eye(CZ) - 1.0 / CZ).astype(bf16))
    weights = (pair_up, pair_down, bias_heads.T, center)
    token_bias, band, edge = pair_rows(place, pair_tensor, weights, (), 0, PART, 2, True)
    shards, band, edge, token_bias = lax.optimization_barrier((shards, band, edge, token_bias))

    here = col // 2 == row
    even = col % 2 == 0
    ring = chips // 2
    flat = lambda k, step: k // ring * ring + (k + step) % ring
    across = lambda k: (k + ring) % chips
    band = jnp.where(
        here & even,
        band[:, :REACH],
        jnp.where(here, band[:, 2 * PART - REACH :], jnp.zeros_like(band[:, :REACH])),
    )
    band_y = lax.ppermute(
        band,
        both,
        [(at(r, r, core), at(r, across(r), core)) for r in range(row_count) for core in range(2)],
    )
    edges = [
        lax.ppermute(
            edge,
            both,
            [(at(r, r - 1, 1), at(r, to(r), 0)) for r in range(1, row_count)]
            + [(at(r, r + 1, 0), at(r, to(r), 1)) for r in range(row_count - 1)],
        )
        for to in (lambda r: r, across)
    ]
    (token_bias,) = pair_rows(
        place, pair_tensor, weights, (token_bias,), 2 * PART, rows - 2 * PART, 1, False
    )
    band_y, edges, token_bias = lax.optimization_barrier((band_y, edges, token_bias))
    edge = edges[0] + edges[1]
    blank = jnp.zeros((HA, REACH - HALO, cols), bf16)
    edge = jnp.where(
        even, jnp.concatenate([blank, edge], axis=1), jnp.concatenate([edge, blank], axis=1)
    )
    place_in = lax.broadcasted_iota(jnp.int32, band.shape, 1)
    lane = lax.broadcasted_iota(jnp.int32, band.shape, 2)
    spare = jnp.where(
        even, (place_in >= REACH - HALO) & (lane < HALO), (place_in < HALO) & (lane >= HALO)
    )
    band = jnp.where(spare, edge, band + band_y)
    sent = [
        lax.ppermute(
            band,
            both,
            [
                (at(r, k, core), at(r, flat(k, step), core))
                for r in range(row_count)
                for k in (r, across(r))
                for core in range(2)
            ],
        )
        for step in range(1, ring)
    ]
    parts = project_atoms(shards, atom_gain[None], atom_proj)
    gain = token_gain[None]
    sent, parts, gain, ext_tokens = lax.optimization_barrier((sent, parts, gain, ext_tokens))
    band = band + sent[0] + sent[1] + sent[2]
    other = lax.ppermute(band, "col", [(i, i ^ 1) for i in range(col_count)])
    token_bias, band = lax.optimization_barrier((token_bias, band))
    head_bias = lax.all_to_all(token_bias, "col", 0, 0)

    atom_mid, token_mid, state, keyvals = atom_attention(
        place,
        (band, other),
        parts,
        ext_tokens,
        atom_exit,
        atom_pool,
        token_single,
        gain,
        token_proj,
        row_count,
    )
    keyvals, head_bias = lax.optimization_barrier((keyvals, head_bias))
    keyvals = lax.all_to_all(keyvals, "row", 0, 0)
    gated = token_attention(place, state, keyvals, head_bias, chain_index[None], chain_bias)
    gated = lax.all_to_all(gated, "col", 0, 0).reshape(CS, rows)
    return tuple(
        updates(
            place, gated, token_exit, token_mid, token_back, atom_mid, own_tokens, atom_rows
        )
    )


def solution(mesh):
    placed = (
        P("row", "col", None),
        P("row", None),
        P(("row", "col"), None),
    ) + (P(),) * 14
    return jax.shard_map(
        local,
        mesh=mesh,
        in_specs=placed,
        out_specs=(P("row", None), P(("row", "col"), None)),
        check_vma=False,
    )
```

```python
import functools

import jax
import jax.numpy as jnp
import numpy as np
from jax import lax
from jax.experimental import pallas as pl
from jax.experimental.pallas import tpu as pltpu
from jax.sharding import PartitionSpec as P

CZ = 128
CS = 768
CA = 128
HT = 16
HA = 4
PH = 256
QB = 32
KW = 128
HDA = 32
HDT = 48
HB = 20
HALO = 64
PART = 112
REACH = 208
GROUP = 1024
EPS = 1e-05

bf16 = jnp.bfloat16
f32 = jnp.float32


def dot(left, right):
    return jnp.dot(left, right, preferred_element_type=f32)


def dot_nt(left, right):
    return lax.dot_general(left, right, (((1,), (1,)), ((), ())), preferred_element_type=f32)


def dot_tn(left, right):
    return lax.dot_general(left, right, (((0,), (0,)), ((), ())), preferred_element_type=f32)


def centered(features):
    return features - jnp.mean(features, axis=-1, keepdims=True)


def scaled(center):
    spread = jnp.mean(center * center, axis=-1, keepdims=True)
    return center * lax.rsqrt(spread + EPS)


def sigmoid(value):
    return 0.5 + 0.5 * jnp.tanh(0.5 * value)


SMEM = pl.BlockSpec(memory_space=pltpu.SMEM)
ANY = pl.BlockSpec(memory_space=pl.ANY)
HBM = pl.BlockSpec(memory_space=pltpu.HBM)
VMEM = pl.BlockSpec(memory_space=pltpu.VMEM)


def full(array):
    return pl.BlockSpec(array.shape, lambda *_: (0,) * len(array.shape))


def held(arrays):
    return [pltpu.VMEM(a.shape, a.dtype) for a in arrays] + [
        pltpu.SemaphoreType.DMA((len(arrays),))
    ]


def fetch(sources, targets, sems):
    copies = [
        pltpu.make_async_copy(source, target, sems.at[i])
        for i, (source, target) in enumerate(zip(sources, targets))
    ]
    for copy in copies:
        copy.start()
    return copies


def pair_body(place, pair_ref, up_ref, down_ref, heads_ref, center_ref, *refs, bands):
    padded = refs[-1]
    outs = refs[-4:-1] if bands else refs[-2:-1]
    pair_part = pair_ref[...].reshape(-1, CZ)
    normed = scaled(dot(pair_part, center_ref[...])).astype(bf16)
    gate = dot(normed, up_ref[:, :PH] * bf16(0.5))
    value = dot(normed, up_ref[:, PH:])
    hidden = ((gate + gate * jnp.tanh(gate)) * value).astype(bf16)
    updated = pair_part.astype(f32) + dot(hidden, down_ref[...])
    normed_two = scaled(centered(updated)).astype(bf16)
    padded[...] = jnp.zeros_like(padded)
    padded[:HB, :] = heads_ref[...].astype(f32)
    biases = dot_nt(padded[...].astype(bf16), normed_two)
    rows = pair_ref.shape[0]
    stacked = jnp.stack([biases[:, i * CZ : (i + 1) * CZ] for i in range(rows)], axis=0)
    stacked = jnp.swapaxes(stacked, 0, 1)
    outs[0][...] = stacked[HA:HB].astype(bf16)
    if bands:
        outs[1][...] = stacked[:HA].astype(bf16)

        @pl.when(pl.program_id(0) == 0)
        def _():
            edge = jnp.where(place[3] == 1, stacked[:HA, rows - HALO :], stacked[:HA, :HALO])
            edge = pltpu.roll(edge.reshape(HA * HALO, CZ), HALO, 1)
            outs[2][...] = edge.reshape(HA, HALO, CZ).astype(bf16)


def pair_rows(place, pair, weights, before, first, size, count, bands):
    rows, cols = pair.shape[:2]

    def start(i, place):
        at = first + i * size
        return pl.multiple_of(at + place[3] * (rows - 2 * at - size), 16)

    in_specs = [
        pl.BlockSpec(
            (pl.Element(size), pl.Element(cols), pl.Element(CZ)),
            lambda i, place: (start(i, place), 0, 0),
        )
    ]
    in_specs += [full(array) for array in weights]
    out_shape = [jax.ShapeDtypeStruct((HT, rows, cols), bf16)]
    out_specs = [
        pl.BlockSpec(
            (pl.Element(HT), pl.Element(size), pl.Element(cols)),
            lambda i, place: (0, start(i, place), 0),
        )
    ]
    if bands:
        out_shape.append(jax.ShapeDtypeStruct((HA, size * count, cols), bf16))
        out_specs.append(
            pl.BlockSpec(
                (HA, size, cols),
                lambda i, place: (0, i + place[3] * (count - 1 - 2 * i), 0),
            )
        )
        out_shape.append(jax.ShapeDtypeStruct((HA, HALO, cols), bf16))
        out_specs.append(full(out_shape[-1]))
    aliases = {}
    if before:
        aliases = {2 + len(weights): 0}
        in_specs += [ANY]
    cells = size * count * cols
    return pl.pallas_call(
        functools.partial(pair_body, bands=bands),
        grid_spec=pltpu.PrefetchScalarGridSpec(
            num_scalar_prefetch=1,
            grid=(count,),
            in_specs=in_specs,
            out_specs=out_specs,
            scratch_shapes=[pltpu.VMEM((32, CZ), f32)],
        ),
        out_shape=out_shape,
        input_output_aliases=aliases,
        compiler_params=pltpu.CompilerParams(vmem_limit_bytes=56 * 2**20),
        cost_estimate=pl.CostEstimate(
            flops=cells * 500000, bytes_accessed=cells * 300, transcendentals=cells * PH
        ),
        name="pair",
    )(place, pair, *weights, *before)


def project_body(
    atoms_ref, before_ref, after_ref, gain_ref, proj_ref, *refs
):
    outs, (ext_ref, query_ref, key_ref, value_ref, gate_ref, sems) = refs[:5], refs[5:]
    atoms = atoms_ref.shape[0]
    ext_ref[:HALO] = before_ref[...]
    ext_ref[HALO : HALO + atoms] = atoms_ref[...]
    ext_ref[HALO + atoms :] = after_ref[...]
    normed = (scaled(centered(ext_ref[...].astype(f32))) * gain_ref[...]).astype(bf16)
    own = normed[HALO : HALO + atoms]
    query_ref[...] = (dot(own, proj_ref[:, :CA]) * HDA ** (-0.5)).astype(bf16)
    key_ref[...] = dot(normed, proj_ref[:, CA : 2 * CA]).astype(bf16)
    value_ref[...] = dot(normed, proj_ref[:, 2 * CA : 3 * CA]).astype(bf16)
    gate_ref[...] = sigmoid(dot(own, proj_ref[:, 3 * CA :]))
    for copy in fetch((ext_ref, query_ref, key_ref, value_ref, gate_ref), outs, sems):
        copy.wait()


def project_atoms(atoms, before, after, gain, proj):
    count = atoms.shape[0]
    total = count + 2 * HALO
    operands = (atoms, before, after, gain, proj)
    out_shape = [
        jax.ShapeDtypeStruct((total, CA), bf16),
        jax.ShapeDtypeStruct((count, CA), bf16),
        jax.ShapeDtypeStruct((total, CA), bf16),
        jax.ShapeDtypeStruct((total, CA), bf16),
        jax.ShapeDtypeStruct((count, CA), f32),
    ]
    return pl.pallas_call(
        project_body,
        grid=(1,),
        in_specs=[full(array) for array in operands],
        out_specs=[HBM] * len(out_shape),
        out_shape=out_shape,
        scratch_shapes=held(out_shape),
        compiler_params=pltpu.CompilerParams(vmem_limit_bytes=24 * 2**20),
        cost_estimate=pl.CostEstimate(flops=10**9, bytes_accessed=2**22, transcendentals=2**18),
        name="atom_projections",
    )(*operands)


def atoms_body(
    place,
    tokens_ref,
    exit_ref,
    pool_ref,
    single_ref,
    gain_ref,
    half_ref,
    other_ref,
    ext_hbm,
    query_hbm,
    key_hbm,
    value_hbm,
    gate_hbm,
    tproj_hbm,
    mid_hbm,
    tmid_hbm,
    state_hbm,
    tkv_hbm,
    bias_ref,
    look_ref,
    sums_ref,
    ext_ref,
    query_ref,
    key_ref,
    value_ref,
    gate_ref,
    tproj_ref,
    sems,
    mid_ref,
    tmid_ref,
    state_ref,
    tkv_ref,
    out_sems,
):
    copies = fetch(
        (ext_hbm, query_hbm, key_hbm, value_hbm, gate_hbm, tproj_hbm),
        (ext_ref, query_ref, key_ref, value_ref, gate_ref, tproj_ref),
        sems,
    )
    row, col, row_count = place[0], place[1], place[2]
    total = ext_ref.shape[0]
    atoms = query_ref.shape[0]
    rows = single_ref.shape[0]
    even = lax.rem(col, 2) == 0
    rest = jnp.zeros((rows - REACH, KW), bf16)
    for h in range(HA):
        mine, theirs = half_ref[h], other_ref[h]
        first = jnp.where(even, mine, theirs)
        second = jnp.where(even, theirs, mine)
        base = h * 3 * KW
        bias_ref[:, base : base + KW] = jnp.concatenate([first, rest], axis=0)
        bias_ref[:, base + KW : base + 2 * KW] = jnp.concatenate([rest, second], axis=0)
        bias_ref[:, base + 2 * KW : base + 3 * KW] = jnp.concatenate(
            [first[REACH - HALO :], jnp.zeros((rows - 2 * HALO, KW), bf16), second[:HALO]], axis=0
        )
    for copy in copies[:-1]:
        copy.wait()
    lane = lax.broadcasted_iota(jnp.int32, (KW, 3 * KW), 1)
    for t in range(total // KW):
        at = slice(t * KW, (t + 1) * KW)
        tokens = jnp.broadcast_to(tokens_ref[:, at], (KW, KW)).astype(f32).T.astype(jnp.int32)
        tokens = jnp.concatenate([tokens] * 3, axis=1)
        tokens = jnp.where(
            tokens < 0,
            tokens + 2 * KW + HALO,
            jnp.where(tokens < 2 * KW, tokens, tokens + HALO),
        )
        look_ref[at, :CA] = key_ref[at, :]
        look_ref[at, CA:] = (tokens == lane).astype(f32).astype(bf16)
    head_of = lax.broadcasted_iota(jnp.int32, (QB, CA), 1) // HDA
    sums_ref[...] = jnp.zeros_like(sums_ref)
    row_lane = lax.broadcasted_iota(jnp.int32, (1, KW), 1)

    def group(g, counts):
        start = pl.multiple_of(g * GROUP, GROUP)
        own = pl.ds(start, GROUP)
        onehot = look_ref[pl.ds(pl.multiple_of(start + HALO, HALO), GROUP), CA : CA + 2 * KW]
        picked = dot(onehot, bias_ref[...]).astype(bf16)
        queries = query_ref[own, :]
        scores = []
        for b in range(GROUP // QB):
            part = slice(b * QB, (b + 1) * QB)
            left = jnp.concatenate(
                [
                    jnp.concatenate(
                        [
                            jnp.where(head_of == h, queries[part].astype(f32), 0.0).astype(bf16),
                            picked[part, h * 3 * KW : (h + 1) * 3 * KW],
                        ],
                        axis=1,
                    )
                    for h in range(HA)
                ],
                axis=0,
            )
            first = start + b * QB + HALO - (KW - QB) // 2
            window = look_ref[pl.ds(pl.multiple_of(first, 16), KW), :]
            at = row_lane + first
            inside = ((at >= HALO) | (row > 0)) & ((at < total - HALO) | (row < row_count - 1))
            scores.append(dot_nt(left, window) + jnp.where(inside, 0.0, -1e30))
        scores = jnp.concatenate(scores, axis=0)
        exps = jnp.exp(scores - jnp.max(scores, axis=-1, keepdims=True))
        inverse = 1.0 / jnp.sum(exps, axis=-1, keepdims=True)
        weights = exps.astype(bf16)
        attended = []
        for b in range(GROUP // QB):
            first = start + b * QB + HALO - (KW - QB) // 2
            part = slice(b * HA * QB, (b + 1) * HA * QB)
            out = dot(weights[part], value_ref[pl.ds(pl.multiple_of(first, 16), KW), :])
            out = out * inverse[part]
            merged = out[:QB]
            for h in range(1, HA):
                merged = jnp.where(head_of == h, out[h * QB : (h + 1) * QB], merged)
            attended.append(merged)
        attended = jnp.concatenate(attended, axis=0)
        gated = (attended * gate_ref[own, :]).astype(bf16)
        single = ext_ref[pl.ds(pl.multiple_of(start + HALO, HALO), GROUP), :].astype(f32)
        mid = (single + dot(gated, exit_ref[...])).astype(bf16)
        mid_ref[own, :] = mid
        pooled = jnp.maximum(dot(mid, pool_ref[...]), 0.0).astype(bf16)
        sums_ref[...] += dot_tn(onehot, pooled)
        return counts + jnp.sum(onehot.astype(f32).T, axis=1, keepdims=True)

    counts = lax.fori_loop(0, atoms // GROUP, group, jnp.zeros((rows, 1), f32))
    token_mid = (single_ref[...].astype(f32) + sums_ref[...] / counts).astype(bf16)
    tmid_ref[...] = token_mid
    stores = fetch((mid_ref, tmid_ref), (mid_hbm, tmid_hbm), out_sems)
    normed = (scaled(centered(token_mid.astype(f32))) * gain_ref[...]).astype(bf16)

    copies[-1].wait()

    def head_part(part):
        start = part * CS + col * HDT
        base = jnp.minimum(start // KW * KW, 4 * CS - 2 * KW)
        base = pl.multiple_of(base, KW)
        wide = dot(normed, tproj_ref[:, pl.ds(base, 2 * KW)])
        return pltpu.roll(wide, lax.rem(2 * KW - (start - base), 2 * KW), 1)[:, :KW]

    state_ref[...] = jnp.concatenate([head_part(0), sigmoid(head_part(1))], axis=1)
    keyvals = jnp.concatenate([head_part(2).T[:HDT], head_part(3).T[:HDT]], axis=0)
    tkv_ref[...] = keyvals.astype(bf16)
    last = [(state_ref, state_hbm)] + [(tkv_ref, tkv_hbm.at[k]) for k in range(tkv_hbm.shape[0])]
    for i, (source, target) in enumerate(last):
        stores.append(pltpu.make_async_copy(source, target, out_sems.at[2 + i]))
        stores[-1].start()
    for copy in stores:
        copy.wait()


def atom_attention(place, bands, parts, tokens, exit_w, pool, single, gain, tproj, copies):
    total = parts[0].shape[0]
    atoms = total - 2 * HALO
    rows = single.shape[0]
    operands = (tokens, exit_w, pool, single, gain)
    fetched = (*parts, tproj)
    out_shape = [
        jax.ShapeDtypeStruct((atoms, CA), bf16),
        jax.ShapeDtypeStruct((rows, CS), bf16),
        jax.ShapeDtypeStruct((rows, 2 * KW), f32),
        jax.ShapeDtypeStruct((copies, 2 * HDT, rows), bf16),
    ]
    return pl.pallas_call(
        atoms_body,
        grid=(1,),
        in_specs=[SMEM]
        + [full(array) for array in operands]
        + [VMEM] * len(bands)
        + [HBM] * len(fetched),
        out_specs=[HBM] * len(out_shape),
        out_shape=out_shape,
        scratch_shapes=[
            pltpu.VMEM((rows, HA * 3 * KW), bf16),
            pltpu.VMEM((total, CA + 3 * KW), bf16),
            pltpu.VMEM((rows, CS), f32),
        ]
        + held(fetched)
        + [pltpu.VMEM(a.shape, a.dtype) for a in out_shape[:3]]
        + [pltpu.VMEM((2 * HDT, rows), bf16), pltpu.SemaphoreType.DMA((3 + copies,))],
        compiler_params=pltpu.CompilerParams(vmem_limit_bytes=44 * 2**20),
        cost_estimate=pl.CostEstimate(
            flops=10**10, bytes_accessed=2**24, transcendentals=2**22
        ),
        name="atoms",
    )(place, *operands, *bands, *fetched)


def tokens_body(
    place, strength, chain_ref, state_hbm, kv_hbm, bias_hbm, out_ref, state_ref, kv_ref, bias_ref, sems
):
    copies = fetch((state_hbm, kv_hbm, bias_hbm), (state_ref, kv_ref, bias_ref), sems)
    col = place[1]
    rows = state_ref.shape[0]
    own = pl.multiple_of(place[0] * rows, rows)
    mine = chain_ref[:, pl.ds(own, rows)].astype(f32)
    mine = jnp.broadcast_to(mine, (KW, rows)).T
    mine = jnp.concatenate([mine] * (rows // KW), axis=1).astype(jnp.int32)
    for copy in copies:
        copy.wait()
    query = state_ref[:, :HDT].astype(bf16)
    shards, cols = bias_ref.shape[0], bias_ref.shape[2]
    strong = strength[col]
    scores = []
    for r in range(kv_ref.shape[0]):
        raw = dot(query, kv_ref[r, :HDT, :]) * HDT ** (-0.5)
        per = rows // cols
        bias = jnp.concatenate([bias_ref[r * per + k].astype(f32) for k in range(per)], axis=1)
        same = mine == chain_ref[:, r * rows : (r + 1) * rows]
        scores.append(raw + bias + jnp.where(same, strong, 0.0))
    top = scores[0]
    for part in scores[1:]:
        top = jnp.maximum(top, part)
    top = jnp.max(top, axis=-1, keepdims=True)
    exps = [jnp.exp(part - top) for part in scores]
    total = exps[0]
    for part in exps[1:]:
        total = total + part
    total = jnp.sum(total, axis=-1, keepdims=True)
    out = jnp.zeros((rows, HDT), f32)
    for r in range(kv_ref.shape[0]):
        out = out + dot_nt(exps[r].astype(bf16), kv_ref[r, HDT:, :])
    gated = out / total * state_ref[:, KW : KW + HDT]
    wide = jnp.concatenate([gated, jnp.zeros((rows, KW - HDT), f32)], axis=1)
    gated = wide.T[:HDT].astype(bf16)
    for k in range(out_ref.shape[0]):
        out_ref[k] = gated


def token_attention(place, state, kv, bias, chain, strength):
    rows = state.shape[0]
    out_shape = jax.ShapeDtypeStruct((bias.shape[0], HDT, rows), bf16)
    return pl.pallas_call(
        tokens_body,
        grid=(1,),
        in_specs=[SMEM] * 2 + [full(chain)] + [HBM] * 3,
        out_specs=full(out_shape),
        out_shape=out_shape,
        scratch_shapes=held((state, kv, bias)),
        compiler_params=pltpu.CompilerParams(vmem_limit_bytes=24 * 2**20),
        cost_estimate=pl.CostEstimate(flops=10**9, bytes_accessed=2**22, transcendentals=2**19),
        name="tokens",
    )(place, strength, chain, state, kv, bias)


def update_body(
    place,
    tokens_ref,
    gated_hbm,
    exit_hbm,
    tmid_hbm,
    back_hbm,
    mid_hbm,
    tout_ref,
    aout_ref,
    gated_ref,
    exit_ref,
    tmid_ref,
    back_ref,
    mid_ref,
    sems,
):
    col = place[1]
    atoms, rows = aout_ref.shape[0], tmid_ref.shape[0]
    at = pl.multiple_of(col * atoms, atoms)
    copies = fetch(
        (gated_hbm, exit_hbm, tmid_hbm, back_hbm, mid_hbm.at[pl.ds(at, atoms)]),
        (gated_ref, exit_ref, tmid_ref, back_ref, mid_ref),
        sems,
    )
    for copy in copies:
        copy.wait()
    added = dot_tn(gated_ref[...], exit_ref[...])
    update = (tmid_ref[...].astype(f32) + added).astype(bf16)
    tout_ref[...] = update
    sent = dot(update, back_ref[...]).astype(bf16)
    own = tokens_ref[...]
    onehot = (lax.broadcasted_iota(jnp.int32, (rows, atoms), 0) == own).astype(f32).astype(bf16)
    aout_ref[...] = (mid_ref[...].astype(f32) + dot_tn(onehot, sent)).astype(bf16)


def updates(place, gated, exit_w, tmid, back, mid, tokens, atoms):
    rows = tmid.shape[0]
    out_shape = [
        jax.ShapeDtypeStruct((rows, CS), bf16),
        jax.ShapeDtypeStruct((atoms, CA), bf16),
    ]
    return pl.pallas_call(
        update_body,
        grid=(1,),
        in_specs=[SMEM, full(tokens)] + [HBM] * 5,
        out_specs=[full(shape) for shape in out_shape],
        out_shape=out_shape,
        scratch_shapes=held((gated, exit_w, tmid, back, jax.ShapeDtypeStruct((atoms, CA), bf16))),
        compiler_params=pltpu.CompilerParams(vmem_limit_bytes=24 * 2**20),
        name="updates",
    )(place, tokens, gated, exit_w, tmid, back, mid)


def local(
    pair_tensor,
    token_single,
    atom_single,
    atom_token,
    chain_index,
    pair_up,
    pair_down,
    bias_heads,
    atom_gain,
    atom_proj,
    atom_exit,
    atom_pool,
    token_gain,
    token_proj,
    token_exit,
    chain_bias,
    token_back,
):
    rows, cols = pair_tensor.shape[:2]
    atom_rows = atom_single.shape[0]
    row_count = lax.axis_size("row")
    col_count = lax.axis_size("col")
    row = lax.axis_index("row")
    col = lax.axis_index("col")
    chips = col_count // 2
    row_atoms = atom_rows * col_count

    both = ("row", "col")
    at = lambda r, k, core: r * col_count + 2 * k + core
    last = col_count - 1

    spread = jnp.broadcast_to(atom_single[None], (col_count,) + atom_single.shape)
    shards = lax.all_to_all(spread, "col", 0, 0)
    ext_tokens = lax.dynamic_slice_in_dim(
        jnp.pad(atom_token, (HALO, HALO)), row * row_atoms, row_atoms + 2 * HALO
    )
    ext_tokens = (ext_tokens - row * rows)[None, :]
    own_tokens = lax.dynamic_slice_in_dim(
        atom_token, row * row_atoms + col * atom_rows, atom_rows
    )
    own_tokens = (own_tokens - row * rows)[None, :]

    flip = ((col == 2 * row + 1) | (col == 2 * row + 2)).astype(jnp.int32)
    place = jnp.stack([row, col, jnp.int32(row_count), flip]).astype(jnp.int32)
    center = jnp.asarray((np.eye(CZ) - 1.0 / CZ).astype(bf16))
    weights = (pair_up, pair_down, bias_heads.T, center)
    token_bias, band, edge = pair_rows(place, pair_tensor, weights, (), 0, PART, 2, True)
    shards, band, edge, token_bias = lax.optimization_barrier((shards, band, edge, token_bias))

    here = col // 2 == row
    even = col % 2 == 0
    ring = chips // 2
    flat = lambda k, step: k // ring * ring + (k + step) % ring
    across = lambda k: (k + ring) % chips
    band = jnp.where(
        here & even,
        band[:, :REACH],
        jnp.where(here, band[:, 2 * PART - REACH :], jnp.zeros_like(band[:, :REACH])),
    )
    band_y = lax.ppermute(
        band,
        both,
        [(at(r, r, core), at(r, across(r), core)) for r in range(row_count) for core in range(2)],
    )
    edges = [
        lax.ppermute(
            edge,
            both,
            [(at(r, r - 1, 1), at(r, to(r), 0)) for r in range(1, row_count)]
            + [(at(r, r + 1, 0), at(r, to(r), 1)) for r in range(row_count - 1)],
        )
        for to in (lambda r: r, across)
    ]
    (token_bias,) = pair_rows(
        place, pair_tensor, weights, (token_bias,), 2 * PART, rows - 2 * PART, 1, False
    )
    band_y, edges, token_bias = lax.optimization_barrier((band_y, edges, token_bias))
    edge = edges[0] + edges[1]
    blank = jnp.zeros((HA, REACH - HALO, cols), bf16)
    edge = jnp.where(
        even, jnp.concatenate([blank, edge], axis=1), jnp.concatenate([edge, blank], axis=1)
    )
    place_in = lax.broadcasted_iota(jnp.int32, band.shape, 1)
    lane = lax.broadcasted_iota(jnp.int32, band.shape, 2)
    spare = jnp.where(
        even, (place_in >= REACH - HALO) & (lane < HALO), (place_in < HALO) & (lane >= HALO)
    )
    band = jnp.where(spare, edge, band + band_y)
    sent = [
        lax.ppermute(
            band,
            both,
            [
                (at(r, k, core), at(r, flat(k, step), core))
                for r in range(row_count)
                for k in (r, across(r))
                for core in range(2)
            ],
        )
        for step in range(1, ring)
    ]
    atoms, _ = lax.optimization_barrier((shards.reshape(row_atoms, CA), band))
    before = lax.ppermute(
        atoms[-HALO:], "row", [(i, i + 1) for i in range(row_count - 1)]
    )
    after = lax.ppermute(atoms[:HALO], "row", [(i + 1, i) for i in range(row_count - 1)])
    parts = project_atoms(atoms, before, after, atom_gain[None], atom_proj)
    gain = token_gain[None]
    parts, token_bias = lax.optimization_barrier((parts, token_bias))
    head_bias = lax.all_to_all(token_bias, "col", 0, 0)
    sent, parts, gain, ext_tokens = lax.optimization_barrier((sent, parts, gain, ext_tokens))
    band = band + sent[0] + sent[1] + sent[2]
    other = lax.ppermute(band, "col", [(i, i ^ 1) for i in range(col_count)])

    atom_mid, token_mid, state, keyvals = atom_attention(
        place,
        (band, other),
        parts,
        ext_tokens,
        atom_exit,
        atom_pool,
        token_single,
        gain,
        token_proj,
        row_count,
    )
    keyvals, head_bias = lax.optimization_barrier((keyvals, head_bias))
    keyvals = lax.all_to_all(keyvals, "row", 0, 0)
    gated = token_attention(place, state, keyvals, head_bias, chain_index[None], chain_bias)
    gated = lax.all_to_all(gated, "col", 0, 0).reshape(CS, rows)
    return tuple(
        updates(
            place, gated, token_exit, token_mid, token_back, atom_mid, own_tokens, atom_rows
        )
    )


def solution(mesh):
    placed = (
        P("row", "col", None),
        P("row", None),
        P(("row", "col"), None),
    ) + (P(),) * 14
    return jax.shard_map(
        local,
        mesh=mesh,
        in_specs=placed,
        out_specs=(P("row", None), P(("row", "col"), None)),
        check_vma=False,
    )
```

```python
import functools

import jax
import jax.numpy as jnp
import numpy as np
from jax import lax
from jax.experimental import pallas as pl
from jax.experimental.pallas import tpu as pltpu
from jax.sharding import PartitionSpec as P

CZ = 128
CS = 768
CA = 128
HT = 16
HA = 4
PH = 256
QB = 32
KW = 128
HDA = 32
HDT = 48
HB = 20
HALO = 64
PART = 112
REACH = 208
GROUP = 1024
EPS = 1e-05
GRANT = 60 * 2**20

bf16 = jnp.bfloat16
f32 = jnp.float32


def dot(left, right):
    return jnp.dot(left, right, preferred_element_type=f32)


def dot_nt(left, right):
    return lax.dot_general(left, right, (((1,), (1,)), ((), ())), preferred_element_type=f32)


def dot_tn(left, right):
    return lax.dot_general(left, right, (((0,), (0,)), ((), ())), preferred_element_type=f32)


def centered(features):
    return features - jnp.mean(features, axis=-1, keepdims=True)


def scaled(center):
    spread = jnp.mean(center * center, axis=-1, keepdims=True)
    return center * lax.rsqrt(spread + EPS)


def sigmoid(value):
    return 0.5 + 0.5 * jnp.tanh(0.5 * value)


SMEM = pl.BlockSpec(memory_space=pltpu.SMEM)
ANY = pl.BlockSpec(memory_space=pl.ANY)
HBM = pl.BlockSpec(memory_space=pltpu.HBM)
VMEM = pl.BlockSpec(memory_space=pltpu.VMEM)


def full(array):
    return pl.BlockSpec(array.shape, lambda *_: (0,) * len(array.shape))


def held(arrays):
    return [pltpu.VMEM(a.shape, a.dtype) for a in arrays] + [
        pltpu.SemaphoreType.DMA((len(arrays),))
    ]


def fetch(sources, targets, sems):
    copies = [
        pltpu.make_async_copy(source, target, sems.at[i])
        for i, (source, target) in enumerate(zip(sources, targets))
    ]
    for copy in copies:
        copy.start()
    return copies


def pair_body(place, pair_ref, up_ref, down_ref, heads_ref, center_ref, *refs, bands):
    padded = refs[-1]
    outs = refs[-4:-1] if bands else refs[-2:-1]
    pair_part = pair_ref[...].reshape(-1, CZ)
    normed = scaled(dot(pair_part, center_ref[...])).astype(bf16)
    gate = dot(normed, up_ref[:, :PH] * bf16(0.5))
    value = dot(normed, up_ref[:, PH:])
    hidden = ((gate + gate * jnp.tanh(gate)) * value).astype(bf16)
    updated = pair_part.astype(f32) + dot(hidden, down_ref[...])
    normed_two = scaled(centered(updated)).astype(bf16)
    padded[...] = jnp.zeros_like(padded)
    padded[:HB, :] = heads_ref[...].astype(f32)
    biases = dot_nt(padded[...].astype(bf16), normed_two)
    rows = pair_ref.shape[0]
    stacked = jnp.stack([biases[:, i * CZ : (i + 1) * CZ] for i in range(rows)], axis=0)
    stacked = jnp.swapaxes(stacked, 0, 1)
    outs[0][...] = stacked[HA:HB].astype(bf16)
    if bands:
        outs[1][...] = stacked[:HA].astype(bf16)

        @pl.when(pl.program_id(0) == 0)
        def _():
            edge = jnp.where(place[3] == 1, stacked[:HA, rows - HALO :], stacked[:HA, :HALO])
            edge = pltpu.roll(edge.reshape(HA * HALO, CZ), HALO, 1)
            outs[2][...] = edge.reshape(HA, HALO, CZ).astype(bf16)


def pair_rows(place, pair, weights, before, first, size, count, bands):
    rows, cols = pair.shape[:2]

    def start(i, place):
        at = first + i * size
        return pl.multiple_of(at + place[3] * (rows - 2 * at - size), 16)

    in_specs = [
        pl.BlockSpec(
            (pl.Element(size), pl.Element(cols), pl.Element(CZ)),
            lambda i, place: (start(i, place), 0, 0),
        )
    ]
    in_specs += [full(array) for array in weights]
    out_shape = [jax.ShapeDtypeStruct((HT, rows, cols), bf16)]
    out_specs = [
        pl.BlockSpec(
            (pl.Element(HT), pl.Element(size), pl.Element(cols)),
            lambda i, place: (0, start(i, place), 0),
        )
    ]
    if bands:
        out_shape.append(jax.ShapeDtypeStruct((HA, size * count, cols), bf16))
        out_specs.append(
            pl.BlockSpec(
                (HA, size, cols),
                lambda i, place: (0, i + place[3] * (count - 1 - 2 * i), 0),
            )
        )
        out_shape.append(jax.ShapeDtypeStruct((HA, HALO, cols), bf16))
        out_specs.append(full(out_shape[-1]))
    aliases = {}
    if before:
        aliases = {2 + len(weights): 0}
        in_specs += [ANY]
    cells = size * count * cols
    return pl.pallas_call(
        functools.partial(pair_body, bands=bands),
        grid_spec=pltpu.PrefetchScalarGridSpec(
            num_scalar_prefetch=1,
            grid=(count,),
            in_specs=in_specs,
            out_specs=out_specs,
            scratch_shapes=[pltpu.VMEM((32, CZ), f32)],
        ),
        out_shape=out_shape,
        input_output_aliases=aliases,
        compiler_params=pltpu.CompilerParams(vmem_limit_bytes=56 * 2**20),
        cost_estimate=pl.CostEstimate(
            flops=cells * 500000, bytes_accessed=cells * 300, transcendentals=cells * PH
        ),
        name="pair",
    )(place, pair, *weights, *before)


def project_body(place, mine_ref, theirs_ref, gain_ref, proj_ref, *refs):
    outs, (atoms_ref, query_ref, key_ref, value_ref, gate_ref, sems) = refs[:5], refs[5:]
    even = lax.rem(place[1], 2) == 0
    per = mine_ref.shape[1]
    for k in range(mine_ref.shape[0]):
        mine, theirs = mine_ref[k], theirs_ref[k]
        start = 2 * k * per
        atoms_ref[start : start + per] = jnp.where(even, mine, theirs)
        atoms_ref[start + per : start + 2 * per] = jnp.where(even, theirs, mine)
    normed = (scaled(centered(atoms_ref[...].astype(f32))) * gain_ref[...]).astype(bf16)
    query_ref[...] = (dot(normed, proj_ref[:, :CA]) * HDA ** (-0.5)).astype(bf16)
    key_ref[...] = dot(normed, proj_ref[:, CA : 2 * CA]).astype(bf16)
    value_ref[...] = dot(normed, proj_ref[:, 2 * CA : 3 * CA]).astype(bf16)
    gate_ref[...] = sigmoid(dot(normed, proj_ref[:, 3 * CA :]))
    for copy in fetch((atoms_ref, query_ref, key_ref, value_ref, gate_ref), outs, sems):
        copy.wait()


def project_atoms(place, mine, theirs, gain, proj):
    count = 2 * mine.shape[0] * mine.shape[1]
    operands = (mine, theirs, gain, proj)
    out_shape = [jax.ShapeDtypeStruct((count, CA), bf16)] * 4
    out_shape += [jax.ShapeDtypeStruct((count, CA), f32)]
    return pl.pallas_call(
        project_body,
        grid=(1,),
        in_specs=[SMEM] + [full(array) for array in operands],
        out_specs=[HBM] * len(out_shape),
        out_shape=out_shape,
        scratch_shapes=held(out_shape),
        compiler_params=pltpu.CompilerParams(vmem_limit_bytes=GRANT),
        cost_estimate=pl.CostEstimate(flops=10**9, bytes_accessed=2**22, transcendentals=2**18),
        name="atom_projections",
    )(place, *operands)


def atoms_body(
    place,
    tokens_ref,
    atom_gain_ref,
    proj_ref,
    exit_ref,
    pool_ref,
    single_ref,
    gain_ref,
    half_ref,
    other_ref,
    atoms_hbm,
    query_hbm,
    key_hbm,
    value_hbm,
    gate_hbm,
    tproj_hbm,
    mid_hbm,
    tmid_hbm,
    state_hbm,
    tkv_hbm,
    bias_ref,
    look_ref,
    sums_ref,
    value_ref,
    atoms_ref,
    query_ref,
    key_ref,
    gate_ref,
    tproj_ref,
    sems,
    mid_ref,
    tmid_ref,
    state_ref,
    tkv_ref,
    out_sems,
):
    copies = fetch(
        (atoms_hbm, query_hbm, key_hbm, value_hbm, gate_hbm, tproj_hbm),
        (
            atoms_ref,
            query_ref,
            key_ref,
            value_ref.at[HALO : HALO + atoms_ref.shape[0]],
            gate_ref,
            tproj_ref,
        ),
        sems,
    )
    row, col, row_count = place[0], place[1], place[2]
    total = look_ref.shape[0]
    atoms = query_ref.shape[0]
    rows = single_ref.shape[0]
    even = lax.rem(col, 2) == 0
    rest = jnp.zeros((rows - REACH, KW), bf16)
    before, after = [], []
    for h in range(HA):
        mine, theirs = half_ref[h], other_ref[h]
        mine, theirs = jnp.where(even, mine, theirs), jnp.where(even, theirs, mine)
        first, second = mine[:REACH], theirs[:REACH]
        before.append(mine[REACH:])
        after.append(theirs[REACH:])
        base = h * 3 * KW
        bias_ref[:, base : base + KW] = jnp.concatenate([first, rest], axis=0)
        bias_ref[:, base + KW : base + 2 * KW] = jnp.concatenate([rest, second], axis=0)
        bias_ref[:, base + 2 * KW : base + 3 * KW] = jnp.concatenate(
            [first[REACH - HALO :], jnp.zeros((rows - 2 * HALO, KW), bf16), second[:HALO]], axis=0
        )
    near = jnp.concatenate(before + after, axis=0).astype(f32)
    near = (scaled(centered(near)) * atom_gain_ref[...]).astype(bf16)
    near_keys = dot(near, proj_ref[:, CA : 2 * CA]).astype(bf16)
    near_values = dot(near, proj_ref[:, 2 * CA : 3 * CA]).astype(bf16)
    for copy in copies[:-1]:
        copy.wait()
    look_ref[:HALO, :CA] = near_keys[:HALO]
    look_ref[HALO : HALO + atoms, :CA] = key_ref[...]
    look_ref[HALO + atoms :, :CA] = near_keys[HALO:]
    value_ref[:HALO] = near_values[:HALO]
    value_ref[HALO + atoms :] = near_values[HALO:]
    lane = lax.broadcasted_iota(jnp.int32, (KW, 3 * KW), 1)
    for t in range(total // KW):
        at = slice(t * KW, (t + 1) * KW)
        tokens = jnp.broadcast_to(tokens_ref[:, at], (KW, KW)).astype(f32).T.astype(jnp.int32)
        tokens = jnp.concatenate([tokens] * 3, axis=1)
        tokens = jnp.where(
            tokens < 0,
            tokens + 2 * KW + HALO,
            jnp.where(tokens < 2 * KW, tokens, tokens + HALO),
        )
        look_ref[at, CA:] = (tokens == lane).astype(f32).astype(bf16)
    head_of = lax.broadcasted_iota(jnp.int32, (QB, CA), 1) // HDA
    sums_ref[...] = jnp.zeros_like(sums_ref)
    row_lane = lax.broadcasted_iota(jnp.int32, (1, KW), 1)

    def group(g, counts):
        start = pl.multiple_of(g * GROUP, GROUP)
        own = pl.ds(start, GROUP)
        onehot = look_ref[pl.ds(pl.multiple_of(start + HALO, HALO), GROUP), CA : CA + 2 * KW]
        picked = dot(onehot, bias_ref[...]).astype(bf16)
        queries = query_ref[own, :]
        scores = []
        for b in range(GROUP // QB):
            part = slice(b * QB, (b + 1) * QB)
            left = jnp.concatenate(
                [
                    jnp.concatenate(
                        [
                            jnp.where(head_of == h, queries[part].astype(f32), 0.0).astype(bf16),
                            picked[part, h * 3 * KW : (h + 1) * 3 * KW],
                        ],
                        axis=1,
                    )
                    for h in range(HA)
                ],
                axis=0,
            )
            first = start + b * QB + HALO - (KW - QB) // 2
            window = look_ref[pl.ds(pl.multiple_of(first, 16), KW), :]
            at = row_lane + first
            inside = ((at >= HALO) | (row > 0)) & ((at < total - HALO) | (row < row_count - 1))
            scores.append(dot_nt(left, window) + jnp.where(inside, 0.0, -1e30))
        scores = jnp.concatenate(scores, axis=0)
        exps = jnp.exp(scores - jnp.max(scores, axis=-1, keepdims=True))
        inverse = 1.0 / jnp.sum(exps, axis=-1, keepdims=True)
        weights = exps.astype(bf16)
        attended = []
        for b in range(GROUP // QB):
            first = start + b * QB + HALO - (KW - QB) // 2
            part = slice(b * HA * QB, (b + 1) * HA * QB)
            out = dot(weights[part], value_ref[pl.ds(pl.multiple_of(first, 16), KW), :])
            out = out * inverse[part]
            merged = out[:QB]
            for h in range(1, HA):
                merged = jnp.where(head_of == h, out[h * QB : (h + 1) * QB], merged)
            attended.append(merged)
        attended = jnp.concatenate(attended, axis=0)
        gated = (attended * gate_ref[own, :]).astype(bf16)
        single = atoms_ref[own, :].astype(f32)
        mid = (single + dot(gated, exit_ref[...])).astype(bf16)
        mid_ref[own, :] = mid
        pooled = jnp.maximum(dot(mid, pool_ref[...]), 0.0).astype(bf16)
        sums_ref[...] += dot_tn(onehot, pooled)
        return counts + jnp.sum(onehot.astype(f32).T, axis=1, keepdims=True)

    counts = lax.fori_loop(0, atoms // GROUP, group, jnp.zeros((rows, 1), f32))
    token_mid = (single_ref[...].astype(f32) + sums_ref[...] / counts).astype(bf16)
    tmid_ref[...] = token_mid
    stores = fetch((mid_ref, tmid_ref), (mid_hbm, tmid_hbm), out_sems)
    normed = (scaled(centered(token_mid.astype(f32))) * gain_ref[...]).astype(bf16)

    copies[-1].wait()

    def head_part(part):
        start = part * CS + col * HDT
        base = jnp.minimum(start // KW * KW, 4 * CS - 2 * KW)
        base = pl.multiple_of(base, KW)
        wide = dot(normed, tproj_ref[:, pl.ds(base, 2 * KW)])
        return pltpu.roll(wide, lax.rem(2 * KW - (start - base), 2 * KW), 1)[:, :KW]

    state_ref[...] = jnp.concatenate([head_part(0), sigmoid(head_part(1))], axis=1)
    keyvals = jnp.concatenate([head_part(2).T[:HDT], head_part(3).T[:HDT]], axis=0)
    tkv_ref[...] = keyvals.astype(bf16)
    last = [(state_ref, state_hbm)] + [(tkv_ref, tkv_hbm.at[k]) for k in range(tkv_hbm.shape[0])]
    for i, (source, target) in enumerate(last):
        stores.append(pltpu.make_async_copy(source, target, out_sems.at[2 + i]))
        stores[-1].start()
    for copy in stores:
        copy.wait()


def atom_attention(
    place, bands, parts, tokens, atom_gain, proj, exit_w, pool, single, gain, tproj, copies
):
    atoms = parts[0].shape[0]
    total = atoms + 2 * HALO
    rows = single.shape[0]
    operands = (tokens, atom_gain, proj, exit_w, pool, single, gain)
    fetched = (*parts, tproj)
    out_shape = [
        jax.ShapeDtypeStruct((atoms, CA), bf16),
        jax.ShapeDtypeStruct((rows, CS), bf16),
        jax.ShapeDtypeStruct((rows, 2 * KW), f32),
        jax.ShapeDtypeStruct((copies, 2 * HDT, rows), bf16),
    ]
    return pl.pallas_call(
        atoms_body,
        grid=(1,),
        in_specs=[SMEM]
        + [full(array) for array in operands]
        + [VMEM] * len(bands)
        + [HBM] * len(fetched),
        out_specs=[HBM] * len(out_shape),
        out_shape=out_shape,
        scratch_shapes=[
            pltpu.VMEM((rows, HA * 3 * KW), bf16),
            pltpu.VMEM((total, CA + 3 * KW), bf16),
            pltpu.VMEM((rows, CS), f32),
            pltpu.VMEM((total, CA), bf16),
        ]
        + held((*parts[:3], *parts[4:], tproj))[:-1]
        + [pltpu.SemaphoreType.DMA((len(fetched),))]
        + [pltpu.VMEM(a.shape, a.dtype) for a in out_shape[:3]]
        + [pltpu.VMEM((2 * HDT, rows), bf16), pltpu.SemaphoreType.DMA((3 + copies,))],
        compiler_params=pltpu.CompilerParams(vmem_limit_bytes=GRANT),
        cost_estimate=pl.CostEstimate(
            flops=10**10, bytes_accessed=2**24, transcendentals=2**22
        ),
        name="atoms",
    )(place, *operands, *bands, *fetched)


def tokens_body(
    place, strength, chain_ref, state_hbm, kv_hbm, bias_hbm, out_ref, state_ref, kv_ref, bias_ref, sems
):
    copies = fetch((state_hbm, kv_hbm, bias_hbm), (state_ref, kv_ref, bias_ref), sems)
    col = place[1]
    rows = state_ref.shape[0]
    own = pl.multiple_of(place[0] * rows, rows)
    mine = chain_ref[:, pl.ds(own, rows)].astype(f32)
    mine = jnp.broadcast_to(mine, (KW, rows)).T
    mine = jnp.concatenate([mine] * (rows // KW), axis=1).astype(jnp.int32)
    for copy in copies:
        copy.wait()
    query = state_ref[:, :HDT].astype(bf16)
    shards, cols = bias_ref.shape[0], bias_ref.shape[2]
    strong = strength[col]
    scores = []
    for r in range(kv_ref.shape[0]):
        raw = dot(query, kv_ref[r, :HDT, :]) * HDT ** (-0.5)
        per = rows // cols
        bias = jnp.concatenate([bias_ref[r * per + k].astype(f32) for k in range(per)], axis=1)
        same = mine == chain_ref[:, r * rows : (r + 1) * rows]
        scores.append(raw + bias + jnp.where(same, strong, 0.0))
    top = scores[0]
    for part in scores[1:]:
        top = jnp.maximum(top, part)
    top = jnp.max(top, axis=-1, keepdims=True)
    exps = [jnp.exp(part - top) for part in scores]
    total = exps[0]
    for part in exps[1:]:
        total = total + part
    total = jnp.sum(total, axis=-1, keepdims=True)
    out = jnp.zeros((rows, HDT), f32)
    for r in range(kv_ref.shape[0]):
        out = out + dot_nt(exps[r].astype(bf16), kv_ref[r, HDT:, :])
    gated = out / total * state_ref[:, KW : KW + HDT]
    wide = jnp.concatenate([gated, jnp.zeros((rows, KW - HDT), f32)], axis=1)
    gated = wide.T[:HDT].astype(bf16)
    for k in range(out_ref.shape[0]):
        out_ref[k] = gated


def token_attention(place, state, kv, bias, chain, strength):
    rows = state.shape[0]
    out_shape = jax.ShapeDtypeStruct((bias.shape[0], HDT, rows), bf16)
    return pl.pallas_call(
        tokens_body,
        grid=(1,),
        in_specs=[SMEM] * 2 + [full(chain)] + [HBM] * 3,
        out_specs=full(out_shape),
        out_shape=out_shape,
        scratch_shapes=held((state, kv, bias)),
        compiler_params=pltpu.CompilerParams(vmem_limit_bytes=GRANT),
        cost_estimate=pl.CostEstimate(flops=10**9, bytes_accessed=2**22, transcendentals=2**19),
        name="tokens",
    )(place, strength, chain, state, kv, bias)


def update_body(
    place,
    tokens_ref,
    gated_hbm,
    exit_hbm,
    tmid_hbm,
    back_hbm,
    mid_hbm,
    tout_ref,
    aout_ref,
    gated_ref,
    exit_ref,
    tmid_ref,
    back_ref,
    mid_ref,
    sems,
):
    col = place[1]
    atoms, rows = aout_ref.shape[0], tmid_ref.shape[0]
    at = pl.multiple_of(col * atoms, atoms)
    copies = fetch(
        (gated_hbm, exit_hbm, tmid_hbm, back_hbm, mid_hbm.at[pl.ds(at, atoms)]),
        (gated_ref, exit_ref, tmid_ref, back_ref, mid_ref),
        sems,
    )
    for copy in copies:
        copy.wait()
    added = dot_tn(gated_ref[...], exit_ref[...])
    update = (tmid_ref[...].astype(f32) + added).astype(bf16)
    tout_ref[...] = update
    sent = dot(update, back_ref[...]).astype(bf16)
    own = tokens_ref[...]
    onehot = (lax.broadcasted_iota(jnp.int32, (rows, atoms), 0) == own).astype(f32).astype(bf16)
    aout_ref[...] = (mid_ref[...].astype(f32) + dot_tn(onehot, sent)).astype(bf16)


def updates(place, gated, exit_w, tmid, back, mid, tokens, atoms):
    rows = tmid.shape[0]
    out_shape = [
        jax.ShapeDtypeStruct((rows, CS), bf16),
        jax.ShapeDtypeStruct((atoms, CA), bf16),
    ]
    return pl.pallas_call(
        update_body,
        grid=(1,),
        in_specs=[SMEM, full(tokens)] + [HBM] * 5,
        out_specs=[full(shape) for shape in out_shape],
        out_shape=out_shape,
        scratch_shapes=held((gated, exit_w, tmid, back, jax.ShapeDtypeStruct((atoms, CA), bf16))),
        compiler_params=pltpu.CompilerParams(vmem_limit_bytes=GRANT),
        name="updates",
    )(place, tokens, gated, exit_w, tmid, back, mid)


def local(
    pair_tensor,
    token_single,
    atom_single,
    atom_token,
    chain_index,
    pair_up,
    pair_down,
    bias_heads,
    atom_gain,
    atom_proj,
    atom_exit,
    atom_pool,
    token_gain,
    token_proj,
    token_exit,
    chain_bias,
    token_back,
):
    rows, cols = pair_tensor.shape[:2]
    atom_rows = atom_single.shape[0]
    row_count = lax.axis_size("row")
    col_count = lax.axis_size("col")
    row = lax.axis_index("row")
    col = lax.axis_index("col")
    chips = col_count // 2
    row_atoms = atom_rows * col_count

    both = ("row", "col")
    at = lambda r, k, core: r * col_count + 2 * k + core
    last = col_count - 1

    last = col_count - 1
    halo = lax.ppermute(
        jnp.where(col == last, atom_single[-HALO:], atom_single[:HALO]),
        both,
        [(r * col_count + last, at(r + 1, r + 1, 0)) for r in range(row_count - 1)]
        + [((r + 1) * col_count, at(r, r, 1)) for r in range(row_count - 1)],
    )
    ext_tokens = lax.dynamic_slice_in_dim(
        jnp.pad(atom_token, (HALO, HALO)), row * row_atoms, row_atoms + 2 * HALO
    )
    ext_tokens = (ext_tokens - row * rows)[None, :]
    own_tokens = lax.dynamic_slice_in_dim(
        atom_token, row * row_atoms + col * atom_rows, atom_rows
    )
    own_tokens = (own_tokens - row * rows)[None, :]

    flip = ((col == 2 * row + 1) | (col == 2 * row + 2)).astype(jnp.int32)
    place = jnp.stack([row, col, jnp.int32(row_count), flip]).astype(jnp.int32)
    center = jnp.asarray((np.eye(CZ) - 1.0 / CZ).astype(bf16))
    weights = (pair_up, pair_down, bias_heads.T, center)
    token_bias, band, edge = pair_rows(place, pair_tensor, weights, (), 0, PART, 2, True)
    halo, band, edge, token_bias, own_atoms = lax.optimization_barrier(
        (halo, band, edge, token_bias, atom_single)
    )

    here = col // 2 == row
    even = col % 2 == 0
    ring = chips // 2
    flat = lambda k, step: k // ring * ring + (k + step) % ring
    across = lambda k: (k + ring) % chips
    band = jnp.where(even, band[:, :REACH], band[:, 2 * PART - REACH :])
    band = jnp.concatenate([band, halo.reshape(HA, HALO // HA, CA)], axis=1)
    band = jnp.where(here, band, jnp.zeros_like(band))
    band_y = lax.ppermute(
        band,
        both,
        [(at(r, r, core), at(r, across(r), core)) for r in range(row_count) for core in range(2)],
    )
    edges = [
        lax.ppermute(
            edge,
            both,
            [(at(r, r - 1, 1), at(r, to(r), 0)) for r in range(1, row_count)]
            + [(at(r, r + 1, 0), at(r, to(r), 1)) for r in range(row_count - 1)],
        )
        for to in (lambda r: r, across)
    ]
    cores = [[at(0, k, core) for k in range(chips)] for core in range(2)]
    own_atoms = jnp.broadcast_to(own_atoms[None], (chips,) + own_atoms.shape)
    shards = lax.all_to_all(own_atoms, "col", 0, 0, axis_index_groups=cores)
    swap = [(i, i ^ 1) for i in range(col_count)]
    band_y, edges = lax.optimization_barrier((band_y, edges))
    edge = edges[0] + edges[1]
    blank = jnp.zeros((HA, band.shape[1] - HALO, cols), bf16)
    split = REACH - HALO
    edge = jnp.where(
        even,
        jnp.concatenate([blank[:, :split], edge, blank[:, split:]], axis=1),
        jnp.concatenate([edge, blank], axis=1),
    )
    place_in = lax.broadcasted_iota(jnp.int32, band.shape, 1)
    lane = lax.broadcasted_iota(jnp.int32, band.shape, 2)
    spare = jnp.where(
        even,
        (place_in >= split) & (place_in < REACH) & (lane < HALO),
        (place_in < HALO) & (lane >= HALO),
    )
    band = jnp.where(spare, edge, band + band_y)
    band, token_bias = lax.optimization_barrier((band, token_bias))
    sent = [
        lax.ppermute(
            band,
            both,
            [
                (at(r, k, core), at(r, flat(k, step), core))
                for r in range(row_count)
                for k in (r, across(r))
                for core in range(2)
            ],
        )
        for step in range(1, ring)
    ]
    (token_bias,) = pair_rows(
        place, pair_tensor, weights, (token_bias,), 2 * PART, rows - 2 * PART, 1, False
    )
    theirs = lax.ppermute(shards, "col", swap)
    parts = project_atoms(place, shards, theirs, atom_gain[None], atom_proj)
    gain = token_gain[None]
    parts, token_bias = lax.optimization_barrier((parts, token_bias))
    head_bias = lax.all_to_all(token_bias, "col", 0, 0)
    sent, parts, gain, ext_tokens = lax.optimization_barrier((sent, parts, gain, ext_tokens))
    band = band + sent[0] + sent[1] + sent[2]
    other = lax.ppermute(band, "col", swap)

    atom_mid, token_mid, state, keyvals = atom_attention(
        place,
        (band, other),
        parts,
        ext_tokens,
        atom_gain[None],
        atom_proj,
        atom_exit,
        atom_pool,
        token_single,
        gain,
        token_proj,
        row_count,
    )
    keyvals, head_bias = lax.optimization_barrier((keyvals, head_bias))
    keyvals = lax.all_to_all(keyvals, "row", 0, 0)
    gated = token_attention(place, state, keyvals, head_bias, chain_index[None], chain_bias)
    gated = lax.all_to_all(gated, "col", 0, 0).reshape(CS, rows)
    return tuple(
        updates(
            place, gated, token_exit, token_mid, token_back, atom_mid, own_tokens, atom_rows
        )
    )


def solution(mesh):
    placed = (
        P("row", "col", None),
        P("row", None),
        P(("row", "col"), None),
    ) + (P(),) * 14
    return jax.shard_map(
        local,
        mesh=mesh,
        in_specs=placed,
        out_specs=(P("row", None), P(("row", "col"), None)),
        check_vma=False,
    )
```

```python
import functools

import jax
import jax.numpy as jnp
import numpy as np
from jax import lax
from jax.experimental import pallas as pl
from jax.experimental.pallas import tpu as pltpu
from jax.sharding import PartitionSpec as P

CZ = 128
CS = 768
CA = 128
HT = 16
HA = 4
PH = 256
QB = 32
KW = 128
HDA = 32
HDT = 48
HB = 20
HALO = 64
PART = 112
REACH = 208
GROUP = 1024
EPS = 1e-05
GRANT = 60 * 2**20

bf16 = jnp.bfloat16
f32 = jnp.float32


def dot(left, right):
    return jnp.dot(left, right, preferred_element_type=f32)


def dot_nt(left, right):
    return lax.dot_general(left, right, (((1,), (1,)), ((), ())), preferred_element_type=f32)


def dot_tn(left, right):
    return lax.dot_general(left, right, (((0,), (0,)), ((), ())), preferred_element_type=f32)


def centered(features):
    return features - jnp.mean(features, axis=-1, keepdims=True)


def scaled(center):
    spread = jnp.mean(center * center, axis=-1, keepdims=True)
    return center * lax.rsqrt(spread + EPS)


def sigmoid(value):
    return 0.5 + 0.5 * jnp.tanh(0.5 * value)


SMEM = pl.BlockSpec(memory_space=pltpu.SMEM)
ANY = pl.BlockSpec(memory_space=pl.ANY)
HBM = pl.BlockSpec(memory_space=pltpu.HBM)
VMEM = pl.BlockSpec(memory_space=pltpu.VMEM)


def full(array):
    return pl.BlockSpec(array.shape, lambda *_: (0,) * len(array.shape))


def held(arrays):
    return [pltpu.VMEM(a.shape, a.dtype) for a in arrays] + [
        pltpu.SemaphoreType.DMA((len(arrays),))
    ]


def fetch(sources, targets, sems):
    copies = [
        pltpu.make_async_copy(source, target, sems.at[i])
        for i, (source, target) in enumerate(zip(sources, targets))
    ]
    for copy in copies:
        copy.start()
    return copies


def pair_body(place, pair_ref, up_ref, down_ref, heads_ref, center_ref, *refs, bands):
    padded = refs[-1]
    outs = refs[-4:-1] if bands else refs[-2:-1]
    pair_part = pair_ref[...].reshape(-1, CZ)
    normed = scaled(dot(pair_part, center_ref[...])).astype(bf16)
    gate = dot(normed, up_ref[:, :PH] * bf16(0.5))
    value = dot(normed, up_ref[:, PH:])
    hidden = ((gate + gate * jnp.tanh(gate)) * value).astype(bf16)
    updated = pair_part.astype(f32) + dot(hidden, down_ref[...])
    normed_two = scaled(centered(updated)).astype(bf16)
    padded[...] = jnp.zeros_like(padded)
    padded[:HB, :] = heads_ref[...].astype(f32)
    biases = dot_nt(padded[...].astype(bf16), normed_two)
    rows = pair_ref.shape[0]
    stacked = jnp.stack([biases[:, i * CZ : (i + 1) * CZ] for i in range(rows)], axis=0)
    stacked = jnp.swapaxes(stacked, 0, 1)
    outs[0][...] = stacked[HA:HB].astype(bf16)
    if bands:
        outs[1][...] = stacked[:HA].astype(bf16)

        @pl.when(pl.program_id(0) == 0)
        def _():
            flip = place[3] == 1
            edge = jnp.where(flip, stacked[:HA, rows - HALO :], stacked[:HA, :HALO])
            edge = edge.reshape(HA * HALO, CZ)
            turned = pltpu.roll(edge, HALO, 1)
            half = HA * HALO // 2
            low = jnp.where(flip, edge[:half], turned[:half])
            high = jnp.where(flip, turned[half:], edge[half:])
            lane = lax.broadcasted_iota(jnp.int32, (half, CZ), 1)
            outs[2][...] = jnp.where(lane < HALO, low, high).astype(bf16)


def pair_rows(place, pair, weights, before, first, size, count, bands):
    rows, cols = pair.shape[:2]

    def start(i, place):
        at = first + i * size
        return pl.multiple_of(at + place[3] * (rows - 2 * at - size), 16)

    in_specs = [
        pl.BlockSpec(
            (pl.Element(size), pl.Element(cols), pl.Element(CZ)),
            lambda i, place: (start(i, place), 0, 0),
        )
    ]
    in_specs += [full(array) for array in weights]
    out_shape = [jax.ShapeDtypeStruct((HT, rows, cols), bf16)]
    out_specs = [
        pl.BlockSpec(
            (pl.Element(HT), pl.Element(size), pl.Element(cols)),
            lambda i, place: (0, start(i, place), 0),
        )
    ]
    if bands:
        out_shape.append(jax.ShapeDtypeStruct((HA, size * count, cols), bf16))
        out_specs.append(
            pl.BlockSpec(
                (HA, size, cols),
                lambda i, place: (0, i + place[3] * (count - 1 - 2 * i), 0),
            )
        )
        out_shape.append(jax.ShapeDtypeStruct((HA * HALO // 2, cols), bf16))
        out_specs.append(full(out_shape[-1]))
    aliases = {}
    if before:
        aliases = {2 + len(weights): 0}
        in_specs += [ANY]
    cells = size * count * cols
    return pl.pallas_call(
        functools.partial(pair_body, bands=bands),
        grid_spec=pltpu.PrefetchScalarGridSpec(
            num_scalar_prefetch=1,
            grid=(count,),
            in_specs=in_specs,
            out_specs=out_specs,
            scratch_shapes=[pltpu.VMEM((32, CZ), f32)],
        ),
        out_shape=out_shape,
        input_output_aliases=aliases,
        compiler_params=pltpu.CompilerParams(vmem_limit_bytes=56 * 2**20),
        cost_estimate=pl.CostEstimate(
            flops=cells * 500000, bytes_accessed=cells * 300, transcendentals=cells * PH
        ),
        name="pair",
    )(place, pair, *weights, *before)


def atoms_body(
    place,
    tokens_ref,
    atom_gain_ref,
    proj_ref,
    exit_ref,
    pool_ref,
    single_ref,
    gain_ref,
    half_ref,
    other_ref,
    mine_hbm,
    theirs_hbm,
    tproj_hbm,
    mid_hbm,
    tmid_hbm,
    state_hbm,
    tkv_hbm,
    bias_ref,
    look_ref,
    sums_ref,
    value_ref,
    ext_ref,
    query_ref,
    gate_ref,
    mine_ref,
    theirs_ref,
    tproj_ref,
    sems,
    mid_ref,
    tmid_ref,
    state_ref,
    tkv_ref,
    out_sems,
):
    copies = fetch(
        (mine_hbm, theirs_hbm, tproj_hbm), (mine_ref, theirs_ref, tproj_ref), sems
    )
    row, col, row_count = place[0], place[1], place[2]
    total = look_ref.shape[0]
    atoms = query_ref.shape[0]
    rows = single_ref.shape[0]
    chips = mine_ref.shape[0]
    per = atoms // (2 * chips)
    even = lax.rem(col, 2) == 0
    copies[0].wait()
    copies[1].wait()
    rest = jnp.zeros((rows - REACH, KW), bf16)
    middle = jnp.zeros((rows - 2 * HALO, KW), bf16)
    left = jnp.maximum(row - 1, 0)
    right = jnp.minimum(row + 1, chips - 1)
    left = jnp.where(even, theirs_ref[left, per:], mine_ref[left, per:])
    right = jnp.where(even, mine_ref[right, per:], theirs_ref[right, per:])
    left_turned = pltpu.roll(left.astype(f32), HALO, 1).astype(bf16)
    right_turned = pltpu.roll(right.astype(f32), HALO, 1).astype(bf16)
    before, after = [], []
    for h in range(HA):
        mine, theirs = half_ref[h], other_ref[h]
        mine, theirs = jnp.where(even, mine, theirs), jnp.where(even, theirs, mine)
        before.append(mine[REACH:])
        after.append(theirs[REACH:])
        base = h * 3 * KW
        part = slice(h % 2 * HALO, (h % 2 + 1) * HALO)
        edges = (left, right_turned) if h < HA // 2 else (left_turned, right)
        bias_ref[:, base : base + KW] = jnp.concatenate([mine[:REACH], rest], axis=0)
        bias_ref[:, base + KW : base + 2 * KW] = jnp.concatenate([rest, theirs[:REACH]], axis=0)
        bias_ref[:, base + 2 * KW : base + 3 * KW] = jnp.concatenate(
            [edges[0][part], middle, edges[1][part]], axis=0
        )
    ext_ref[:HALO] = jnp.concatenate(before, axis=0)
    ext_ref[HALO + atoms :] = jnp.concatenate(after, axis=0)
    for k in range(chips):
        mine, theirs = mine_ref[k, :per], theirs_ref[k, :per]
        at = HALO + 2 * k * per
        ext_ref[at : at + per] = jnp.where(even, mine, theirs)
        ext_ref[at + per : at + 2 * per] = jnp.where(even, theirs, mine)
    normed = (scaled(centered(ext_ref[...].astype(f32))) * atom_gain_ref[...]).astype(bf16)
    own = normed[HALO : HALO + atoms]
    query_ref[...] = (dot(own, proj_ref[:, :CA]) * HDA ** (-0.5)).astype(bf16)
    look_ref[:, :CA] = dot(normed, proj_ref[:, CA : 2 * CA]).astype(bf16)
    value_ref[...] = dot(normed, proj_ref[:, 2 * CA : 3 * CA]).astype(bf16)
    gate_ref[...] = sigmoid(dot(own, proj_ref[:, 3 * CA :]))
    lane = lax.broadcasted_iota(jnp.int32, (KW, 3 * KW), 1)
    for t in range(total // KW):
        at = slice(t * KW, (t + 1) * KW)
        tokens = jnp.broadcast_to(tokens_ref[:, at], (KW, KW)).astype(f32).T.astype(jnp.int32)
        tokens = jnp.concatenate([tokens] * 3, axis=1)
        tokens = jnp.where(
            tokens < 0,
            tokens + 2 * KW + HALO,
            jnp.where(tokens < 2 * KW, tokens, tokens + HALO),
        )
        look_ref[at, CA:] = (tokens == lane).astype(f32).astype(bf16)
    head_of = lax.broadcasted_iota(jnp.int32, (QB, CA), 1) // HDA
    sums_ref[...] = jnp.zeros_like(sums_ref)
    row_lane = lax.broadcasted_iota(jnp.int32, (1, KW), 1)

    def group(g, counts):
        start = pl.multiple_of(g * GROUP, GROUP)
        own = pl.ds(start, GROUP)
        onehot = look_ref[pl.ds(pl.multiple_of(start + HALO, HALO), GROUP), CA : CA + 2 * KW]
        picked = dot(onehot, bias_ref[...]).astype(bf16)
        queries = query_ref[own, :]
        scores = []
        for b in range(GROUP // QB):
            part = slice(b * QB, (b + 1) * QB)
            left = jnp.concatenate(
                [
                    jnp.concatenate(
                        [
                            jnp.where(head_of == h, queries[part].astype(f32), 0.0).astype(bf16),
                            picked[part, h * 3 * KW : (h + 1) * 3 * KW],
                        ],
                        axis=1,
                    )
                    for h in range(HA)
                ],
                axis=0,
            )
            first = start + b * QB + HALO - (KW - QB) // 2
            window = look_ref[pl.ds(pl.multiple_of(first, 16), KW), :]
            at = row_lane + first
            inside = ((at >= HALO) | (row > 0)) & ((at < total - HALO) | (row < row_count - 1))
            scores.append(dot_nt(left, window) + jnp.where(inside, 0.0, -1e30))
        scores = jnp.concatenate(scores, axis=0)
        exps = jnp.exp(scores - jnp.max(scores, axis=-1, keepdims=True))
        inverse = 1.0 / jnp.sum(exps, axis=-1, keepdims=True)
        weights = exps.astype(bf16)
        attended = []
        for b in range(GROUP // QB):
            first = start + b * QB + HALO - (KW - QB) // 2
            part = slice(b * HA * QB, (b + 1) * HA * QB)
            out = dot(weights[part], value_ref[pl.ds(pl.multiple_of(first, 16), KW), :])
            out = out * inverse[part]
            merged = out[:QB]
            for h in range(1, HA):
                merged = jnp.where(head_of == h, out[h * QB : (h + 1) * QB], merged)
            attended.append(merged)
        attended = jnp.concatenate(attended, axis=0)
        gated = (attended * gate_ref[own, :]).astype(bf16)
        single = ext_ref[pl.ds(pl.multiple_of(start + HALO, HALO), GROUP), :].astype(f32)
        mid = (single + dot(gated, exit_ref[...])).astype(bf16)
        mid_ref[own, :] = mid
        pooled = jnp.maximum(dot(mid, pool_ref[...]), 0.0).astype(bf16)
        sums_ref[...] += dot_tn(onehot, pooled)
        return counts + jnp.sum(onehot.astype(f32).T, axis=1, keepdims=True)

    counts = lax.fori_loop(0, atoms // GROUP, group, jnp.zeros((rows, 1), f32))
    token_mid = (single_ref[...].astype(f32) + sums_ref[...] / counts).astype(bf16)
    tmid_ref[...] = token_mid
    stores = fetch((mid_ref, tmid_ref), (mid_hbm, tmid_hbm), out_sems)
    normed = (scaled(centered(token_mid.astype(f32))) * gain_ref[...]).astype(bf16)

    copies[-1].wait()

    def head_part(part):
        start = part * CS + col * HDT
        base = jnp.minimum(start // KW * KW, 4 * CS - 2 * KW)
        base = pl.multiple_of(base, KW)
        wide = dot(normed, tproj_ref[:, pl.ds(base, 2 * KW)])
        return pltpu.roll(wide, lax.rem(2 * KW - (start - base), 2 * KW), 1)[:, :KW]

    state_ref[...] = jnp.concatenate([head_part(0), sigmoid(head_part(1))], axis=1)
    keyvals = jnp.concatenate([head_part(2).T[:HDT], head_part(3).T[:HDT]], axis=0)
    tkv_ref[...] = keyvals.astype(bf16)
    last = [(state_ref, state_hbm)] + [(tkv_ref, tkv_hbm.at[k]) for k in range(tkv_hbm.shape[0])]
    for i, (source, target) in enumerate(last):
        stores.append(pltpu.make_async_copy(source, target, out_sems.at[2 + i]))
        stores[-1].start()
    for copy in stores:
        copy.wait()


def atom_attention(
    place, bands, shards, tokens, atom_gain, proj, exit_w, pool, single, gain, tproj, copies
):
    total = tokens.shape[1]
    atoms = total - 2 * HALO
    rows = single.shape[0]
    operands = (tokens, atom_gain, proj, exit_w, pool, single, gain)
    fetched = (*shards, tproj)
    out_shape = [
        jax.ShapeDtypeStruct((atoms, CA), bf16),
        jax.ShapeDtypeStruct((rows, CS), bf16),
        jax.ShapeDtypeStruct((rows, 2 * KW), f32),
        jax.ShapeDtypeStruct((copies, 2 * HDT, rows), bf16),
    ]
    return pl.pallas_call(
        atoms_body,
        grid=(1,),
        in_specs=[SMEM]
        + [full(array) for array in operands]
        + [VMEM] * len(bands)
        + [HBM] * len(fetched),
        out_specs=[HBM] * len(out_shape),
        out_shape=out_shape,
        scratch_shapes=[
            pltpu.VMEM((rows, HA * 3 * KW), bf16),
            pltpu.VMEM((total, CA + 3 * KW), bf16),
            pltpu.VMEM((rows, CS), f32),
            pltpu.VMEM((total, CA), bf16),
            pltpu.VMEM((total, CA), bf16),
            pltpu.VMEM((atoms, CA), bf16),
            pltpu.VMEM((atoms, CA), f32),
        ]
        + held(fetched)
        + [pltpu.VMEM(a.shape, a.dtype) for a in out_shape[:3]]
        + [pltpu.VMEM((2 * HDT, rows), bf16), pltpu.SemaphoreType.DMA((3 + copies,))],
        compiler_params=pltpu.CompilerParams(vmem_limit_bytes=GRANT),
        cost_estimate=pl.CostEstimate(
            flops=10**7, bytes_accessed=2**14, transcendentals=2**10
        ),
        name="atoms",
    )(place, *operands, *bands, *fetched)


def tokens_body(
    place, strength, chain_ref, state_hbm, kv_hbm, bias_hbm, out_ref, state_ref, kv_ref, bias_ref, sems
):
    per = state_hbm.shape[0] // bias_hbm.shape[2]
    groups = kv_hbm.shape[0]
    bias_parts = [pl.ds(r * per, per) for r in range(groups)]
    copies = fetch(
        [state_hbm, kv_hbm] + [bias_hbm.at[part] for part in bias_parts],
        [state_ref, kv_ref] + [bias_ref.at[part] for part in bias_parts],
        sems,
    )
    col = place[1]
    rows = state_ref.shape[0]
    own = pl.multiple_of(place[0] * rows, rows)
    mine = chain_ref[:, pl.ds(own, rows)].astype(f32)
    mine = jnp.broadcast_to(mine, (KW, rows)).T
    mine = jnp.concatenate([mine] * (rows // KW), axis=1).astype(jnp.int32)
    copies[0].wait()
    copies[1].wait()
    query = state_ref[:, :HDT].astype(bf16)
    strong = strength[col]
    raws = [dot(query, kv_ref[r, :HDT, :]) * HDT ** (-0.5) for r in range(groups)]
    scores = []
    for r, raw in enumerate(raws):
        copies[2 + r].wait()
        bias = jnp.concatenate([bias_ref[r * per + k].astype(f32) for k in range(per)], axis=1)
        same = mine == chain_ref[:, r * rows : (r + 1) * rows]
        scores.append(raw + bias + jnp.where(same, strong, 0.0))
    top = scores[0]
    for part in scores[1:]:
        top = jnp.maximum(top, part)
    top = jnp.max(top, axis=-1, keepdims=True)
    exps = [jnp.exp(part - top) for part in scores]
    total = exps[0]
    for part in exps[1:]:
        total = total + part
    total = jnp.sum(total, axis=-1, keepdims=True)
    out = jnp.zeros((rows, HDT), f32)
    for r in range(kv_ref.shape[0]):
        out = out + dot_nt(exps[r].astype(bf16), kv_ref[r, HDT:, :])
    gated = out / total * state_ref[:, KW : KW + HDT]
    wide = jnp.concatenate([gated, jnp.zeros((rows, KW - HDT), f32)], axis=1)
    gated = wide.T[:HDT].astype(bf16)
    for k in range(out_ref.shape[0]):
        out_ref[k] = gated


def token_attention(place, state, kv, bias, chain, strength):
    rows = state.shape[0]
    out_shape = jax.ShapeDtypeStruct((bias.shape[0], HDT, rows), bf16)
    return pl.pallas_call(
        tokens_body,
        grid=(1,),
        in_specs=[SMEM] * 2 + [full(chain)] + [HBM] * 3,
        out_specs=full(out_shape),
        out_shape=out_shape,
        scratch_shapes=held((state, kv, bias))[:-1]
        + [pltpu.SemaphoreType.DMA((2 + kv.shape[0],))],
        compiler_params=pltpu.CompilerParams(vmem_limit_bytes=GRANT),
        cost_estimate=pl.CostEstimate(flops=10**9, bytes_accessed=2**22, transcendentals=2**19),
        name="tokens",
    )(place, strength, chain, state, kv, bias)


def update_body(
    place, tokens_ref, gated_ref, exit_ref, tmid_ref, back_ref, mid_ref, tout_ref, aout_ref
):
    col = place[1]
    atoms, rows = aout_ref.shape[0], tmid_ref.shape[0]
    at = pl.multiple_of(col * atoms, atoms)
    added = dot_tn(gated_ref[...], exit_ref[...])
    update = (tmid_ref[...].astype(f32) + added).astype(bf16)
    tout_ref[...] = update
    sent = dot(update, back_ref[...]).astype(bf16)
    own = tokens_ref[...]
    onehot = (lax.broadcasted_iota(jnp.int32, (rows, atoms), 0) == own).astype(f32).astype(bf16)
    aout_ref[...] = (mid_ref[pl.ds(at, atoms), :].astype(f32) + dot_tn(onehot, sent)).astype(bf16)


def updates(place, gated, exit_w, tmid, back, mid, tokens, atoms):
    rows = tmid.shape[0]
    out_shape = [
        jax.ShapeDtypeStruct((rows, CS), bf16),
        jax.ShapeDtypeStruct((atoms, CA), bf16),
    ]
    return pl.pallas_call(
        update_body,
        grid=(1,),
        in_specs=[SMEM] + [VMEM] * 6,
        out_specs=[full(shape) for shape in out_shape],
        out_shape=out_shape,
        compiler_params=pltpu.CompilerParams(vmem_limit_bytes=16 * 2**20),
        name="updates",
    )(place, tokens, gated, exit_w, tmid, back, mid)


def local(
    pair_tensor,
    token_single,
    atom_single,
    atom_token,
    chain_index,
    pair_up,
    pair_down,
    bias_heads,
    atom_gain,
    atom_proj,
    atom_exit,
    atom_pool,
    token_gain,
    token_proj,
    token_exit,
    chain_bias,
    token_back,
):
    rows, cols = pair_tensor.shape[:2]
    atom_rows = atom_single.shape[0]
    row_count = lax.axis_size("row")
    col_count = lax.axis_size("col")
    row = lax.axis_index("row")
    col = lax.axis_index("col")
    chips = col_count // 2
    row_atoms = atom_rows * col_count

    both = ("row", "col")
    at = lambda r, k, core: r * col_count + 2 * k + core
    last = col_count - 1

    last = col_count - 1
    halo = lax.ppermute(
        jnp.where(col == last, atom_single[-HALO:], atom_single[:HALO]),
        both,
        [(r * col_count + last, at(r + 1, r + 1, 0)) for r in range(row_count - 1)]
        + [((r + 1) * col_count, at(r, r, 1)) for r in range(row_count - 1)],
    )
    ext_tokens = lax.dynamic_slice_in_dim(
        jnp.pad(atom_token, (HALO, HALO)), row * row_atoms, row_atoms + 2 * HALO
    )
    ext_tokens = (ext_tokens - row * rows)[None, :]
    own_tokens = lax.dynamic_slice_in_dim(
        atom_token, row * row_atoms + col * atom_rows, atom_rows
    )
    own_tokens = (own_tokens - row * rows)[None, :]

    flip = ((col == 2 * row + 1) | (col == 2 * row + 2)).astype(jnp.int32)
    place = jnp.stack([row, col, jnp.int32(row_count), flip]).astype(jnp.int32)
    center = jnp.asarray((np.eye(CZ) - 1.0 / CZ).astype(bf16))
    weights = (pair_up, pair_down, bias_heads.T, center)
    token_bias, band, edge = pair_rows(place, pair_tensor, weights, (), 0, PART, 2, True)
    halo, band, edge, token_bias, own_atoms = lax.optimization_barrier(
        (halo, band, edge, token_bias, atom_single)
    )

    here = col // 2 == row
    even = col % 2 == 0
    ring = chips // 2
    flat = lambda k, step: k // ring * ring + (k + step) % ring
    across = lambda k: (k + ring) % chips
    band = jnp.where(even, band[:, :REACH], band[:, 2 * PART - REACH :])
    band = jnp.concatenate([band, halo.reshape(HA, HALO // HA, CA)], axis=1)
    band = jnp.where(here, band, jnp.zeros_like(band))
    band_y = lax.ppermute(
        band,
        both,
        [(at(r, r, core), at(r, across(r), core)) for r in range(row_count) for core in range(2)],
    )
    cores = [[at(0, k, core) for k in range(chips)] for core in range(2)]
    own_part = jnp.concatenate([own_atoms, edge], axis=0)
    own_part = jnp.broadcast_to(own_part[None], (chips,) + own_part.shape)
    shards = lax.all_to_all(own_part, "col", 0, 0, axis_index_groups=cores)
    swap = [(i, i ^ 1) for i in range(col_count)]
    band = band + band_y
    band, token_bias = lax.optimization_barrier((band, token_bias))
    sent = [
        lax.ppermute(
            band,
            both,
            [
                (at(r, k, core), at(r, flat(k, step), core))
                for r in range(row_count)
                for k in (r, across(r))
                for core in range(2)
            ],
        )
        for step in range(1, ring)
    ]
    (token_bias,) = pair_rows(
        place, pair_tensor, weights, (token_bias,), 2 * PART, rows - 2 * PART, 1, False
    )
    theirs = lax.ppermute(shards, "col", swap)
    gain = token_gain[None]
    head_bias = lax.all_to_all(token_bias, "col", 0, 0)
    sent, theirs, gain, ext_tokens = lax.optimization_barrier((sent, theirs, gain, ext_tokens))
    band = band + sent[0] + sent[1] + sent[2]
    other = lax.ppermute(band, "col", swap)

    atom_mid, token_mid, state, keyvals = atom_attention(
        place,
        (band, other),
        (shards, theirs),
        ext_tokens,
        atom_gain[None],
        atom_proj,
        atom_exit,
        atom_pool,
        token_single,
        gain,
        token_proj,
        row_count,
    )
    keyvals, head_bias = lax.optimization_barrier((keyvals, head_bias))
    keyvals = lax.all_to_all(keyvals, "row", 0, 0)
    gated = token_attention(place, state, keyvals, head_bias, chain_index[None], chain_bias)
    gated = lax.all_to_all(gated, "col", 0, 0).reshape(CS, rows)
    return tuple(
        updates(
            place, gated, token_exit, token_mid, token_back, atom_mid, own_tokens, atom_rows
        )
    )


def solution(mesh):
    placed = (
        P("row", "col", None),
        P("row", None),
        P(("row", "col"), None),
    ) + (P(),) * 14
    return jax.shard_map(
        local,
        mesh=mesh,
        in_specs=placed,
        out_specs=(P("row", None), P(("row", "col"), None)),
        check_vma=False,
    )
```

```python
import functools

import jax
import jax.numpy as jnp
import numpy as np
from jax import lax
from jax.experimental import pallas as pl
from jax.experimental.pallas import tpu as pltpu
from jax.sharding import PartitionSpec as P

CZ = 128
CS = 768
CA = 128
HT = 16
HA = 4
PH = 256
QB = 32
KW = 128
HDA = 32
HDT = 48
HB = 20
HALO = 64
PART = 112
REACH = 208
GROUP = 1024
EPS = 1e-05
GRANT = 60 * 2**20

bf16 = jnp.bfloat16
f32 = jnp.float32


def dot(left, right):
    return jnp.dot(left, right, preferred_element_type=f32)


def dot_nt(left, right):
    return lax.dot_general(left, right, (((1,), (1,)), ((), ())), preferred_element_type=f32)


def dot_tn(left, right):
    return lax.dot_general(left, right, (((0,), (0,)), ((), ())), preferred_element_type=f32)


def centered(features):
    return features - jnp.mean(features, axis=-1, keepdims=True)


def scaled(center):
    spread = jnp.mean(center * center, axis=-1, keepdims=True)
    return center * lax.rsqrt(spread + EPS)


def sigmoid(value):
    return 0.5 + 0.5 * jnp.tanh(0.5 * value)


SMEM = pl.BlockSpec(memory_space=pltpu.SMEM)
ANY = pl.BlockSpec(memory_space=pl.ANY)
HBM = pl.BlockSpec(memory_space=pltpu.HBM)
VMEM = pl.BlockSpec(memory_space=pltpu.VMEM)


def full(array):
    return pl.BlockSpec(array.shape, lambda *_: (0,) * len(array.shape))


def held(arrays):
    return [pltpu.VMEM(a.shape, a.dtype) for a in arrays] + [
        pltpu.SemaphoreType.DMA((len(arrays),))
    ]


def fetch(sources, targets, sems):
    copies = [
        pltpu.make_async_copy(source, target, sems.at[i])
        for i, (source, target) in enumerate(zip(sources, targets))
    ]
    for copy in copies:
        copy.start()
    return copies


def pair_body(place, pair_ref, up_ref, down_ref, heads_ref, center_ref, *refs, bands):
    padded = refs[-1]
    outs = refs[-4:-1] if bands else refs[-2:-1]
    pair_part = pair_ref[...].reshape(-1, CZ)
    normed = scaled(dot(pair_part, center_ref[...])).astype(bf16)
    gate = dot(normed, up_ref[:, :PH] * bf16(0.5))
    value = dot(normed, up_ref[:, PH:])
    hidden = ((gate + gate * jnp.tanh(gate)) * value).astype(bf16)
    updated = pair_part.astype(f32) + dot(hidden, down_ref[...])
    normed_two = scaled(centered(updated)).astype(bf16)
    padded[...] = jnp.zeros_like(padded)
    padded[:HB, :] = heads_ref[...].astype(f32)
    biases = dot_nt(padded[...].astype(bf16), normed_two)
    rows = pair_ref.shape[0]
    stacked = jnp.stack([biases[:, i * CZ : (i + 1) * CZ] for i in range(rows)], axis=0)
    stacked = jnp.swapaxes(stacked, 0, 1)
    outs[0][...] = stacked[HA:HB].astype(bf16)
    if bands:
        outs[1][...] = stacked[:HA].astype(bf16)

        @pl.when(pl.program_id(0) == 0)
        def _():
            flip = place[3] == 1
            edge = jnp.where(flip, stacked[:HA, rows - HALO :], stacked[:HA, :HALO])
            edge = edge.reshape(HA * HALO, CZ)
            turned = pltpu.roll(edge, HALO, 1)
            half = HA * HALO // 2
            low = jnp.where(flip, edge[:half], turned[:half])
            high = jnp.where(flip, turned[half:], edge[half:])
            lane = lax.broadcasted_iota(jnp.int32, (half, CZ), 1)
            outs[2][...] = jnp.where(lane < HALO, low, high).astype(bf16)


def pair_rows(place, pair, weights, before, first, size, count, bands):
    rows, cols = pair.shape[:2]

    def start(i, place):
        at = first + i * size
        return pl.multiple_of(at + place[3] * (rows - 2 * at - size), 16)

    in_specs = [
        pl.BlockSpec(
            (pl.Element(size), pl.Element(cols), pl.Element(CZ)),
            lambda i, place: (start(i, place), 0, 0),
        )
    ]
    in_specs += [full(array) for array in weights]
    out_shape = [jax.ShapeDtypeStruct((HT, rows, cols), bf16)]
    out_specs = [
        pl.BlockSpec(
            (pl.Element(HT), pl.Element(size), pl.Element(cols)),
            lambda i, place: (0, start(i, place), 0),
        )
    ]
    if bands:
        out_shape.append(jax.ShapeDtypeStruct((HA, size * count, cols), bf16))
        out_specs.append(
            pl.BlockSpec(
                (HA, size, cols),
                lambda i, place: (0, i + place[3] * (count - 1 - 2 * i), 0),
            )
        )
        out_shape.append(jax.ShapeDtypeStruct((HA * HALO // 2, cols), bf16))
        out_specs.append(full(out_shape[-1]))
    aliases = {}
    if before:
        aliases = {2 + len(weights): 0}
        in_specs += [ANY]
    cells = size * count * cols
    return pl.pallas_call(
        functools.partial(pair_body, bands=bands),
        grid_spec=pltpu.PrefetchScalarGridSpec(
            num_scalar_prefetch=1,
            grid=(count,),
            in_specs=in_specs,
            out_specs=out_specs,
            scratch_shapes=[pltpu.VMEM((32, CZ), f32)],
        ),
        out_shape=out_shape,
        input_output_aliases=aliases,
        compiler_params=pltpu.CompilerParams(vmem_limit_bytes=56 * 2**20),
        cost_estimate=pl.CostEstimate(
            flops=cells * 500000, bytes_accessed=cells * 300, transcendentals=cells * PH
        ),
        name="pair",
    )(place, pair, *weights, *before)


def atoms_body(
    place,
    tokens_ref,
    atom_gain_ref,
    proj_ref,
    exit_ref,
    pool_ref,
    single_ref,
    gain_ref,
    half_ref,
    other_ref,
    mine_hbm,
    theirs_hbm,
    tproj_hbm,
    mid_hbm,
    tmid_hbm,
    state_hbm,
    tkv_hbm,
    bias_ref,
    look_ref,
    sums_ref,
    value_ref,
    ext_ref,
    query_ref,
    gate_ref,
    mine_ref,
    theirs_ref,
    tproj_ref,
    sems,
    mid_ref,
    tmid_ref,
    state_ref,
    tkv_ref,
    out_sems,
):
    copies = fetch(
        (mine_hbm, theirs_hbm, tproj_hbm), (mine_ref, theirs_ref, tproj_ref), sems
    )
    row, col, row_count = place[0], place[1], place[2]
    total = look_ref.shape[0]
    atoms = query_ref.shape[0]
    rows = single_ref.shape[0]
    chips = mine_ref.shape[0]
    per = atoms // (2 * chips)
    even = lax.rem(col, 2) == 0
    copies[0].wait()
    copies[1].wait()
    rest = jnp.zeros((rows - REACH, KW), bf16)
    middle = jnp.zeros((rows - 2 * HALO, KW), bf16)
    left = jnp.maximum(row - 1, 0)
    right = jnp.minimum(row + 1, chips - 1)
    left = jnp.where(even, theirs_ref[left, per:], mine_ref[left, per:])
    right = jnp.where(even, mine_ref[right, per:], theirs_ref[right, per:])
    left_turned = pltpu.roll(left.astype(f32), HALO, 1).astype(bf16)
    right_turned = pltpu.roll(right.astype(f32), HALO, 1).astype(bf16)
    before, after = [], []
    for h in range(HA):
        mine, theirs = half_ref[h], other_ref[h]
        mine, theirs = jnp.where(even, mine, theirs), jnp.where(even, theirs, mine)
        before.append(mine[REACH:])
        after.append(theirs[REACH:])
        base = h * 3 * KW
        part = slice(h % 2 * HALO, (h % 2 + 1) * HALO)
        edges = (left, right_turned) if h < HA // 2 else (left_turned, right)
        bias_ref[:, base : base + KW] = jnp.concatenate([mine[:REACH], rest], axis=0)
        bias_ref[:, base + KW : base + 2 * KW] = jnp.concatenate([rest, theirs[:REACH]], axis=0)
        bias_ref[:, base + 2 * KW : base + 3 * KW] = jnp.concatenate(
            [edges[0][part], middle, edges[1][part]], axis=0
        )
    ext_ref[:HALO] = jnp.concatenate(before, axis=0)
    ext_ref[HALO + atoms :] = jnp.concatenate(after, axis=0)
    for k in range(chips):
        mine, theirs = mine_ref[k, :per], theirs_ref[k, :per]
        at = HALO + 2 * k * per
        ext_ref[at : at + per] = jnp.where(even, mine, theirs)
        ext_ref[at + per : at + 2 * per] = jnp.where(even, theirs, mine)
    normed = (scaled(centered(ext_ref[...].astype(f32))) * atom_gain_ref[...]).astype(bf16)
    own = normed[HALO : HALO + atoms]
    query_ref[...] = (dot(own, proj_ref[:, :CA]) * HDA ** (-0.5)).astype(bf16)
    look_ref[:, :CA] = dot(normed, proj_ref[:, CA : 2 * CA]).astype(bf16)
    value_ref[...] = dot(normed, proj_ref[:, 2 * CA : 3 * CA]).astype(bf16)
    gate_ref[...] = sigmoid(dot(own, proj_ref[:, 3 * CA :]))
    lane = lax.broadcasted_iota(jnp.int32, (KW, 3 * KW), 1)
    for t in range(total // KW):
        at = slice(t * KW, (t + 1) * KW)
        tokens = jnp.broadcast_to(tokens_ref[:, at], (KW, KW)).astype(f32).T.astype(jnp.int32)
        tokens = jnp.concatenate([tokens] * 3, axis=1)
        tokens = jnp.where(
            tokens < 0,
            tokens + 2 * KW + HALO,
            jnp.where(tokens < 2 * KW, tokens, tokens + HALO),
        )
        look_ref[at, CA:] = (tokens == lane).astype(f32).astype(bf16)
    head_of = lax.broadcasted_iota(jnp.int32, (QB, CA), 1) // HDA
    sums_ref[...] = jnp.zeros_like(sums_ref)
    row_lane = lax.broadcasted_iota(jnp.int32, (1, KW), 1)

    def group(g, counts):
        start = pl.multiple_of(g * GROUP, GROUP)
        own = pl.ds(start, GROUP)
        onehot = look_ref[pl.ds(pl.multiple_of(start + HALO, HALO), GROUP), CA : CA + 2 * KW]
        picked = dot(onehot, bias_ref[...]).astype(bf16)
        queries = query_ref[own, :]
        scores = []
        for b in range(GROUP // QB):
            part = slice(b * QB, (b + 1) * QB)
            left = jnp.concatenate(
                [
                    jnp.concatenate(
                        [
                            jnp.where(head_of == h, queries[part].astype(f32), 0.0).astype(bf16),
                            picked[part, h * 3 * KW : (h + 1) * 3 * KW],
                        ],
                        axis=1,
                    )
                    for h in range(HA)
                ],
                axis=0,
            )
            first = start + b * QB + HALO - (KW - QB) // 2
            window = look_ref[pl.ds(pl.multiple_of(first, 16), KW), :]
            at = row_lane + first
            inside = ((at >= HALO) | (row > 0)) & ((at < total - HALO) | (row < row_count - 1))
            scores.append(dot_nt(left, window) + jnp.where(inside, 0.0, -1e30))
        scores = jnp.concatenate(scores, axis=0)
        exps = jnp.exp(scores - jnp.max(scores, axis=-1, keepdims=True))
        inverse = 1.0 / jnp.sum(exps, axis=-1, keepdims=True)
        weights = exps.astype(bf16)
        attended = []
        for b in range(GROUP // QB):
            first = start + b * QB + HALO - (KW - QB) // 2
            part = slice(b * HA * QB, (b + 1) * HA * QB)
            out = dot(weights[part], value_ref[pl.ds(pl.multiple_of(first, 16), KW), :])
            out = out * inverse[part]
            merged = out[:QB]
            for h in range(1, HA):
                merged = jnp.where(head_of == h, out[h * QB : (h + 1) * QB], merged)
            attended.append(merged)
        attended = jnp.concatenate(attended, axis=0)
        gated = (attended * gate_ref[own, :]).astype(bf16)
        single = ext_ref[pl.ds(pl.multiple_of(start + HALO, HALO), GROUP), :].astype(f32)
        mid = (single + dot(gated, exit_ref[...])).astype(bf16)
        mid_ref[own, :] = mid
        pooled = jnp.maximum(dot(mid, pool_ref[...]), 0.0).astype(bf16)
        sums_ref[...] += dot_tn(onehot, pooled)
        return counts + jnp.sum(onehot.astype(f32).T, axis=1, keepdims=True)

    counts = lax.fori_loop(0, atoms // GROUP, group, jnp.zeros((rows, 1), f32))
    token_mid = (single_ref[...].astype(f32) + sums_ref[...] / counts).astype(bf16)
    tmid_ref[...] = token_mid
    stores = fetch((mid_ref, tmid_ref), (mid_hbm, tmid_hbm), out_sems)
    normed = (scaled(centered(token_mid.astype(f32))) * gain_ref[...]).astype(bf16)

    copies[-1].wait()

    def head_part(part):
        start = part * CS + col * HDT
        base = jnp.minimum(start // KW * KW, 4 * CS - 2 * KW)
        base = pl.multiple_of(base, KW)
        wide = dot(normed, tproj_ref[:, pl.ds(base, 2 * KW)])
        return pltpu.roll(wide, lax.rem(2 * KW - (start - base), 2 * KW), 1)[:, :KW]

    state_ref[...] = jnp.concatenate([head_part(0), sigmoid(head_part(1))], axis=1)
    keyvals = jnp.concatenate([head_part(2).T[:HDT], head_part(3).T[:HDT]], axis=0)
    tkv_ref[...] = keyvals.astype(bf16)
    last = [(state_ref, state_hbm)] + [(tkv_ref, tkv_hbm.at[k]) for k in range(tkv_hbm.shape[0])]
    for i, (source, target) in enumerate(last):
        stores.append(pltpu.make_async_copy(source, target, out_sems.at[2 + i]))
        stores[-1].start()
    for copy in stores:
        copy.wait()


def atom_attention(
    place, bands, shards, tokens, atom_gain, proj, exit_w, pool, single, gain, tproj, copies
):
    total = tokens.shape[1]
    atoms = total - 2 * HALO
    rows = single.shape[0]
    operands = (tokens, atom_gain, proj, exit_w, pool, single, gain)
    fetched = (*shards, tproj)
    out_shape = [
        jax.ShapeDtypeStruct((atoms, CA), bf16),
        jax.ShapeDtypeStruct((rows, CS), bf16),
        jax.ShapeDtypeStruct((rows, 2 * KW), f32),
        jax.ShapeDtypeStruct((copies, 2 * HDT, rows), bf16),
    ]
    return pl.pallas_call(
        atoms_body,
        grid=(1,),
        in_specs=[SMEM]
        + [full(array) for array in operands]
        + [VMEM] * len(bands)
        + [HBM] * len(fetched),
        out_specs=[HBM] * len(out_shape),
        out_shape=out_shape,
        scratch_shapes=[
            pltpu.VMEM((rows, HA * 3 * KW), bf16),
            pltpu.VMEM((total, CA + 3 * KW), bf16),
            pltpu.VMEM((rows, CS), f32),
            pltpu.VMEM((total, CA), bf16),
            pltpu.VMEM((total, CA), bf16),
            pltpu.VMEM((atoms, CA), bf16),
            pltpu.VMEM((atoms, CA), f32),
        ]
        + held(fetched)
        + [pltpu.VMEM(a.shape, a.dtype) for a in out_shape[:3]]
        + [pltpu.VMEM((2 * HDT, rows), bf16), pltpu.SemaphoreType.DMA((3 + copies,))],
        compiler_params=pltpu.CompilerParams(vmem_limit_bytes=GRANT),
        cost_estimate=pl.CostEstimate(
            flops=10**10, bytes_accessed=2**24, transcendentals=2**22
        ),
        name="atoms",
    )(place, *operands, *bands, *fetched)


def tokens_body(
    place, strength, chain_ref, state_hbm, kv_hbm, bias_hbm, out_ref, state_ref, kv_ref, bias_ref, sems
):
    per = state_hbm.shape[0] // bias_hbm.shape[2]
    groups = kv_hbm.shape[0]
    bias_parts = [pl.ds(r * per, per) for r in range(groups)]
    copies = fetch(
        [state_hbm, kv_hbm] + [bias_hbm.at[part] for part in bias_parts],
        [state_ref, kv_ref] + [bias_ref.at[part] for part in bias_parts],
        sems,
    )
    col = place[1]
    rows = state_ref.shape[0]
    own = pl.multiple_of(place[0] * rows, rows)
    mine = chain_ref[:, pl.ds(own, rows)].astype(f32)
    mine = jnp.broadcast_to(mine, (KW, rows)).T
    mine = jnp.concatenate([mine] * (rows // KW), axis=1).astype(jnp.int32)
    copies[0].wait()
    copies[1].wait()
    query = state_ref[:, :HDT].astype(bf16)
    strong = strength[col]
    raws = [dot(query, kv_ref[r, :HDT, :]) * HDT ** (-0.5) for r in range(groups)]
    scores = []
    for r, raw in enumerate(raws):
        copies[2 + r].wait()
        bias = jnp.concatenate([bias_ref[r * per + k].astype(f32) for k in range(per)], axis=1)
        same = mine == chain_ref[:, r * rows : (r + 1) * rows]
        scores.append(raw + bias + jnp.where(same, strong, 0.0))
    top = scores[0]
    for part in scores[1:]:
        top = jnp.maximum(top, part)
    top = jnp.max(top, axis=-1, keepdims=True)
    exps = [jnp.exp(part - top) for part in scores]
    total = exps[0]
    for part in exps[1:]:
        total = total + part
    total = jnp.sum(total, axis=-1, keepdims=True)
    out = jnp.zeros((rows, HDT), f32)
    for r in range(kv_ref.shape[0]):
        out = out + dot_nt(exps[r].astype(bf16), kv_ref[r, HDT:, :])
    gated = out / total * state_ref[:, KW : KW + HDT]
    wide = jnp.concatenate([gated, jnp.zeros((rows, KW - HDT), f32)], axis=1)
    gated = wide.T[:HDT].astype(bf16)
    for k in range(out_ref.shape[0]):
        out_ref[k] = gated


def token_attention(place, state, kv, bias, chain, strength):
    rows = state.shape[0]
    out_shape = jax.ShapeDtypeStruct((bias.shape[0], HDT, rows), bf16)
    return pl.pallas_call(
        tokens_body,
        grid=(1,),
        in_specs=[SMEM] * 2 + [full(chain)] + [HBM] * 3,
        out_specs=full(out_shape),
        out_shape=out_shape,
        scratch_shapes=held((state, kv, bias))[:-1]
        + [pltpu.SemaphoreType.DMA((2 + kv.shape[0],))],
        compiler_params=pltpu.CompilerParams(vmem_limit_bytes=GRANT),
        cost_estimate=pl.CostEstimate(flops=10**9, bytes_accessed=2**22, transcendentals=2**19),
        name="tokens",
    )(place, strength, chain, state, kv, bias)


def update_body(
    place, tokens_ref, gated_ref, exit_ref, tmid_ref, back_ref, mid_ref, tout_ref, aout_ref
):
    col = place[1]
    atoms, rows = aout_ref.shape[0], tmid_ref.shape[0]
    at = pl.multiple_of(col * atoms, atoms)
    added = dot_tn(gated_ref[...], exit_ref[...])
    update = (tmid_ref[...].astype(f32) + added).astype(bf16)
    tout_ref[...] = update
    sent = dot(update, back_ref[...]).astype(bf16)
    own = tokens_ref[...]
    onehot = (lax.broadcasted_iota(jnp.int32, (rows, atoms), 0) == own).astype(f32).astype(bf16)
    aout_ref[...] = (mid_ref[pl.ds(at, atoms), :].astype(f32) + dot_tn(onehot, sent)).astype(bf16)


def updates(place, gated, exit_w, tmid, back, mid, tokens, atoms):
    rows = tmid.shape[0]
    out_shape = [
        jax.ShapeDtypeStruct((rows, CS), bf16),
        jax.ShapeDtypeStruct((atoms, CA), bf16),
    ]
    return pl.pallas_call(
        update_body,
        grid=(1,),
        in_specs=[SMEM] + [VMEM] * 6,
        out_specs=[full(shape) for shape in out_shape],
        out_shape=out_shape,
        compiler_params=pltpu.CompilerParams(vmem_limit_bytes=16 * 2**20),
        name="updates",
    )(place, tokens, gated, exit_w, tmid, back, mid)


def local(
    pair_tensor,
    token_single,
    atom_single,
    atom_token,
    chain_index,
    pair_up,
    pair_down,
    bias_heads,
    atom_gain,
    atom_proj,
    atom_exit,
    atom_pool,
    token_gain,
    token_proj,
    token_exit,
    chain_bias,
    token_back,
):
    rows, cols = pair_tensor.shape[:2]
    atom_rows = atom_single.shape[0]
    row_count = lax.axis_size("row")
    col_count = lax.axis_size("col")
    row = lax.axis_index("row")
    col = lax.axis_index("col")
    chips = col_count // 2
    row_atoms = atom_rows * col_count

    both = ("row", "col")
    at = lambda r, k, core: r * col_count + 2 * k + core
    last = col_count - 1

    last = col_count - 1
    halo = lax.ppermute(
        jnp.where(col == last, atom_single[-HALO:], atom_single[:HALO]),
        both,
        [(r * col_count + last, at(r + 1, r + 1, 0)) for r in range(row_count - 1)]
        + [((r + 1) * col_count, at(r, r, 1)) for r in range(row_count - 1)],
    )
    ext_tokens = lax.dynamic_slice_in_dim(
        jnp.pad(atom_token, (HALO, HALO)), row * row_atoms, row_atoms + 2 * HALO
    )
    ext_tokens = (ext_tokens - row * rows)[None, :]
    own_tokens = lax.dynamic_slice_in_dim(
        atom_token, row * row_atoms + col * atom_rows, atom_rows
    )
    own_tokens = (own_tokens - row * rows)[None, :]

    flip = ((col == 2 * row + 1) | (col == 2 * row + 2)).astype(jnp.int32)
    place = jnp.stack([row, col, jnp.int32(row_count), flip]).astype(jnp.int32)
    center = jnp.asarray((np.eye(CZ) - 1.0 / CZ).astype(bf16))
    weights = (pair_up, pair_down, bias_heads.T, center)
    token_bias, band, edge = pair_rows(place, pair_tensor, weights, (), 0, PART, 2, True)
    halo, band, edge, token_bias, own_atoms = lax.optimization_barrier(
        (halo, band, edge, token_bias, atom_single)
    )

    here = col // 2 == row
    even = col % 2 == 0
    ring = chips // 2
    flat = lambda k, step: k // ring * ring + (k + step) % ring
    across = lambda k: (k + ring) % chips
    band = jnp.where(even, band[:, :REACH], band[:, 2 * PART - REACH :])
    band = jnp.concatenate([band, halo.reshape(HA, HALO // HA, CA)], axis=1)
    band = jnp.where(here, band, jnp.zeros_like(band))
    band, own_atoms, edge = lax.optimization_barrier((band, own_atoms, edge))
    band_y = lax.ppermute(
        band,
        both,
        [(at(r, r, core), at(r, across(r), core)) for r in range(row_count) for core in range(2)],
    )
    cores = [[at(0, k, core) for k in range(chips)] for core in range(2)]
    own_part = jnp.concatenate([own_atoms, edge], axis=0)
    own_part = jnp.broadcast_to(own_part[None], (chips,) + own_part.shape)
    shards = lax.all_to_all(own_part, "col", 0, 0, axis_index_groups=cores)
    swap = [(i, i ^ 1) for i in range(col_count)]
    band = band + band_y
    band, token_bias = lax.optimization_barrier((band, token_bias))
    sent = [
        lax.ppermute(
            band,
            both,
            [
                (at(r, k, core), at(r, flat(k, step), core))
                for r in range(row_count)
                for k in (r, across(r))
                for core in range(2)
            ],
        )
        for step in range(1, ring)
    ]
    (token_bias,) = pair_rows(
        place, pair_tensor, weights, (token_bias,), 2 * PART, rows - 2 * PART, 1, False
    )
    theirs = lax.ppermute(shards, "col", swap)
    gain = token_gain[None]
    sent, theirs, gain, ext_tokens = lax.optimization_barrier((sent, theirs, gain, ext_tokens))
    band = band + sent[0] + sent[1] + sent[2]
    other = lax.ppermute(band, "col", swap)
    band, token_bias = lax.optimization_barrier((band, token_bias))
    head_bias = lax.all_to_all(token_bias, "col", 0, 0)

    atom_mid, token_mid, state, keyvals = atom_attention(
        place,
        (band, other),
        (shards, theirs),
        ext_tokens,
        atom_gain[None],
        atom_proj,
        atom_exit,
        atom_pool,
        token_single,
        gain,
        token_proj,
        row_count,
    )
    keyvals, head_bias = lax.optimization_barrier((keyvals, head_bias))
    keyvals = lax.all_to_all(keyvals, "row", 0, 0)
    gated = token_attention(place, state, keyvals, head_bias, chain_index[None], chain_bias)
    gated = lax.all_to_all(gated, "col", 0, 0).reshape(CS, rows)
    return tuple(
        updates(
            place, gated, token_exit, token_mid, token_back, atom_mid, own_tokens, atom_rows
        )
    )


def solution(mesh):
    placed = (
        P("row", "col", None),
        P("row", None),
        P(("row", "col"), None),
    ) + (P(),) * 14
    return jax.shard_map(
        local,
        mesh=mesh,
        in_specs=placed,
        out_specs=(P("row", None), P(("row", "col"), None)),
        check_vma=False,
    )
```

```python
import functools

import jax
import jax.numpy as jnp
import numpy as np
from jax import lax
from jax.experimental import pallas as pl
from jax.experimental.pallas import tpu as pltpu
from jax.sharding import PartitionSpec as P

CZ = 128
CS = 768
CA = 128
HT = 16
HA = 4
PH = 256
QB = 32
KW = 128
HDA = 32
HDT = 48
HB = 20
HALO = 64
PART = 112
REACH = 208
GROUP = 1024
EPS = 1e-05
GRANT = 60 * 2**20

bf16 = jnp.bfloat16
f32 = jnp.float32


def dot(left, right):
    return jnp.dot(left, right, preferred_element_type=f32)


def dot_nt(left, right):
    return lax.dot_general(left, right, (((1,), (1,)), ((), ())), preferred_element_type=f32)


def dot_tn(left, right):
    return lax.dot_general(left, right, (((0,), (0,)), ((), ())), preferred_element_type=f32)


def centered(features):
    return features - jnp.mean(features, axis=-1, keepdims=True)


def scaled(center):
    spread = jnp.mean(center * center, axis=-1, keepdims=True)
    return center * lax.rsqrt(spread + EPS)


def sigmoid(value):
    return 0.5 + 0.5 * jnp.tanh(0.5 * value)


SMEM = pl.BlockSpec(memory_space=pltpu.SMEM)
ANY = pl.BlockSpec(memory_space=pl.ANY)
HBM = pl.BlockSpec(memory_space=pltpu.HBM)
VMEM = pl.BlockSpec(memory_space=pltpu.VMEM)


def full(array):
    return pl.BlockSpec(array.shape, lambda *_: (0,) * len(array.shape))


def held(arrays):
    return [pltpu.VMEM(a.shape, a.dtype) for a in arrays] + [
        pltpu.SemaphoreType.DMA((len(arrays),))
    ]


def fetch(sources, targets, sems):
    copies = [
        pltpu.make_async_copy(source, target, sems.at[i])
        for i, (source, target) in enumerate(zip(sources, targets))
    ]
    for copy in copies:
        copy.start()
    return copies


def pair_body(place, pair_ref, up_ref, down_ref, heads_ref, center_ref, *refs, bands):
    padded = refs[-1]
    outs = refs[-4:-1] if bands else refs[-2:-1]
    pair_part = pair_ref[...].reshape(-1, CZ)
    normed = scaled(dot(pair_part, center_ref[...])).astype(bf16)
    gate = dot(normed, up_ref[:, :PH] * bf16(0.5))
    value = dot(normed, up_ref[:, PH:])
    hidden = ((gate + gate * jnp.tanh(gate)) * value).astype(bf16)
    updated = pair_part.astype(f32) + dot(hidden, down_ref[...])
    normed_two = scaled(centered(updated)).astype(bf16)
    padded[...] = jnp.zeros_like(padded)
    padded[:HB, :] = heads_ref[...].astype(f32)
    biases = dot_nt(padded[...].astype(bf16), normed_two)
    rows = pair_ref.shape[0]
    stacked = jnp.stack([biases[:, i * CZ : (i + 1) * CZ] for i in range(rows)], axis=0)
    stacked = jnp.swapaxes(stacked, 0, 1)
    outs[0][...] = stacked[HA:HB].astype(bf16)
    if bands:
        outs[1][...] = stacked[:HA].astype(bf16)

        @pl.when(pl.program_id(0) == 0)
        def _():
            edge = jnp.where(place[3] == 1, stacked[:HA, rows - HALO :], stacked[:HA, :HALO])
            edge = pltpu.roll(edge.reshape(HA * HALO, CZ), HALO, 1)
            outs[2][...] = edge.reshape(HA, HALO, CZ).astype(bf16)


def pair_rows(place, pair, weights, before, first, size, count, bands):
    rows, cols = pair.shape[:2]

    def start(i, place):
        at = first + i * size
        return pl.multiple_of(at + place[3] * (rows - 2 * at - size), 16)

    in_specs = [
        pl.BlockSpec(
            (pl.Element(size), pl.Element(cols), pl.Element(CZ)),
            lambda i, place: (start(i, place), 0, 0),
        )
    ]
    in_specs += [full(array) for array in weights]
    out_shape = [jax.ShapeDtypeStruct((HT, rows, cols), bf16)]
    out_specs = [
        pl.BlockSpec(
            (pl.Element(HT), pl.Element(size), pl.Element(cols)),
            lambda i, place: (0, start(i, place), 0),
        )
    ]
    if bands:
        out_shape.append(jax.ShapeDtypeStruct((HA, size * count, cols), bf16))
        out_specs.append(
            pl.BlockSpec(
                (HA, size, cols),
                lambda i, place: (0, i + place[3] * (count - 1 - 2 * i), 0),
            )
        )
        out_shape.append(jax.ShapeDtypeStruct((HA, HALO, cols), bf16))
        out_specs.append(full(out_shape[-1]))
    aliases = {}
    if before:
        aliases = {2 + len(weights): 0}
        in_specs += [ANY]
    cells = size * count * cols
    return pl.pallas_call(
        functools.partial(pair_body, bands=bands),
        grid_spec=pltpu.PrefetchScalarGridSpec(
            num_scalar_prefetch=1,
            grid=(count,),
            in_specs=in_specs,
            out_specs=out_specs,
            scratch_shapes=[pltpu.VMEM((32, CZ), f32)],
        ),
        out_shape=out_shape,
        input_output_aliases=aliases,
        compiler_params=pltpu.CompilerParams(vmem_limit_bytes=56 * 2**20),
        cost_estimate=pl.CostEstimate(
            flops=cells * 500000, bytes_accessed=cells * 300, transcendentals=cells * PH
        ),
        name="pair",
    )(place, pair, *weights, *before)


def atoms_body(
    place,
    tokens_ref,
    atom_gain_ref,
    proj_ref,
    exit_ref,
    pool_ref,
    single_ref,
    gain_ref,
    half_ref,
    other_ref,
    mine_hbm,
    theirs_hbm,
    tproj_hbm,
    mid_hbm,
    tmid_hbm,
    state_hbm,
    tkv_hbm,
    bias_ref,
    look_ref,
    sums_ref,
    value_ref,
    ext_ref,
    query_ref,
    gate_ref,
    mine_ref,
    theirs_ref,
    tproj_ref,
    sems,
    mid_ref,
    tmid_ref,
    state_ref,
    tkv_ref,
    out_sems,
):
    copies = fetch(
        (mine_hbm, theirs_hbm, tproj_hbm), (mine_ref, theirs_ref, tproj_ref), sems
    )
    row, col, row_count = place[0], place[1], place[2]
    total = look_ref.shape[0]
    atoms = query_ref.shape[0]
    rows = single_ref.shape[0]
    chips = mine_ref.shape[0]
    per = atoms // (2 * chips)
    even = lax.rem(col, 2) == 0
    copies[0].wait()
    copies[1].wait()
    rest = jnp.zeros((rows - REACH, KW), bf16)
    middle = jnp.zeros((rows - 2 * HALO, KW), bf16)
    before, after = [], []
    for h in range(HA):
        mine, theirs = half_ref[h], other_ref[h]
        mine, theirs = jnp.where(even, mine, theirs), jnp.where(even, theirs, mine)
        before.append(mine[REACH:])
        after.append(theirs[REACH:])
        base = h * 3 * KW
        bias_ref[:, base : base + KW] = jnp.concatenate([mine[:REACH], rest], axis=0)
        bias_ref[:, base + KW : base + 2 * KW] = jnp.concatenate([rest, theirs[:REACH]], axis=0)
        bias_ref[:, base + 2 * KW : base + 3 * KW] = jnp.concatenate(
            [mine[REACH - HALO : REACH], middle, theirs[:HALO]], axis=0
        )
    ext_ref[:HALO] = jnp.concatenate(before, axis=0)
    ext_ref[HALO + atoms :] = jnp.concatenate(after, axis=0)
    for k in range(chips):
        mine, theirs = mine_ref[k], theirs_ref[k]
        at = HALO + 2 * k * per
        ext_ref[at : at + per] = jnp.where(even, mine, theirs)
        ext_ref[at + per : at + 2 * per] = jnp.where(even, theirs, mine)
    normed = (scaled(centered(ext_ref[...].astype(f32))) * atom_gain_ref[...]).astype(bf16)
    own = normed[HALO : HALO + atoms]
    query_ref[...] = (dot(own, proj_ref[:, :CA]) * HDA ** (-0.5)).astype(bf16)
    look_ref[:, :CA] = dot(normed, proj_ref[:, CA : 2 * CA]).astype(bf16)
    value_ref[...] = dot(normed, proj_ref[:, 2 * CA : 3 * CA]).astype(bf16)
    gate_ref[...] = sigmoid(dot(own, proj_ref[:, 3 * CA :]))
    lane = lax.broadcasted_iota(jnp.int32, (KW, 3 * KW), 1)
    for t in range(total // KW):
        at = slice(t * KW, (t + 1) * KW)
        tokens = jnp.broadcast_to(tokens_ref[:, at], (KW, KW)).astype(f32).T.astype(jnp.int32)
        tokens = jnp.concatenate([tokens] * 3, axis=1)
        tokens = jnp.where(
            tokens < 0,
            tokens + 2 * KW + HALO,
            jnp.where(tokens < 2 * KW, tokens, tokens + HALO),
        )
        look_ref[at, CA:] = (tokens == lane).astype(f32).astype(bf16)
    head_of = lax.broadcasted_iota(jnp.int32, (QB, CA), 1) // HDA
    sums_ref[...] = jnp.zeros_like(sums_ref)
    row_lane = lax.broadcasted_iota(jnp.int32, (1, KW), 1)

    def group(g, counts):
        start = pl.multiple_of(g * GROUP, GROUP)
        own = pl.ds(start, GROUP)
        onehot = look_ref[pl.ds(pl.multiple_of(start + HALO, HALO), GROUP), CA : CA + 2 * KW]
        picked = dot(onehot, bias_ref[...]).astype(bf16)
        queries = query_ref[own, :]
        scores = []
        for b in range(GROUP // QB):
            part = slice(b * QB, (b + 1) * QB)
            left = jnp.concatenate(
                [
                    jnp.concatenate(
                        [
                            jnp.where(head_of == h, queries[part].astype(f32), 0.0).astype(bf16),
                            picked[part, h * 3 * KW : (h + 1) * 3 * KW],
                        ],
                        axis=1,
                    )
                    for h in range(HA)
                ],
                axis=0,
            )
            first = start + b * QB + HALO - (KW - QB) // 2
            window = look_ref[pl.ds(pl.multiple_of(first, 16), KW), :]
            at = row_lane + first
            inside = ((at >= HALO) | (row > 0)) & ((at < total - HALO) | (row < row_count - 1))
            scores.append(dot_nt(left, window) + jnp.where(inside, 0.0, -1e30))
        scores = jnp.concatenate(scores, axis=0)
        exps = jnp.exp(scores - jnp.max(scores, axis=-1, keepdims=True))
        inverse = 1.0 / jnp.sum(exps, axis=-1, keepdims=True)
        weights = exps.astype(bf16)
        attended = []
        for b in range(GROUP // QB):
            first = start + b * QB + HALO - (KW - QB) // 2
            part = slice(b * HA * QB, (b + 1) * HA * QB)
            out = dot(weights[part], value_ref[pl.ds(pl.multiple_of(first, 16), KW), :])
            out = out * inverse[part]
            merged = out[:QB]
            for h in range(1, HA):
                merged = jnp.where(head_of == h, out[h * QB : (h + 1) * QB], merged)
            attended.append(merged)
        attended = jnp.concatenate(attended, axis=0)
        gated = (attended * gate_ref[own, :]).astype(bf16)
        single = ext_ref[pl.ds(pl.multiple_of(start + HALO, HALO), GROUP), :].astype(f32)
        mid = (single + dot(gated, exit_ref[...])).astype(bf16)
        mid_ref[own, :] = mid
        pooled = jnp.maximum(dot(mid, pool_ref[...]), 0.0).astype(bf16)
        sums_ref[...] += dot_tn(onehot, pooled)
        return counts + jnp.sum(onehot.astype(f32).T, axis=1, keepdims=True)

    counts = lax.fori_loop(0, atoms // GROUP, group, jnp.zeros((rows, 1), f32))
    token_mid = (single_ref[...].astype(f32) + sums_ref[...] / counts).astype(bf16)
    tmid_ref[...] = token_mid
    stores = fetch((mid_ref, tmid_ref), (mid_hbm, tmid_hbm), out_sems)
    normed = (scaled(centered(token_mid.astype(f32))) * gain_ref[...]).astype(bf16)

    copies[-1].wait()

    def head_part(part):
        start = part * CS + col * HDT
        base = jnp.minimum(start // KW * KW, 4 * CS - 2 * KW)
        base = pl.multiple_of(base, KW)
        wide = dot(normed, tproj_ref[:, pl.ds(base, 2 * KW)])
        return pltpu.roll(wide, lax.rem(2 * KW - (start - base), 2 * KW), 1)[:, :KW]

    state_ref[...] = jnp.concatenate([head_part(0), sigmoid(head_part(1))], axis=1)
    keyvals = jnp.concatenate([head_part(2).T[:HDT], head_part(3).T[:HDT]], axis=0)
    tkv_ref[...] = keyvals.astype(bf16)
    last = [(state_ref, state_hbm)] + [(tkv_ref, tkv_hbm.at[k]) for k in range(tkv_hbm.shape[0])]
    for i, (source, target) in enumerate(last):
        stores.append(pltpu.make_async_copy(source, target, out_sems.at[2 + i]))
        stores[-1].start()
    for copy in stores:
        copy.wait()


def atom_attention(
    place, bands, shards, tokens, atom_gain, proj, exit_w, pool, single, gain, tproj, copies
):
    total = tokens.shape[1]
    atoms = total - 2 * HALO
    rows = single.shape[0]
    operands = (tokens, atom_gain, proj, exit_w, pool, single, gain)
    fetched = (*shards, tproj)
    out_shape = [
        jax.ShapeDtypeStruct((atoms, CA), bf16),
        jax.ShapeDtypeStruct((rows, CS), bf16),
        jax.ShapeDtypeStruct((rows, 2 * KW), f32),
        jax.ShapeDtypeStruct((copies, 2 * HDT, rows), bf16),
    ]
    return pl.pallas_call(
        atoms_body,
        grid=(1,),
        in_specs=[SMEM]
        + [full(array) for array in operands]
        + [VMEM] * len(bands)
        + [HBM] * len(fetched),
        out_specs=[HBM] * len(out_shape),
        out_shape=out_shape,
        scratch_shapes=[
            pltpu.VMEM((rows, HA * 3 * KW), bf16),
            pltpu.VMEM((total, CA + 3 * KW), bf16),
            pltpu.VMEM((rows, CS), f32),
            pltpu.VMEM((total, CA), bf16),
            pltpu.VMEM((total, CA), bf16),
            pltpu.VMEM((atoms, CA), bf16),
            pltpu.VMEM((atoms, CA), f32),
        ]
        + held(fetched)
        + [pltpu.VMEM(a.shape, a.dtype) for a in out_shape[:3]]
        + [pltpu.VMEM((2 * HDT, rows), bf16), pltpu.SemaphoreType.DMA((3 + copies,))],
        compiler_params=pltpu.CompilerParams(vmem_limit_bytes=GRANT),
        cost_estimate=pl.CostEstimate(
            flops=10**10, bytes_accessed=2**24, transcendentals=2**22
        ),
        name="atoms",
    )(place, *operands, *bands, *fetched)


def tokens_body(
    place, strength, chain_ref, state_hbm, kv_hbm, bias_hbm, out_ref, state_ref, kv_ref, bias_ref, sems
):
    per = state_hbm.shape[0] // bias_hbm.shape[2]
    groups = kv_hbm.shape[0]
    bias_parts = [pl.ds(r * per, per) for r in range(groups)]
    copies = fetch(
        [state_hbm, kv_hbm] + [bias_hbm.at[part] for part in bias_parts],
        [state_ref, kv_ref] + [bias_ref.at[part] for part in bias_parts],
        sems,
    )
    col = place[1]
    rows = state_ref.shape[0]
    own = pl.multiple_of(place[0] * rows, rows)
    mine = chain_ref[:, pl.ds(own, rows)].astype(f32)
    mine = jnp.broadcast_to(mine, (KW, rows)).T
    mine = jnp.concatenate([mine] * (rows // KW), axis=1).astype(jnp.int32)
    copies[0].wait()
    copies[1].wait()
    query = state_ref[:, :HDT].astype(bf16)
    strong = strength[col]
    raws = [dot(query, kv_ref[r, :HDT, :]) * HDT ** (-0.5) for r in range(groups)]
    scores = []
    for r, raw in enumerate(raws):
        copies[2 + r].wait()
        bias = jnp.concatenate([bias_ref[r * per + k].astype(f32) for k in range(per)], axis=1)
        same = mine == chain_ref[:, r * rows : (r + 1) * rows]
        scores.append(raw + bias + jnp.where(same, strong, 0.0))
    top = scores[0]
    for part in scores[1:]:
        top = jnp.maximum(top, part)
    top = jnp.max(top, axis=-1, keepdims=True)
    exps = [jnp.exp(part - top) for part in scores]
    total = exps[0]
    for part in exps[1:]:
        total = total + part
    total = jnp.sum(total, axis=-1, keepdims=True)
    out = jnp.zeros((rows, HDT), f32)
    for r in range(kv_ref.shape[0]):
        out = out + dot_nt(exps[r].astype(bf16), kv_ref[r, HDT:, :])
    gated = out / total * state_ref[:, KW : KW + HDT]
    wide = jnp.concatenate([gated, jnp.zeros((rows, KW - HDT), f32)], axis=1)
    gated = wide.T[:HDT].astype(bf16)
    for k in range(out_ref.shape[0]):
        out_ref[k] = gated


def token_attention(place, state, kv, bias, chain, strength):
    rows = state.shape[0]
    out_shape = jax.ShapeDtypeStruct((bias.shape[0], HDT, rows), bf16)
    return pl.pallas_call(
        tokens_body,
        grid=(1,),
        in_specs=[SMEM] * 2 + [full(chain)] + [HBM] * 3,
        out_specs=full(out_shape),
        out_shape=out_shape,
        scratch_shapes=held((state, kv, bias))[:-1]
        + [pltpu.SemaphoreType.DMA((2 + kv.shape[0],))],
        compiler_params=pltpu.CompilerParams(vmem_limit_bytes=GRANT),
        cost_estimate=pl.CostEstimate(flops=10**9, bytes_accessed=2**22, transcendentals=2**19),
        name="tokens",
    )(place, strength, chain, state, kv, bias)


def update_body(
    place, tokens_ref, gated_ref, exit_ref, tmid_ref, back_ref, mid_ref, tout_ref, aout_ref
):
    col = place[1]
    atoms, rows = aout_ref.shape[0], tmid_ref.shape[0]
    at = pl.multiple_of(col * atoms, atoms)
    added = dot_tn(gated_ref[...], exit_ref[...])
    update = (tmid_ref[...].astype(f32) + added).astype(bf16)
    tout_ref[...] = update
    sent = dot(update, back_ref[...]).astype(bf16)
    own = tokens_ref[...]
    onehot = (lax.broadcasted_iota(jnp.int32, (rows, atoms), 0) == own).astype(f32).astype(bf16)
    aout_ref[...] = (mid_ref[pl.ds(at, atoms), :].astype(f32) + dot_tn(onehot, sent)).astype(bf16)


def updates(place, gated, exit_w, tmid, back, mid, tokens, atoms):
    rows = tmid.shape[0]
    out_shape = [
        jax.ShapeDtypeStruct((rows, CS), bf16),
        jax.ShapeDtypeStruct((atoms, CA), bf16),
    ]
    return pl.pallas_call(
        update_body,
        grid=(1,),
        in_specs=[SMEM] + [VMEM] * 6,
        out_specs=[full(shape) for shape in out_shape],
        out_shape=out_shape,
        compiler_params=pltpu.CompilerParams(vmem_limit_bytes=16 * 2**20),
        name="updates",
    )(place, tokens, gated, exit_w, tmid, back, mid)


def local(
    pair_tensor,
    token_single,
    atom_single,
    atom_token,
    chain_index,
    pair_up,
    pair_down,
    bias_heads,
    atom_gain,
    atom_proj,
    atom_exit,
    atom_pool,
    token_gain,
    token_proj,
    token_exit,
    chain_bias,
    token_back,
):
    rows, cols = pair_tensor.shape[:2]
    atom_rows = atom_single.shape[0]
    row_count = lax.axis_size("row")
    col_count = lax.axis_size("col")
    row = lax.axis_index("row")
    col = lax.axis_index("col")
    chips = col_count // 2
    row_atoms = atom_rows * col_count

    both = ("row", "col")
    at = lambda r, k, core: r * col_count + 2 * k + core
    last = col_count - 1

    last = col_count - 1
    halo = lax.ppermute(
        jnp.where(col == last, atom_single[-HALO:], atom_single[:HALO]),
        both,
        [(r * col_count + last, at(r + 1, r + 1, 0)) for r in range(row_count - 1)]
        + [((r + 1) * col_count, at(r, r, 1)) for r in range(row_count - 1)],
    )
    ext_tokens = lax.dynamic_slice_in_dim(
        jnp.pad(atom_token, (HALO, HALO)), row * row_atoms, row_atoms + 2 * HALO
    )
    ext_tokens = (ext_tokens - row * rows)[None, :]
    own_tokens = lax.dynamic_slice_in_dim(
        atom_token, row * row_atoms + col * atom_rows, atom_rows
    )
    own_tokens = (own_tokens - row * rows)[None, :]

    flip = ((col == 2 * row + 1) | (col == 2 * row + 2)).astype(jnp.int32)
    place = jnp.stack([row, col, jnp.int32(row_count), flip]).astype(jnp.int32)
    center = jnp.asarray((np.eye(CZ) - 1.0 / CZ).astype(bf16))
    weights = (pair_up, pair_down, bias_heads.T, center)
    token_bias, band, edge = pair_rows(place, pair_tensor, weights, (), 0, PART, 2, True)
    halo, band, edge, token_bias, own_atoms = lax.optimization_barrier(
        (halo, band, edge, token_bias, atom_single)
    )

    here = col // 2 == row
    even = col % 2 == 0
    ring = chips // 2
    flat = lambda k, step: k // ring * ring + (k + step) % ring
    across = lambda k: (k + ring) % chips
    split = REACH - HALO
    band = jnp.where(even, band[:, :REACH], band[:, 2 * PART - REACH :])
    band = jnp.concatenate([band, halo.reshape(HA, HALO // HA, CA)], axis=1)
    none = jnp.zeros_like(band)
    place_in = lax.broadcasted_iota(jnp.int32, band.shape, 1)
    lane = lax.broadcasted_iota(jnp.int32, band.shape, 2)
    late = (place_in >= split) & (place_in < REACH) & (lane < HALO)
    early = (place_in < HALO) & (lane >= HALO)
    late_edge = jnp.concatenate([none[:, :split], edge, none[:, REACH:]], axis=1)
    early_edge = jnp.concatenate([edge, none[:, HALO:]], axis=1)
    band = jnp.where(jnp.where(even, late, early), none, band)
    edge = jnp.where(
        even, jnp.where(early, early_edge, none), jnp.where(late, late_edge, none)
    )
    band = jnp.where(here, band, edge)
    over_y = [
        (at(r, r, core), at(r, across(r), core)) for r in range(row_count) for core in range(2)
    ]
    beside = lambda to: [(at(r, r - 1, 1), at(r, to(r), 0)) for r in range(1, row_count)] + [
        (at(r, r + 1, 0), at(r, to(r), 1)) for r in range(row_count - 1)
    ]
    arrived = [
        lax.ppermute(band, both, over_y + beside(lambda r: r)),
        lax.ppermute(band, both, beside(across)),
    ]
    cores = [[at(0, k, core) for k in range(chips)] for core in range(2)]
    own_atoms = jnp.broadcast_to(own_atoms[None], (chips,) + own_atoms.shape)
    shards = lax.all_to_all(own_atoms, "col", 0, 0, axis_index_groups=cores)
    swap = [(i, i ^ 1) for i in range(col_count)]
    arrived = lax.optimization_barrier(arrived)
    band = jnp.where(here, band, none) + arrived[0] + arrived[1]
    band, token_bias = lax.optimization_barrier((band, token_bias))
    sent = [
        lax.ppermute(
            band,
            both,
            [
                (at(r, k, core), at(r, flat(k, step), core))
                for r in range(row_count)
                for k in (r, across(r))
                for core in range(2)
            ],
        )
        for step in range(1, ring)
    ]
    (token_bias,) = pair_rows(
        place, pair_tensor, weights, (token_bias,), 2 * PART, rows - 2 * PART, 1, False
    )
    theirs = lax.ppermute(shards, "col", swap)
    gain = token_gain[None]
    theirs, token_bias = lax.optimization_barrier((theirs, token_bias))
    head_bias = lax.all_to_all(token_bias, "col", 0, 0)
    sent, theirs, gain, ext_tokens = lax.optimization_barrier((sent, theirs, gain, ext_tokens))
    band = band + sent[0] + sent[1] + sent[2]
    other = lax.ppermute(band, "col", swap)

    atom_mid, token_mid, state, keyvals = atom_attention(
        place,
        (band, other),
        (shards, theirs),
        ext_tokens,
        atom_gain[None],
        atom_proj,
        atom_exit,
        atom_pool,
        token_single,
        gain,
        token_proj,
        row_count,
    )
    keyvals, head_bias = lax.optimization_barrier((keyvals, head_bias))
    keyvals = lax.all_to_all(keyvals, "row", 0, 0)
    gated = token_attention(place, state, keyvals, head_bias, chain_index[None], chain_bias)
    gated = lax.all_to_all(gated, "col", 0, 0).reshape(CS, rows)
    return tuple(
        updates(
            place, gated, token_exit, token_mid, token_back, atom_mid, own_tokens, atom_rows
        )
    )


def solution(mesh):
    placed = (
        P("row", "col", None),
        P("row", None),
        P(("row", "col"), None),
    ) + (P(),) * 14
    return jax.shard_map(
        local,
        mesh=mesh,
        in_specs=placed,
        out_specs=(P("row", None), P(("row", "col"), None)),
        check_vma=False,
    )
```

```python
import functools

import jax
import jax.numpy as jnp
import numpy as np
from jax import lax
from jax.experimental import pallas as pl
from jax.experimental.pallas import tpu as pltpu
from jax.sharding import PartitionSpec as P

CZ = 128
CS = 768
CA = 128
HT = 16
HA = 4
PH = 256
QB = 32
KW = 128
HDA = 32
HDT = 48
HB = 20
HALO = 64
PART = 112
REACH = 208
GROUP = 1024
EPS = 1e-05
GRANT = 60 * 2**20

bf16 = jnp.bfloat16
f32 = jnp.float32


def dot(left, right):
    return jnp.dot(left, right, preferred_element_type=f32)


def dot_nt(left, right):
    return lax.dot_general(left, right, (((1,), (1,)), ((), ())), preferred_element_type=f32)


def dot_tn(left, right):
    return lax.dot_general(left, right, (((0,), (0,)), ((), ())), preferred_element_type=f32)


def centered(features):
    return features - jnp.mean(features, axis=-1, keepdims=True)


def scaled(center):
    spread = jnp.mean(center * center, axis=-1, keepdims=True)
    return center * lax.rsqrt(spread + EPS)


def sigmoid(value):
    return 0.5 + 0.5 * jnp.tanh(0.5 * value)


SMEM = pl.BlockSpec(memory_space=pltpu.SMEM)
ANY = pl.BlockSpec(memory_space=pl.ANY)
HBM = pl.BlockSpec(memory_space=pltpu.HBM)
VMEM = pl.BlockSpec(memory_space=pltpu.VMEM)


def full(array):
    return pl.BlockSpec(array.shape, lambda *_: (0,) * len(array.shape))


def held(arrays):
    return [pltpu.VMEM(a.shape, a.dtype) for a in arrays] + [
        pltpu.SemaphoreType.DMA((len(arrays),))
    ]


def fetch(sources, targets, sems):
    copies = [
        pltpu.make_async_copy(source, target, sems.at[i])
        for i, (source, target) in enumerate(zip(sources, targets))
    ]
    for copy in copies:
        copy.start()
    return copies


def pair_body(place, pair_ref, up_ref, down_ref, heads_ref, center_ref, *refs, bands):
    if bands:
        *_, bias_ref, band_ref, padded, saved = refs
    else:
        *_, bias_ref, padded = refs
    pair_part = pair_ref[...].reshape(-1, CZ)
    normed = scaled(dot(pair_part, center_ref[...])).astype(bf16)
    gate = dot(normed, up_ref[:, :PH] * bf16(0.5))
    value = dot(normed, up_ref[:, PH:])
    hidden = ((gate + gate * jnp.tanh(gate)) * value).astype(bf16)
    updated = pair_part.astype(f32) + dot(hidden, down_ref[...])
    normed_two = scaled(centered(updated)).astype(bf16)
    padded[...] = jnp.zeros_like(padded)
    padded[:HB, :] = heads_ref[...].astype(f32)
    biases = dot_nt(padded[...].astype(bf16), normed_two)
    rows = pair_ref.shape[0]
    stacked = jnp.stack([biases[:, i * CZ : (i + 1) * CZ] for i in range(rows)], axis=0)
    stacked = jnp.swapaxes(stacked, 0, 1)
    bias_ref[...] = stacked[HA:HB].astype(bf16)
    if bands:
        step = pl.program_id(0)
        flip, here = place[3] == 1, place[4] == 1

        @pl.when(step == 0)
        def _():
            edge = jnp.where(flip, stacked[:HA, rows - HALO :], stacked[:HA, :HALO])
            edge = pltpu.roll(edge.reshape(HA * HALO, CZ), HALO, 1)
            saved[...] = edge.reshape(HA, HALO, CZ)

        low = REACH - HALO - rows
        high = rows - HALO - low
        edge = saved[...]
        blank = jnp.zeros((HA, rows, CZ), f32)
        placed = jnp.where(
            flip,
            jnp.concatenate([blank[:, :high], edge, blank[:, :low]], axis=1),
            jnp.concatenate([blank[:, :low], edge, blank[:, :high]], axis=1),
        )
        at = lax.broadcasted_iota(jnp.int32, (HA, rows, CZ), 1) - jnp.where(flip, high, low)
        lane = lax.broadcasted_iota(jnp.int32, (HA, rows, CZ), 2)
        side = jnp.where(flip, lane - HALO, lane)
        spare = (at >= 0) & (at < HALO) & (side >= 0) & (side < HALO) & (step == 1)
        own = jnp.where(here, stacked[:HA], 0.0)
        band_ref[...] = jnp.where(spare, jnp.where(here, 0.0, placed), own).astype(bf16)


def pair_rows(place, pair, weights, before, first, size, count, bands):
    rows, cols = pair.shape[:2]

    def start(i, place):
        at = first + i * size
        return pl.multiple_of(at + place[3] * (rows - 2 * at - size), 16)

    in_specs = [
        pl.BlockSpec(
            (pl.Element(size), pl.Element(cols), pl.Element(CZ)),
            lambda i, place: (start(i, place), 0, 0),
        )
    ]
    in_specs += [full(array) for array in weights]
    out_shape = [jax.ShapeDtypeStruct((HT, rows, cols), bf16)]
    out_specs = [
        pl.BlockSpec(
            (pl.Element(HT), pl.Element(size), pl.Element(cols)),
            lambda i, place: (0, start(i, place), 0),
        )
    ]
    if bands:
        out_shape.append(jax.ShapeDtypeStruct((HA, size * count, cols), bf16))
        out_specs.append(
            pl.BlockSpec(
                (HA, size, cols),
                lambda i, place: (0, i + place[3] * (count - 1 - 2 * i), 0),
            )
        )
    aliases = {}
    if before:
        aliases = {2 + len(weights): 0}
        in_specs += [ANY]
    cells = size * count * cols
    return pl.pallas_call(
        functools.partial(pair_body, bands=bands),
        grid_spec=pltpu.PrefetchScalarGridSpec(
            num_scalar_prefetch=1,
            grid=(count,),
            in_specs=in_specs,
            out_specs=out_specs,
            scratch_shapes=[pltpu.VMEM((32, CZ), f32)]
            + [pltpu.VMEM((HA, HALO, CZ), f32)] * bands,
        ),
        out_shape=out_shape,
        input_output_aliases=aliases,
        compiler_params=pltpu.CompilerParams(vmem_limit_bytes=56 * 2**20),
        cost_estimate=pl.CostEstimate(
            flops=cells * 500000, bytes_accessed=cells * 300, transcendentals=cells * PH
        ),
        name="pair",
    )(place, pair, *weights, *before)


def atoms_body(
    place,
    tokens_ref,
    atom_gain_ref,
    proj_ref,
    exit_ref,
    pool_ref,
    single_ref,
    gain_ref,
    half_ref,
    other_ref,
    mine_hbm,
    theirs_hbm,
    tproj_hbm,
    mid_hbm,
    tmid_hbm,
    state_hbm,
    tkv_hbm,
    bias_ref,
    look_ref,
    sums_ref,
    value_ref,
    ext_ref,
    query_ref,
    gate_ref,
    mine_ref,
    theirs_ref,
    tproj_ref,
    sems,
    mid_ref,
    tmid_ref,
    state_ref,
    tkv_ref,
    out_sems,
):
    copies = fetch(
        (mine_hbm, theirs_hbm, tproj_hbm), (mine_ref, theirs_ref, tproj_ref), sems
    )
    row, col, row_count = place[0], place[1], place[2]
    total = look_ref.shape[0]
    atoms = query_ref.shape[0]
    rows = single_ref.shape[0]
    chips = mine_ref.shape[0]
    per = atoms // (2 * chips)
    even = lax.rem(col, 2) == 0
    copies[0].wait()
    copies[1].wait()
    rest = jnp.zeros((rows - REACH, KW), bf16)
    skip = 2 * PART - REACH
    middle = jnp.zeros((rows - 2 * HALO, KW), bf16)
    for h in range(HA):
        mine, theirs = half_ref[h], other_ref[h]
        mine, theirs = jnp.where(even, mine, theirs), jnp.where(even, theirs, mine)
        base = h * 3 * KW
        bias_ref[:, base : base + KW] = jnp.concatenate([mine[:REACH], rest], axis=0)
        bias_ref[:, base + KW : base + 2 * KW] = jnp.concatenate([rest, theirs[skip:]], axis=0)
        bias_ref[:, base + 2 * KW : base + 3 * KW] = jnp.concatenate(
            [mine[REACH - HALO : REACH], middle, theirs[skip : skip + HALO]], axis=0
        )
    mine, theirs = mine_ref[row, per:], theirs_ref[row, per:]
    ext_ref[:HALO] = jnp.where(even, mine, theirs)
    ext_ref[HALO + atoms :] = jnp.where(even, theirs, mine)
    for k in range(chips):
        mine, theirs = mine_ref[k, :per], theirs_ref[k, :per]
        at = HALO + 2 * k * per
        ext_ref[at : at + per] = jnp.where(even, mine, theirs)
        ext_ref[at + per : at + 2 * per] = jnp.where(even, theirs, mine)
    normed = (scaled(centered(ext_ref[...].astype(f32))) * atom_gain_ref[...]).astype(bf16)
    own = normed[HALO : HALO + atoms]
    query_ref[...] = (dot(own, proj_ref[:, :CA]) * HDA ** (-0.5)).astype(bf16)
    look_ref[:, :CA] = dot(normed, proj_ref[:, CA : 2 * CA]).astype(bf16)
    value_ref[...] = dot(normed, proj_ref[:, 2 * CA : 3 * CA]).astype(bf16)
    gate_ref[...] = sigmoid(dot(own, proj_ref[:, 3 * CA :]))
    lane = lax.broadcasted_iota(jnp.int32, (KW, 3 * KW), 1)
    for t in range(total // KW):
        at = slice(t * KW, (t + 1) * KW)
        tokens = jnp.broadcast_to(tokens_ref[t : t + 1, :], (KW, KW)).astype(f32).T.astype(jnp.int32)
        tokens = jnp.concatenate([tokens] * 3, axis=1)
        tokens = jnp.where(
            tokens < 0,
            tokens + 2 * KW + HALO,
            jnp.where(tokens < 2 * KW, tokens, tokens + HALO),
        )
        look_ref[at, CA:] = (tokens == lane).astype(f32).astype(bf16)
    head_of = lax.broadcasted_iota(jnp.int32, (QB, CA), 1) // HDA
    sums_ref[...] = jnp.zeros_like(sums_ref)
    row_lane = lax.broadcasted_iota(jnp.int32, (1, KW), 1)

    def group(g, counts):
        start = pl.multiple_of(g * GROUP, GROUP)
        own = pl.ds(start, GROUP)
        onehot = look_ref[pl.ds(pl.multiple_of(start + HALO, HALO), GROUP), CA : CA + 2 * KW]
        picked = dot(onehot, bias_ref[...]).astype(bf16)
        queries = query_ref[own, :]
        scores = []
        for b in range(GROUP // QB):
            part = slice(b * QB, (b + 1) * QB)
            left = jnp.concatenate(
                [
                    jnp.concatenate(
                        [
                            jnp.where(head_of == h, queries[part].astype(f32), 0.0).astype(bf16),
                            picked[part, h * 3 * KW : (h + 1) * 3 * KW],
                        ],
                        axis=1,
                    )
                    for h in range(HA)
                ],
                axis=0,
            )
            first = start + b * QB + HALO - (KW - QB) // 2
            window = look_ref[pl.ds(pl.multiple_of(first, 16), KW), :]
            at = row_lane + first
            inside = ((at >= HALO) | (row > 0)) & ((at < total - HALO) | (row < row_count - 1))
            scores.append(dot_nt(left, window) + jnp.where(inside, 0.0, -1e30))
        scores = jnp.concatenate(scores, axis=0)
        exps = jnp.exp(scores - jnp.max(scores, axis=-1, keepdims=True))
        inverse = 1.0 / jnp.sum(exps, axis=-1, keepdims=True)
        weights = exps.astype(bf16)
        attended = []
        for b in range(GROUP // QB):
            first = start + b * QB + HALO - (KW - QB) // 2
            part = slice(b * HA * QB, (b + 1) * HA * QB)
            out = dot(weights[part], value_ref[pl.ds(pl.multiple_of(first, 16), KW), :])
            out = out * inverse[part]
            merged = out[:QB]
            for h in range(1, HA):
                merged = jnp.where(head_of == h, out[h * QB : (h + 1) * QB], merged)
            attended.append(merged)
        attended = jnp.concatenate(attended, axis=0)
        gated = (attended * gate_ref[own, :]).astype(bf16)
        single = ext_ref[pl.ds(pl.multiple_of(start + HALO, HALO), GROUP), :].astype(f32)
        mid = (single + dot(gated, exit_ref[...])).astype(bf16)
        mid_ref[own, :] = mid
        pooled = jnp.maximum(dot(mid, pool_ref[...]), 0.0).astype(bf16)
        sums_ref[...] += dot_tn(onehot, pooled)
        return counts + jnp.sum(onehot.astype(f32).T, axis=1, keepdims=True)

    counts = lax.fori_loop(0, atoms // GROUP, group, jnp.zeros((rows, 1), f32), unroll=True)
    token_mid = (single_ref[...].astype(f32) + sums_ref[...] / counts).astype(bf16)
    tmid_ref[...] = token_mid
    stores = fetch((mid_ref, tmid_ref), (mid_hbm, tmid_hbm), out_sems)
    gain = jnp.concatenate([gain_ref[k : k + 1, :] for k in range(gain_ref.shape[0])], axis=1)
    normed = (scaled(centered(token_mid.astype(f32))) * gain).astype(bf16)

    copies[-1].wait()

    def head_part(part):
        start = part * CS + col * HDT
        base = jnp.minimum(start // KW * KW, 4 * CS - 2 * KW)
        base = pl.multiple_of(base, KW)
        wide = dot(normed, tproj_ref[:, pl.ds(base, 2 * KW)])
        return pltpu.roll(wide, lax.rem(2 * KW - (start - base), 2 * KW), 1)[:, :KW]

    state_ref[...] = jnp.concatenate([head_part(0), sigmoid(head_part(1))], axis=1)
    keyvals = jnp.concatenate([head_part(2).T[:HDT], head_part(3).T[:HDT]], axis=0)
    tkv_ref[...] = keyvals.astype(bf16)
    last = [(state_ref, state_hbm)] + [(tkv_ref, tkv_hbm.at[k]) for k in range(tkv_hbm.shape[0])]
    for i, (source, target) in enumerate(last):
        stores.append(pltpu.make_async_copy(source, target, out_sems.at[2 + i]))
        stores[-1].start()
    for copy in stores:
        copy.wait()


def atom_attention(
    place, bands, shards, tokens, atom_gain, proj, exit_w, pool, single, gain, tproj, copies
):
    total = tokens.size
    atoms = total - 2 * HALO
    rows = single.shape[0]
    operands = (tokens, atom_gain, proj, exit_w, pool, single, gain)
    fetched = (*shards, tproj)
    out_shape = [
        jax.ShapeDtypeStruct((atoms, CA), bf16),
        jax.ShapeDtypeStruct((rows, CS), bf16),
        jax.ShapeDtypeStruct((rows, 2 * KW), f32),
        jax.ShapeDtypeStruct((copies, 2 * HDT, rows), bf16),
    ]
    return pl.pallas_call(
        atoms_body,
        grid=(1,),
        in_specs=[SMEM]
        + [full(array) for array in operands]
        + [VMEM] * len(bands)
        + [HBM] * len(fetched),
        out_specs=[HBM] * len(out_shape),
        out_shape=out_shape,
        scratch_shapes=[
            pltpu.VMEM((rows, HA * 3 * KW), bf16),
            pltpu.VMEM((total, CA + 3 * KW), bf16),
            pltpu.VMEM((rows, CS), f32),
            pltpu.VMEM((total, CA), bf16),
            pltpu.VMEM((total, CA), bf16),
            pltpu.VMEM((atoms, CA), bf16),
            pltpu.VMEM((atoms, CA), f32),
        ]
        + held(fetched)
        + [pltpu.VMEM(a.shape, a.dtype) for a in out_shape[:3]]
        + [pltpu.VMEM((2 * HDT, rows), bf16), pltpu.SemaphoreType.DMA((3 + copies,))],
        compiler_params=pltpu.CompilerParams(vmem_limit_bytes=GRANT),
        cost_estimate=pl.CostEstimate(
            flops=10**10, bytes_accessed=2**24, transcendentals=2**22
        ),
        name="atoms",
    )(place, *operands, *bands, *fetched)


def tokens_body(
    place, strength, chain_ref, state_hbm, kv_hbm, bias_hbm, out_ref, state_ref, kv_ref, bias_ref, sems
):
    per = state_hbm.shape[0] // bias_hbm.shape[2]
    groups = kv_hbm.shape[0]
    bias_parts = [pl.ds(r * per, per) for r in range(groups)]
    copies = fetch(
        [state_hbm, kv_hbm] + [bias_hbm.at[part] for part in bias_parts],
        [state_ref, kv_ref] + [bias_ref.at[part] for part in bias_parts],
        sems,
    )
    col = place[1]
    rows = state_ref.shape[0]
    own = pl.multiple_of(place[0] * rows, rows)
    mine = chain_ref[:, pl.ds(own, rows)].astype(f32)
    mine = jnp.broadcast_to(mine, (KW, rows)).T
    mine = jnp.concatenate([mine] * (rows // KW), axis=1).astype(jnp.int32)
    copies[0].wait()
    copies[1].wait()
    query = state_ref[:, :HDT].astype(bf16)
    strong = strength[col]
    raws = [dot(query, kv_ref[r, :HDT, :]) * HDT ** (-0.5) for r in range(groups)]
    scores = []
    for r, raw in enumerate(raws):
        copies[2 + r].wait()
        bias = jnp.concatenate([bias_ref[r * per + k].astype(f32) for k in range(per)], axis=1)
        same = mine == chain_ref[:, r * rows : (r + 1) * rows]
        scores.append(raw + bias + jnp.where(same, strong, 0.0))
    top = scores[0]
    for part in scores[1:]:
        top = jnp.maximum(top, part)
    top = jnp.max(top, axis=-1, keepdims=True)
    exps = [jnp.exp(part - top) for part in scores]
    total = exps[0]
    for part in exps[1:]:
        total = total + part
    total = jnp.sum(total, axis=-1, keepdims=True)
    out = jnp.zeros((rows, HDT), f32)
    for r in range(kv_ref.shape[0]):
        out = out + dot_nt(exps[r].astype(bf16), kv_ref[r, HDT:, :])
    gated = out / total * state_ref[:, KW : KW + HDT]
    wide = jnp.concatenate([gated, jnp.zeros((rows, KW - HDT), f32)], axis=1)
    gated = wide.T[:HDT].astype(bf16)
    for k in range(out_ref.shape[0]):
        out_ref[k] = gated


def token_attention(place, state, kv, bias, chain, strength):
    rows = state.shape[0]
    out_shape = jax.ShapeDtypeStruct((bias.shape[0], HDT, rows), bf16)
    return pl.pallas_call(
        tokens_body,
        grid=(1,),
        in_specs=[SMEM] * 2 + [full(chain)] + [HBM] * 3,
        out_specs=full(out_shape),
        out_shape=out_shape,
        scratch_shapes=held((state, kv, bias))[:-1]
        + [pltpu.SemaphoreType.DMA((2 + kv.shape[0],))],
        compiler_params=pltpu.CompilerParams(vmem_limit_bytes=GRANT),
        cost_estimate=pl.CostEstimate(flops=10**9, bytes_accessed=2**22, transcendentals=2**19),
        name="tokens",
    )(place, strength, chain, state, kv, bias)


def update_body(
    place, tokens_ref, gated_ref, exit_ref, tmid_ref, back_ref, mid_ref, tout_ref, aout_ref
):
    col = place[1]
    atoms, rows = aout_ref.shape[0], tmid_ref.shape[0]
    at = pl.multiple_of(col * atoms, atoms)
    added = dot_tn(gated_ref[...], exit_ref[...])
    update = (tmid_ref[...].astype(f32) + added).astype(bf16)
    tout_ref[...] = update
    sent = dot(update, back_ref[...]).astype(bf16)
    own = tokens_ref[...]
    onehot = (lax.broadcasted_iota(jnp.int32, (rows, atoms), 0) == own).astype(f32).astype(bf16)
    aout_ref[...] = (mid_ref[pl.ds(at, atoms), :].astype(f32) + dot_tn(onehot, sent)).astype(bf16)


def updates(place, gated, exit_w, tmid, back, mid, tokens, atoms):
    rows = tmid.shape[0]
    out_shape = [
        jax.ShapeDtypeStruct((rows, CS), bf16),
        jax.ShapeDtypeStruct((atoms, CA), bf16),
    ]
    return pl.pallas_call(
        update_body,
        grid=(1,),
        in_specs=[SMEM] + [VMEM] * 6,
        out_specs=[full(shape) for shape in out_shape],
        out_shape=out_shape,
        compiler_params=pltpu.CompilerParams(vmem_limit_bytes=16 * 2**20),
        name="updates",
    )(place, tokens, gated, exit_w, tmid, back, mid)


def local(
    pair_tensor,
    token_single,
    atom_single,
    atom_token,
    chain_index,
    pair_up,
    pair_down,
    bias_heads,
    atom_gain,
    atom_proj,
    atom_exit,
    atom_pool,
    token_gain,
    token_proj,
    token_exit,
    chain_bias,
    token_back,
):
    rows, cols = pair_tensor.shape[:2]
    atom_rows = atom_single.shape[0]
    row_count = lax.axis_size("row")
    col_count = lax.axis_size("col")
    row = lax.axis_index("row")
    col = lax.axis_index("col")
    chips = col_count // 2
    row_atoms = atom_rows * col_count

    both = ("row", "col")
    at = lambda r, k, core: r * col_count + 2 * k + core
    last = col_count - 1

    last = col_count - 1
    halo = lax.ppermute(
        jnp.where(col == last, atom_single[-HALO:], atom_single[:HALO]),
        both,
        [(r * col_count + last, at(r + 1, r + 1, 0)) for r in range(row_count - 1)]
        + [((r + 1) * col_count, at(r, r, 1)) for r in range(row_count - 1)],
    )
    ext_tokens = lax.dynamic_slice_in_dim(
        jnp.pad(atom_token, (HALO, HALO)), row * row_atoms, row_atoms + 2 * HALO
    )
    ext_tokens = (ext_tokens - row * rows).reshape(-1, KW)
    own_tokens = lax.dynamic_slice_in_dim(
        atom_token, row * row_atoms + col * atom_rows, atom_rows
    )
    own_tokens = (own_tokens - row * rows)[None, :]

    flip = ((col == 2 * row + 1) | (col == 2 * row + 2)).astype(jnp.int32)
    here = col // 2 == row
    place = jnp.stack([row, col, jnp.int32(row_count), flip, here.astype(jnp.int32)])
    center = jnp.asarray((np.eye(CZ) - 1.0 / CZ).astype(bf16))
    weights = (pair_up, pair_down, bias_heads.T, center)
    token_bias, band = pair_rows(place, pair_tensor, weights, (), 0, PART, 2, True)
    own_atoms, halo, band, token_bias = lax.optimization_barrier(
        (atom_single, halo, band, token_bias)
    )

    ring = chips // 2
    flat = lambda k, step: k // ring * ring + (k + step) % ring
    across = lambda k: (k + ring) % chips
    over_y = [
        (at(r, r, core), at(r, across(r), core)) for r in range(row_count) for core in range(2)
    ]
    beside = lambda to: [(at(r, r - 1, 1), at(r, to(r), 0)) for r in range(1, row_count)] + [
        (at(r, r + 1, 0), at(r, to(r), 1)) for r in range(row_count - 1)
    ]
    arrived = [
        lax.ppermute(band, both, over_y + beside(lambda r: r)),
        lax.ppermute(band, both, beside(across)),
    ]
    cores = [[at(0, k, core) for k in range(chips)] for core in range(2)]
    own_part = jnp.concatenate([own_atoms, halo], axis=0)
    own_part = jnp.broadcast_to(own_part[None], (chips,) + own_part.shape)
    shards = lax.all_to_all(own_part, "col", 0, 0, axis_index_groups=cores)
    swap = [(i, i ^ 1) for i in range(col_count)]
    arrived = lax.optimization_barrier(arrived)
    band = jnp.where(here, band, jnp.zeros_like(band)) + arrived[0] + arrived[1]
    band, token_bias = lax.optimization_barrier((band, token_bias))
    sent = [
        lax.ppermute(
            band,
            both,
            [
                (at(r, k, core), at(r, flat(k, step), core))
                for r in range(row_count)
                for k in (r, across(r))
                for core in range(2)
            ],
        )
        for step in range(1, ring)
    ]
    (token_bias,) = pair_rows(
        place, pair_tensor, weights, (token_bias,), 2 * PART, rows - 2 * PART, 1, False
    )
    theirs = lax.ppermute(shards, "col", swap)
    gain = token_gain.reshape(-1, KW)
    theirs, token_bias = lax.optimization_barrier((theirs, token_bias))
    head_bias = lax.all_to_all(token_bias, "col", 0, 0)
    sent, theirs, gain, ext_tokens = lax.optimization_barrier((sent, theirs, gain, ext_tokens))
    band = band + sent[0] + sent[1] + sent[2]
    other = lax.ppermute(band, "col", swap)

    atom_mid, token_mid, state, keyvals = atom_attention(
        place,
        (band, other),
        (shards, theirs),
        ext_tokens,
        atom_gain[None],
        atom_proj,
        atom_exit,
        atom_pool,
        token_single,
        gain,
        token_proj,
        row_count,
    )
    keyvals, head_bias = lax.optimization_barrier((keyvals, head_bias))
    keyvals = lax.all_to_all(keyvals, "row", 0, 0)
    gated = token_attention(place, state, keyvals, head_bias, chain_index[None], chain_bias)
    gated = lax.all_to_all(gated, "col", 0, 0).reshape(CS, rows)
    return tuple(
        updates(
            place, gated, token_exit, token_mid, token_back, atom_mid, own_tokens, atom_rows
        )
    )


def solution(mesh):
    placed = (
        P("row", "col", None),
        P("row", None),
        P(("row", "col"), None),
    ) + (P(),) * 14
    return jax.shard_map(
        local,
        mesh=mesh,
        in_specs=placed,
        out_specs=(P("row", None), P(("row", "col"), None)),
        check_vma=False,
    )
```

```python
import functools

import jax
import jax.numpy as jnp
import numpy as np
from jax import lax
from jax.experimental import pallas as pl
from jax.experimental.pallas import tpu as pltpu
from jax.sharding import PartitionSpec as P

CZ = 128
CS = 768
CA = 128
HT = 16
HA = 4
PH = 256
QB = 32
KW = 128
HDA = 32
HDT = 48
HB = 20
HALO = 64
PART = 112
REACH = 208
GROUP = 1024
EPS = 1e-05
GRANT = 60 * 2**20

bf16 = jnp.bfloat16
f32 = jnp.float32


def dot(left, right):
    return jnp.dot(left, right, preferred_element_type=f32)


def dot_nt(left, right):
    return lax.dot_general(left, right, (((1,), (1,)), ((), ())), preferred_element_type=f32)


def dot_tn(left, right):
    return lax.dot_general(left, right, (((0,), (0,)), ((), ())), preferred_element_type=f32)


def centered(features):
    return features - jnp.mean(features, axis=-1, keepdims=True)


def scaled(center):
    spread = jnp.mean(center * center, axis=-1, keepdims=True)
    return center * lax.rsqrt(spread + EPS)


def sigmoid(value):
    return 0.5 + 0.5 * jnp.tanh(0.5 * value)


SMEM = pl.BlockSpec(memory_space=pltpu.SMEM)
ANY = pl.BlockSpec(memory_space=pl.ANY)
HBM = pl.BlockSpec(memory_space=pltpu.HBM)
VMEM = pl.BlockSpec(memory_space=pltpu.VMEM)


def full(array):
    return pl.BlockSpec(array.shape, lambda *_: (0,) * len(array.shape))


def held(arrays):
    return [pltpu.VMEM(a.shape, a.dtype) for a in arrays] + [
        pltpu.SemaphoreType.DMA((len(arrays),))
    ]


def fetch(sources, targets, sems):
    copies = [
        pltpu.make_async_copy(source, target, sems.at[i])
        for i, (source, target) in enumerate(zip(sources, targets))
    ]
    for copy in copies:
        copy.start()
    return copies


def pair_body(place, pair_ref, up_ref, down_ref, heads_ref, center_ref, *refs, bands):
    padded = refs[-1]
    outs = refs[-4:-1] if bands else refs[-2:-1]
    pair_part = pair_ref[...].reshape(-1, CZ)
    normed = scaled(dot(pair_part, center_ref[...])).astype(bf16)
    gate = dot(normed, up_ref[:, :PH] * bf16(0.5))
    value = dot(normed, up_ref[:, PH:])
    hidden = ((gate + gate * jnp.tanh(gate)) * value).astype(bf16)
    updated = pair_part.astype(f32) + dot(hidden, down_ref[...])
    normed_two = scaled(centered(updated)).astype(bf16)
    padded[...] = jnp.zeros_like(padded)
    padded[:HB, :] = heads_ref[...].astype(f32)
    biases = dot_nt(padded[...].astype(bf16), normed_two)
    rows = pair_ref.shape[0]
    stacked = jnp.stack([biases[:, i * CZ : (i + 1) * CZ] for i in range(rows)], axis=0)
    stacked = jnp.swapaxes(stacked, 0, 1)
    outs[0][...] = stacked[HA:HB].astype(bf16)
    if bands:
        outs[1][...] = stacked[:HA].astype(bf16)

        @pl.when(pl.program_id(0) == 0)
        def _():
            edge = jnp.where(place[3] == 1, stacked[:HA, rows - HALO :], stacked[:HA, :HALO])
            edge = pltpu.roll(edge.reshape(HA * HALO, CZ), HALO, 1)
            outs[2][...] = edge.reshape(HA, HALO, CZ).astype(bf16)


def pair_rows(place, pair, weights, before, first, size, count, bands):
    rows, cols = pair.shape[:2]

    def start(i, place):
        at = first + i * size
        return pl.multiple_of(at + place[3] * (rows - 2 * at - size), 16)

    in_specs = [
        pl.BlockSpec(
            (pl.Element(size), pl.Element(cols), pl.Element(CZ)),
            lambda i, place: (start(i, place), 0, 0),
        )
    ]
    in_specs += [full(array) for array in weights]
    out_shape = [jax.ShapeDtypeStruct((HT, rows, cols), bf16)]
    out_specs = [
        pl.BlockSpec(
            (pl.Element(HT), pl.Element(size), pl.Element(cols)),
            lambda i, place: (0, start(i, place), 0),
        )
    ]
    if bands:
        out_shape.append(jax.ShapeDtypeStruct((HA, size * count, cols), bf16))
        out_specs.append(
            pl.BlockSpec(
                (HA, size, cols),
                lambda i, place: (0, i + place[3] * (count - 1 - 2 * i), 0),
            )
        )
        out_shape.append(jax.ShapeDtypeStruct((HA, HALO, cols), bf16))
        out_specs.append(full(out_shape[-1]))
    aliases = {}
    if before:
        aliases = {2 + len(weights): 0}
        in_specs += [ANY]
    cells = size * count * cols
    return pl.pallas_call(
        functools.partial(pair_body, bands=bands),
        grid_spec=pltpu.PrefetchScalarGridSpec(
            num_scalar_prefetch=1,
            grid=(count,),
            in_specs=in_specs,
            out_specs=out_specs,
            scratch_shapes=[pltpu.VMEM((32, CZ), f32)],
        ),
        out_shape=out_shape,
        input_output_aliases=aliases,
        compiler_params=pltpu.CompilerParams(vmem_limit_bytes=56 * 2**20),
        cost_estimate=pl.CostEstimate(
            flops=cells * 500000, bytes_accessed=cells * 300, transcendentals=cells * PH
        ),
        name="pair",
    )(place, pair, *weights, *before)


def atoms_body(
    place,
    tokens_ref,
    atom_gain_ref,
    proj_ref,
    exit_ref,
    pool_ref,
    single_ref,
    gain_ref,
    half_ref,
    other_ref,
    mine_hbm,
    theirs_hbm,
    tproj_hbm,
    mid_hbm,
    tmid_hbm,
    state_hbm,
    tkv_hbm,
    bias_ref,
    look_ref,
    sums_ref,
    value_ref,
    ext_ref,
    query_ref,
    gate_ref,
    mine_ref,
    theirs_ref,
    tproj_ref,
    sems,
    mid_ref,
    tmid_ref,
    state_ref,
    tkv_ref,
    out_sems,
):
    copies = fetch(
        (mine_hbm, theirs_hbm, tproj_hbm), (mine_ref, theirs_ref, tproj_ref), sems
    )
    row, col, row_count = place[0], place[1], place[2]
    total = look_ref.shape[0]
    atoms = query_ref.shape[0]
    rows = single_ref.shape[0]
    chips = mine_ref.shape[0]
    per = atoms // (2 * chips)
    even = lax.rem(col, 2) == 0
    copies[0].wait()
    copies[1].wait()
    rest = jnp.zeros((rows - REACH, KW), bf16)
    middle = jnp.zeros((rows - 2 * HALO, KW), bf16)
    before, after = [], []
    for h in range(HA):
        mine, theirs = half_ref[h], other_ref[h]
        mine, theirs = jnp.where(even, mine, theirs), jnp.where(even, theirs, mine)
        before.append(mine[REACH:])
        after.append(theirs[REACH:])
        base = h * 3 * KW
        bias_ref[:, base : base + KW] = jnp.concatenate([mine[:REACH], rest], axis=0)
        bias_ref[:, base + KW : base + 2 * KW] = jnp.concatenate([rest, theirs[:REACH]], axis=0)
        bias_ref[:, base + 2 * KW : base + 3 * KW] = jnp.concatenate(
            [mine[REACH - HALO : REACH], middle, theirs[:HALO]], axis=0
        )
    ext_ref[:HALO] = jnp.concatenate(before, axis=0)
    ext_ref[HALO + atoms :] = jnp.concatenate(after, axis=0)
    for k in range(chips):
        mine, theirs = mine_ref[k], theirs_ref[k]
        at = HALO + 2 * k * per
        ext_ref[at : at + per] = jnp.where(even, mine, theirs)
        ext_ref[at + per : at + 2 * per] = jnp.where(even, theirs, mine)
    normed = (scaled(centered(ext_ref[...].astype(f32))) * atom_gain_ref[...]).astype(bf16)
    own = normed[HALO : HALO + atoms]
    query_ref[...] = (dot(own, proj_ref[:, :CA]) * HDA ** (-0.5)).astype(bf16)
    look_ref[:, :CA] = dot(normed, proj_ref[:, CA : 2 * CA]).astype(bf16)
    value_ref[...] = dot(normed, proj_ref[:, 2 * CA : 3 * CA]).astype(bf16)
    gate_ref[...] = sigmoid(dot(own, proj_ref[:, 3 * CA :]))
    lane = lax.broadcasted_iota(jnp.int32, (KW, 3 * KW), 1)
    for t in range(total // KW):
        at = slice(t * KW, (t + 1) * KW)
        tokens = jnp.broadcast_to(tokens_ref[t : t + 1, :], (KW, KW)).astype(f32).T.astype(jnp.int32)
        tokens = jnp.concatenate([tokens] * 3, axis=1)
        tokens = jnp.where(
            tokens < 0,
            tokens + 2 * KW + HALO,
            jnp.where(tokens < 2 * KW, tokens, tokens + HALO),
        )
        look_ref[at, CA:] = (tokens == lane).astype(f32).astype(bf16)
    head_of = lax.broadcasted_iota(jnp.int32, (QB, CA), 1) // HDA
    sums_ref[...] = jnp.zeros_like(sums_ref)
    row_lane = lax.broadcasted_iota(jnp.int32, (1, KW), 1)

    def group(g, counts):
        start = pl.multiple_of(g * GROUP, GROUP)
        own = pl.ds(start, GROUP)
        onehot = look_ref[pl.ds(pl.multiple_of(start + HALO, HALO), GROUP), CA : CA + 2 * KW]
        picked = dot(onehot, bias_ref[...]).astype(bf16)
        queries = query_ref[own, :]
        scores = []
        for b in range(GROUP // QB):
            part = slice(b * QB, (b + 1) * QB)
            left = jnp.concatenate(
                [
                    jnp.concatenate(
                        [
                            jnp.where(head_of == h, queries[part].astype(f32), 0.0).astype(bf16),
                            picked[part, h * 3 * KW : (h + 1) * 3 * KW],
                        ],
                        axis=1,
                    )
                    for h in range(HA)
                ],
                axis=0,
            )
            first = start + b * QB + HALO - (KW - QB) // 2
            window = look_ref[pl.ds(pl.multiple_of(first, 16), KW), :]
            at = row_lane + first
            inside = ((at >= HALO) | (row > 0)) & ((at < total - HALO) | (row < row_count - 1))
            scores.append(dot_nt(left, window) + jnp.where(inside, 0.0, -1e30))
        scores = jnp.concatenate(scores, axis=0)
        exps = jnp.exp(scores - jnp.max(scores, axis=-1, keepdims=True))
        inverse = 1.0 / jnp.sum(exps, axis=-1, keepdims=True)
        weights = exps.astype(bf16)
        attended = []
        for b in range(GROUP // QB):
            first = start + b * QB + HALO - (KW - QB) // 2
            part = slice(b * HA * QB, (b + 1) * HA * QB)
            out = dot(weights[part], value_ref[pl.ds(pl.multiple_of(first, 16), KW), :])
            out = out * inverse[part]
            merged = out[:QB]
            for h in range(1, HA):
                merged = jnp.where(head_of == h, out[h * QB : (h + 1) * QB], merged)
            attended.append(merged)
        attended = jnp.concatenate(attended, axis=0)
        gated = (attended * gate_ref[own, :]).astype(bf16)
        single = ext_ref[pl.ds(pl.multiple_of(start + HALO, HALO), GROUP), :].astype(f32)
        mid = (single + dot(gated, exit_ref[...])).astype(bf16)
        mid_ref[own, :] = mid
        pooled = jnp.maximum(dot(mid, pool_ref[...]), 0.0).astype(bf16)
        sums_ref[...] += dot_tn(onehot, pooled)
        return counts + jnp.sum(onehot.astype(f32).T, axis=1, keepdims=True)

    counts = lax.fori_loop(0, atoms // GROUP, group, jnp.zeros((rows, 1), f32), unroll=True)
    token_mid = (single_ref[...].astype(f32) + sums_ref[...] / counts).astype(bf16)
    tmid_ref[...] = token_mid
    stores = fetch((mid_ref, tmid_ref), (mid_hbm, tmid_hbm), out_sems)
    gain = jnp.concatenate([gain_ref[k : k + 1, :] for k in range(gain_ref.shape[0])], axis=1)
    normed = (scaled(centered(token_mid.astype(f32))) * gain).astype(bf16)

    copies[-1].wait()

    def head_part(part):
        start = part * CS + col * HDT
        base = jnp.minimum(start // KW * KW, 4 * CS - 2 * KW)
        base = pl.multiple_of(base, KW)
        wide = dot(normed, tproj_ref[:, pl.ds(base, 2 * KW)])
        return pltpu.roll(wide, lax.rem(2 * KW - (start - base), 2 * KW), 1)[:, :KW]

    state_ref[...] = jnp.concatenate([head_part(0), sigmoid(head_part(1))], axis=1)
    keyvals = jnp.concatenate([head_part(2).T[:HDT], head_part(3).T[:HDT]], axis=0)
    tkv_ref[...] = keyvals.astype(bf16)
    last = [(state_ref, state_hbm)] + [(tkv_ref, tkv_hbm.at[k]) for k in range(tkv_hbm.shape[0])]
    for i, (source, target) in enumerate(last):
        stores.append(pltpu.make_async_copy(source, target, out_sems.at[2 + i]))
        stores[-1].start()
    for copy in stores:
        copy.wait()


def atom_attention(
    place, bands, shards, tokens, atom_gain, proj, exit_w, pool, single, gain, tproj, copies
):
    total = tokens.size
    atoms = total - 2 * HALO
    rows = single.shape[0]
    operands = (tokens, atom_gain, proj, exit_w, pool, single, gain)
    fetched = (*shards, tproj)
    out_shape = [
        jax.ShapeDtypeStruct((atoms, CA), bf16),
        jax.ShapeDtypeStruct((rows, CS), bf16),
        jax.ShapeDtypeStruct((rows, 2 * KW), f32),
        jax.ShapeDtypeStruct((copies, 2 * HDT, rows), bf16),
    ]
    return pl.pallas_call(
        atoms_body,
        grid=(1,),
        in_specs=[SMEM]
        + [full(array) for array in operands]
        + [VMEM] * len(bands)
        + [HBM] * len(fetched),
        out_specs=[HBM] * len(out_shape),
        out_shape=out_shape,
        scratch_shapes=[
            pltpu.VMEM((rows, HA * 3 * KW), bf16),
            pltpu.VMEM((total, CA + 3 * KW), bf16),
            pltpu.VMEM((rows, CS), f32),
            pltpu.VMEM((total, CA), bf16),
            pltpu.VMEM((total, CA), bf16),
            pltpu.VMEM((atoms, CA), bf16),
            pltpu.VMEM((atoms, CA), f32),
        ]
        + held(fetched)
        + [pltpu.VMEM(a.shape, a.dtype) for a in out_shape[:3]]
        + [pltpu.VMEM((2 * HDT, rows), bf16), pltpu.SemaphoreType.DMA((3 + copies,))],
        compiler_params=pltpu.CompilerParams(vmem_limit_bytes=GRANT),
        cost_estimate=pl.CostEstimate(
            flops=10**10, bytes_accessed=2**24, transcendentals=2**22
        ),
        name="atoms",
    )(place, *operands, *bands, *fetched)


def tokens_body(
    place, strength, chain_ref, state_hbm, kv_hbm, bias_hbm, out_ref, state_ref, kv_ref, bias_ref, sems
):
    per = state_hbm.shape[0] // bias_hbm.shape[2]
    groups = kv_hbm.shape[0]
    bias_parts = [pl.ds(r * per, per) for r in range(groups)]
    copies = fetch(
        [state_hbm, kv_hbm] + [bias_hbm.at[part] for part in bias_parts],
        [state_ref, kv_ref] + [bias_ref.at[part] for part in bias_parts],
        sems,
    )
    col = place[1]
    rows = state_ref.shape[0]
    own = pl.multiple_of(place[0] * rows, rows)
    mine = chain_ref[:, pl.ds(own, rows)].astype(f32)
    mine = jnp.broadcast_to(mine, (KW, rows)).T
    mine = jnp.concatenate([mine] * (rows // KW), axis=1).astype(jnp.int32)
    copies[0].wait()
    copies[1].wait()
    query = state_ref[:, :HDT].astype(bf16)
    strong = strength[col]
    raws = [dot(query, kv_ref[r, :HDT, :]) * HDT ** (-0.5) for r in range(groups)]
    scores = []
    for r, raw in enumerate(raws):
        copies[2 + r].wait()
        bias = jnp.concatenate([bias_ref[r * per + k].astype(f32) for k in range(per)], axis=1)
        same = mine == chain_ref[:, r * rows : (r + 1) * rows]
        scores.append(raw + bias + jnp.where(same, strong, 0.0))
    top = scores[0]
    for part in scores[1:]:
        top = jnp.maximum(top, part)
    top = jnp.max(top, axis=-1, keepdims=True)
    exps = [jnp.exp(part - top) for part in scores]
    total = exps[0]
    for part in exps[1:]:
        total = total + part
    total = jnp.sum(total, axis=-1, keepdims=True)
    out = jnp.zeros((rows, HDT), f32)
    for r in range(kv_ref.shape[0]):
        out = out + dot_nt(exps[r].astype(bf16), kv_ref[r, HDT:, :])
    gated = out / total * state_ref[:, KW : KW + HDT]
    wide = jnp.concatenate([gated, jnp.zeros((rows, KW - HDT), f32)], axis=1)
    gated = wide.T[:HDT].astype(bf16)
    for k in range(out_ref.shape[0]):
        out_ref[k] = gated


def token_attention(place, state, kv, bias, chain, strength):
    rows = state.shape[0]
    out_shape = jax.ShapeDtypeStruct((bias.shape[0] // 2, HDT, rows), bf16)
    return pl.pallas_call(
        tokens_body,
        grid=(1,),
        in_specs=[SMEM] * 2 + [full(chain)] + [HBM] * 3,
        out_specs=full(out_shape),
        out_shape=out_shape,
        scratch_shapes=held((state, kv, bias))[:-1]
        + [pltpu.SemaphoreType.DMA((2 + kv.shape[0],))],
        compiler_params=pltpu.CompilerParams(vmem_limit_bytes=GRANT),
        cost_estimate=pl.CostEstimate(flops=10**9, bytes_accessed=2**22, transcendentals=2**19),
        name="tokens",
    )(place, strength, chain, state, kv, bias)


def update_body(
    place,
    tokens_ref,
    mine_ref,
    theirs_ref,
    exit_ref,
    tmid_ref,
    back_ref,
    mid_ref,
    tout_ref,
    aout_ref,
    gated_ref,
):
    even = lax.rem(place[1], 2) == 0
    for k in range(mine_ref.shape[0]):
        mine, theirs = mine_ref[k], theirs_ref[k]
        first = slice(2 * k * HDT, (2 * k + 1) * HDT)
        second = slice((2 * k + 1) * HDT, (2 * k + 2) * HDT)
        gated_ref[first, :] = jnp.where(even, mine, theirs)
        gated_ref[second, :] = jnp.where(even, theirs, mine)
    col = place[1]
    atoms, rows = aout_ref.shape[0], tmid_ref.shape[0]
    at = pl.multiple_of(col * atoms, atoms)
    added = dot_tn(gated_ref[...], exit_ref[...])
    update = (tmid_ref[...].astype(f32) + added).astype(bf16)
    tout_ref[...] = update
    sent = dot(update, back_ref[...]).astype(bf16)
    own = tokens_ref[...]
    onehot = (lax.broadcasted_iota(jnp.int32, (rows, atoms), 0) == own).astype(f32).astype(bf16)
    aout_ref[...] = (mid_ref[pl.ds(at, atoms), :].astype(f32) + dot_tn(onehot, sent)).astype(bf16)


def updates(place, gated, exit_w, tmid, back, mid, tokens, atoms):
    rows = tmid.shape[0]
    out_shape = [
        jax.ShapeDtypeStruct((rows, CS), bf16),
        jax.ShapeDtypeStruct((atoms, CA), bf16),
    ]
    return pl.pallas_call(
        update_body,
        grid=(1,),
        in_specs=[SMEM] + [VMEM] * 7,
        out_specs=[full(shape) for shape in out_shape],
        out_shape=out_shape,
        scratch_shapes=[pltpu.VMEM((CS, rows), bf16)],
        compiler_params=pltpu.CompilerParams(vmem_limit_bytes=16 * 2**20),
        name="updates",
    )(place, tokens, *gated, exit_w, tmid, back, mid)


def local(
    pair_tensor,
    token_single,
    atom_single,
    atom_token,
    chain_index,
    pair_up,
    pair_down,
    bias_heads,
    atom_gain,
    atom_proj,
    atom_exit,
    atom_pool,
    token_gain,
    token_proj,
    token_exit,
    chain_bias,
    token_back,
):
    rows, cols = pair_tensor.shape[:2]
    atom_rows = atom_single.shape[0]
    row_count = lax.axis_size("row")
    col_count = lax.axis_size("col")
    row = lax.axis_index("row")
    col = lax.axis_index("col")
    chips = col_count // 2
    row_atoms = atom_rows * col_count

    both = ("row", "col")
    at = lambda r, k, core: r * col_count + 2 * k + core
    last = col_count - 1

    last = col_count - 1
    halo = lax.ppermute(
        jnp.where(col == last, atom_single[-HALO:], atom_single[:HALO]),
        both,
        [(r * col_count + last, at(r + 1, r + 1, 0)) for r in range(row_count - 1)]
        + [((r + 1) * col_count, at(r, r, 1)) for r in range(row_count - 1)],
    )
    ext_tokens = lax.dynamic_slice_in_dim(
        jnp.pad(atom_token, (HALO, HALO)), row * row_atoms, row_atoms + 2 * HALO
    )
    ext_tokens = (ext_tokens - row * rows).reshape(-1, KW)
    own_tokens = lax.dynamic_slice_in_dim(
        atom_token, row * row_atoms + col * atom_rows, atom_rows
    )
    own_tokens = (own_tokens - row * rows)[None, :]

    flip = ((col == 2 * row + 1) | (col == 2 * row + 2)).astype(jnp.int32)
    place = jnp.stack([row, col, jnp.int32(row_count), flip]).astype(jnp.int32)
    center = jnp.asarray((np.eye(CZ) - 1.0 / CZ).astype(bf16))
    weights = (pair_up, pair_down, bias_heads.T, center)
    token_bias, band, edge = pair_rows(place, pair_tensor, weights, (), 0, PART, 2, True)
    halo, band, edge, token_bias, own_atoms = lax.optimization_barrier(
        (halo, band, edge, token_bias, atom_single)
    )

    here = col // 2 == row
    even = col % 2 == 0
    ring = chips // 2
    flat = lambda k, step: k // ring * ring + (k + step) % ring
    across = lambda k: (k + ring) % chips
    split = REACH - HALO
    band = jnp.where(even, band[:, :REACH], band[:, 2 * PART - REACH :])
    band = jnp.concatenate([band, halo.reshape(HA, HALO // HA, CA)], axis=1)
    none = jnp.zeros_like(band)
    place_in = lax.broadcasted_iota(jnp.int32, band.shape, 1)
    lane = lax.broadcasted_iota(jnp.int32, band.shape, 2)
    late = (place_in >= split) & (place_in < REACH) & (lane < HALO)
    early = (place_in < HALO) & (lane >= HALO)
    late_edge = jnp.concatenate([none[:, :split], edge, none[:, REACH:]], axis=1)
    early_edge = jnp.concatenate([edge, none[:, HALO:]], axis=1)
    band = jnp.where(jnp.where(even, late, early), none, band)
    edge = jnp.where(
        even, jnp.where(early, early_edge, none), jnp.where(late, late_edge, none)
    )
    band = jnp.where(here, band, edge)
    over_y = [
        (at(r, r, core), at(r, across(r), core)) for r in range(row_count) for core in range(2)
    ]
    beside = lambda to: [(at(r, r - 1, 1), at(r, to(r), 0)) for r in range(1, row_count)] + [
        (at(r, r + 1, 0), at(r, to(r), 1)) for r in range(row_count - 1)
    ]
    arrived = [
        lax.ppermute(band, both, over_y + beside(lambda r: r)),
        lax.ppermute(band, both, beside(across)),
    ]
    cores = [[at(0, k, core) for k in range(chips)] for core in range(2)]
    own_atoms = jnp.broadcast_to(own_atoms[None], (chips,) + own_atoms.shape)
    shards = lax.all_to_all(own_atoms, "col", 0, 0, axis_index_groups=cores)
    swap = [(i, i ^ 1) for i in range(col_count)]
    arrived = lax.optimization_barrier(arrived)
    band = jnp.where(here, band, none) + arrived[0] + arrived[1]
    band, token_bias = lax.optimization_barrier((band, token_bias))
    sent = [
        lax.ppermute(
            band,
            both,
            [
                (at(r, k, core), at(r, flat(k, step), core))
                for r in range(row_count)
                for k in (r, across(r))
                for core in range(2)
            ],
        )
        for step in range(1, ring)
    ]
    (token_bias,) = pair_rows(
        place, pair_tensor, weights, (token_bias,), 2 * PART, rows - 2 * PART, 1, False
    )
    theirs = lax.ppermute(shards, "col", swap)
    gain = token_gain.reshape(-1, KW)
    theirs, token_bias = lax.optimization_barrier((theirs, token_bias))
    head_bias = lax.all_to_all(token_bias, "col", 0, 0)
    sent, theirs, gain, ext_tokens = lax.optimization_barrier((sent, theirs, gain, ext_tokens))
    band = band + sent[0] + sent[1] + sent[2]
    other = lax.ppermute(band, "col", swap)

    atom_mid, token_mid, state, keyvals = atom_attention(
        place,
        (band, other),
        (shards, theirs),
        ext_tokens,
        atom_gain[None],
        atom_proj,
        atom_exit,
        atom_pool,
        token_single,
        gain,
        token_proj,
        row_count,
    )
    keyvals, head_bias = lax.optimization_barrier((keyvals, head_bias))
    keyvals = lax.all_to_all(keyvals, "row", 0, 0)
    gated = token_attention(place, state, keyvals, head_bias, chain_index[None], chain_bias)
    gated = lax.all_to_all(gated, "col", 0, 0, axis_index_groups=cores)
    gated = (gated, lax.ppermute(gated, "col", swap))
    return tuple(
        updates(
            place, gated, token_exit, token_mid, token_back, atom_mid, own_tokens, atom_rows
        )
    )


def solution(mesh):
    placed = (
        P("row", "col", None),
        P("row", None),
        P(("row", "col"), None),
    ) + (P(),) * 14
    return jax.shard_map(
        local,
        mesh=mesh,
        in_specs=placed,
        out_specs=(P("row", None), P(("row", "col"), None)),
        check_vma=False,
    )
```

```python
import functools

import jax
import jax.numpy as jnp
import numpy as np
from jax import lax
from jax.experimental import pallas as pl
from jax.experimental.pallas import tpu as pltpu
from jax.sharding import PartitionSpec as P

CZ = 128
CS = 768
CA = 128
HT = 16
HA = 4
PH = 256
QB = 32
KW = 128
HDA = 32
HDT = 48
HB = 20
HALO = 64
PART = 112
REACH = 208
GROUP = 1024
EPS = 1e-05
GRANT = 60 * 2**20

bf16 = jnp.bfloat16
f32 = jnp.float32


def dot(left, right):
    return jnp.dot(left, right, preferred_element_type=f32)


def dot_nt(left, right):
    return lax.dot_general(left, right, (((1,), (1,)), ((), ())), preferred_element_type=f32)


def dot_tn(left, right):
    return lax.dot_general(left, right, (((0,), (0,)), ((), ())), preferred_element_type=f32)


def centered(features):
    return features - jnp.mean(features, axis=-1, keepdims=True)


def scaled(center):
    spread = jnp.mean(center * center, axis=-1, keepdims=True)
    return center * lax.rsqrt(spread + EPS)


def sigmoid(value):
    return 0.5 + 0.5 * jnp.tanh(0.5 * value)


SMEM = pl.BlockSpec(memory_space=pltpu.SMEM)
ANY = pl.BlockSpec(memory_space=pl.ANY)
HBM = pl.BlockSpec(memory_space=pltpu.HBM)
VMEM = pl.BlockSpec(memory_space=pltpu.VMEM)


def full(array):
    return pl.BlockSpec(array.shape, lambda *_: (0,) * len(array.shape))


def held(arrays):
    return [pltpu.VMEM(a.shape, a.dtype) for a in arrays] + [
        pltpu.SemaphoreType.DMA((len(arrays),))
    ]


def fetch(sources, targets, sems):
    copies = [
        pltpu.make_async_copy(source, target, sems.at[i])
        for i, (source, target) in enumerate(zip(sources, targets))
    ]
    for copy in copies:
        copy.start()
    return copies


def pair_body(place, pair_ref, up_ref, down_ref, heads_ref, center_ref, *refs, bands):
    padded = refs[-1]
    outs = refs[-4:-1] if bands else refs[-2:-1]
    pair_part = pair_ref[...].reshape(-1, CZ)
    normed = scaled(dot(pair_part, center_ref[...])).astype(bf16)
    gate = dot(normed, up_ref[:, :PH] * bf16(0.5))
    value = dot(normed, up_ref[:, PH:])
    hidden = ((gate + gate * jnp.tanh(gate)) * value).astype(bf16)
    updated = pair_part.astype(f32) + dot(hidden, down_ref[...])
    normed_two = scaled(centered(updated)).astype(bf16)
    padded[...] = jnp.zeros_like(padded)
    padded[:HB, :] = heads_ref[...].astype(f32)
    biases = dot_nt(padded[...].astype(bf16), normed_two)
    rows = pair_ref.shape[0]
    stacked = jnp.stack([biases[:, i * CZ : (i + 1) * CZ] for i in range(rows)], axis=0)
    stacked = jnp.swapaxes(stacked, 0, 1)
    outs[0][...] = stacked[HA:HB].astype(bf16)
    if bands:
        outs[1][...] = stacked[:HA].astype(bf16)

        @pl.when(pl.program_id(0) == 0)
        def _():
            edge = jnp.where(place[3] == 1, stacked[:HA, rows - HALO :], stacked[:HA, :HALO])
            edge = pltpu.roll(edge.reshape(HA * HALO, CZ), HALO, 1)
            outs[2][...] = edge.reshape(HA, HALO, CZ).astype(bf16)


def pair_rows(place, pair, weights, before, first, size, count, bands):
    rows, cols = pair.shape[:2]

    def start(i, place):
        at = first + i * size
        return pl.multiple_of(at + place[3] * (rows - 2 * at - size), 16)

    in_specs = [
        pl.BlockSpec(
            (pl.Element(size), pl.Element(cols), pl.Element(CZ)),
            lambda i, place: (start(i, place), 0, 0),
        )
    ]
    in_specs += [full(array) for array in weights]
    out_shape = [jax.ShapeDtypeStruct((HT, rows, cols), bf16)]
    out_specs = [
        pl.BlockSpec(
            (pl.Element(HT), pl.Element(size), pl.Element(cols)),
            lambda i, place: (0, start(i, place), 0),
        )
    ]
    if bands:
        out_shape.append(jax.ShapeDtypeStruct((HA, size * count, cols), bf16))
        out_specs.append(
            pl.BlockSpec(
                (HA, size, cols),
                lambda i, place: (0, i + place[3] * (count - 1 - 2 * i), 0),
            )
        )
        out_shape.append(jax.ShapeDtypeStruct((HA, HALO, cols), bf16))
        out_specs.append(full(out_shape[-1]))
    aliases = {}
    if before:
        aliases = {2 + len(weights): 0}
        in_specs += [ANY]
    cells = size * count * cols
    return pl.pallas_call(
        functools.partial(pair_body, bands=bands),
        grid_spec=pltpu.PrefetchScalarGridSpec(
            num_scalar_prefetch=1,
            grid=(count,),
            in_specs=in_specs,
            out_specs=out_specs,
            scratch_shapes=[pltpu.VMEM((32, CZ), f32)],
        ),
        out_shape=out_shape,
        input_output_aliases=aliases,
        compiler_params=pltpu.CompilerParams(vmem_limit_bytes=56 * 2**20),
        cost_estimate=pl.CostEstimate(
            flops=cells * 500000, bytes_accessed=cells * 300, transcendentals=cells * PH
        ),
        name="pair",
    )(place, pair, *weights, *before)


def atoms_body(
    place,
    tokens_ref,
    atom_gain_ref,
    proj_ref,
    exit_ref,
    pool_ref,
    single_ref,
    gain_ref,
    half_ref,
    other_ref,
    mine_hbm,
    theirs_hbm,
    tproj_hbm,
    mid_hbm,
    tmid_hbm,
    state_hbm,
    tkv_hbm,
    bias_ref,
    look_ref,
    sums_ref,
    value_ref,
    ext_ref,
    query_ref,
    gate_ref,
    mine_ref,
    theirs_ref,
    tproj_ref,
    sems,
    mid_ref,
    tmid_ref,
    state_ref,
    tkv_ref,
    out_sems,
):
    copies = fetch(
        (mine_hbm, theirs_hbm, tproj_hbm), (mine_ref, theirs_ref, tproj_ref), sems
    )
    row, col, row_count = place[0], place[1], place[2]
    total = look_ref.shape[0]
    atoms = query_ref.shape[0]
    rows = single_ref.shape[0]
    chips = mine_ref.shape[0]
    per = atoms // (2 * chips)
    even = lax.rem(col, 2) == 0
    copies[0].wait()
    copies[1].wait()
    rest = jnp.zeros((rows - REACH, KW), bf16)
    middle = jnp.zeros((rows - 2 * HALO, KW), bf16)
    before, after = [], []
    for h in range(HA):
        mine, theirs = half_ref[h], other_ref[h]
        mine, theirs = jnp.where(even, mine, theirs), jnp.where(even, theirs, mine)
        before.append(mine[REACH:])
        after.append(theirs[REACH:])
        base = h * 3 * KW
        bias_ref[:, base : base + KW] = jnp.concatenate([mine[:REACH], rest], axis=0)
        bias_ref[:, base + KW : base + 2 * KW] = jnp.concatenate([rest, theirs[:REACH]], axis=0)
        bias_ref[:, base + 2 * KW : base + 3 * KW] = jnp.concatenate(
            [mine[REACH - HALO : REACH], middle, theirs[:HALO]], axis=0
        )
    ext_ref[:HALO] = jnp.concatenate(before, axis=0)
    ext_ref[HALO + atoms :] = jnp.concatenate(after, axis=0)
    for k in range(chips):
        mine, theirs = mine_ref[k], theirs_ref[k]
        at = HALO + 2 * k * per
        ext_ref[at : at + per] = jnp.where(even, mine, theirs)
        ext_ref[at + per : at + 2 * per] = jnp.where(even, theirs, mine)
    normed = (scaled(centered(ext_ref[...].astype(f32))) * atom_gain_ref[...]).astype(bf16)
    own = normed[HALO : HALO + atoms]
    query_ref[...] = (dot(own, proj_ref[:, :CA]) * HDA ** (-0.5)).astype(bf16)
    look_ref[:, :CA] = dot(normed, proj_ref[:, CA : 2 * CA]).astype(bf16)
    value_ref[...] = dot(normed, proj_ref[:, 2 * CA : 3 * CA]).astype(bf16)
    gate_ref[...] = sigmoid(dot(own, proj_ref[:, 3 * CA :]))
    lane = lax.broadcasted_iota(jnp.int32, (KW, 3 * KW), 1)
    for t in range(total // KW):
        at = slice(t * KW, (t + 1) * KW)
        tokens = jnp.broadcast_to(tokens_ref[t : t + 1, :], (KW, KW)).astype(f32).T.astype(jnp.int32)
        tokens = jnp.concatenate([tokens] * 3, axis=1)
        tokens = jnp.where(
            tokens < 0,
            tokens + 2 * KW + HALO,
            jnp.where(tokens < 2 * KW, tokens, tokens + HALO),
        )
        look_ref[at, CA:] = (tokens == lane).astype(f32).astype(bf16)
    head_of = lax.broadcasted_iota(jnp.int32, (QB, CA), 1) // HDA
    sums_ref[...] = jnp.zeros_like(sums_ref)
    row_lane = lax.broadcasted_iota(jnp.int32, (1, KW), 1)

    def group(g, counts):
        start = pl.multiple_of(g * GROUP, GROUP)
        own = pl.ds(start, GROUP)
        onehot = look_ref[pl.ds(pl.multiple_of(start + HALO, HALO), GROUP), CA : CA + 2 * KW]
        picked = dot(onehot, bias_ref[...]).astype(bf16)
        queries = query_ref[own, :]
        scores = []
        for b in range(GROUP // QB):
            part = slice(b * QB, (b + 1) * QB)
            left = jnp.concatenate(
                [
                    jnp.concatenate(
                        [
                            jnp.where(head_of == h, queries[part].astype(f32), 0.0).astype(bf16),
                            picked[part, h * 3 * KW : (h + 1) * 3 * KW],
                        ],
                        axis=1,
                    )
                    for h in range(HA)
                ],
                axis=0,
            )
            first = start + b * QB + HALO - (KW - QB) // 2
            window = look_ref[pl.ds(pl.multiple_of(first, 16), KW), :]
            at = row_lane + first
            inside = ((at >= HALO) | (row > 0)) & ((at < total - HALO) | (row < row_count - 1))
            scores.append(dot_nt(left, window) + jnp.where(inside, 0.0, -1e30))
        scores = jnp.concatenate(scores, axis=0)
        exps = jnp.exp(scores - jnp.max(scores, axis=-1, keepdims=True))
        inverse = 1.0 / jnp.sum(exps, axis=-1, keepdims=True)
        weights = exps.astype(bf16)
        attended = []
        for b in range(GROUP // QB):
            first = start + b * QB + HALO - (KW - QB) // 2
            part = slice(b * HA * QB, (b + 1) * HA * QB)
            out = dot(weights[part], value_ref[pl.ds(pl.multiple_of(first, 16), KW), :])
            out = out * inverse[part]
            merged = out[:QB]
            for h in range(1, HA):
                merged = jnp.where(head_of == h, out[h * QB : (h + 1) * QB], merged)
            attended.append(merged)
        attended = jnp.concatenate(attended, axis=0)
        gated = (attended * gate_ref[own, :]).astype(bf16)
        single = ext_ref[pl.ds(pl.multiple_of(start + HALO, HALO), GROUP), :].astype(f32)
        mid = (single + dot(gated, exit_ref[...])).astype(bf16)
        mid_ref[own, :] = mid
        pooled = jnp.maximum(dot(mid, pool_ref[...]), 0.0).astype(bf16)
        sums_ref[...] += dot_tn(onehot, pooled)
        return counts + jnp.sum(onehot.astype(f32).T, axis=1, keepdims=True)

    counts = lax.fori_loop(0, atoms // GROUP, group, jnp.zeros((rows, 1), f32), unroll=True)
    token_mid = (single_ref[...].astype(f32) + sums_ref[...] / counts).astype(bf16)
    tmid_ref[...] = token_mid
    stores = fetch((mid_ref, tmid_ref), (mid_hbm, tmid_hbm), out_sems)
    gain = jnp.concatenate([gain_ref[k : k + 1, :] for k in range(gain_ref.shape[0])], axis=1)
    normed = (scaled(centered(token_mid.astype(f32))) * gain).astype(bf16)

    copies[-1].wait()

    def head_part(part):
        start = part * CS + col * HDT
        base = jnp.minimum(start // KW * KW, 4 * CS - 2 * KW)
        base = pl.multiple_of(base, KW)
        wide = dot(normed, tproj_ref[:, pl.ds(base, 2 * KW)])
        return pltpu.roll(wide, lax.rem(2 * KW - (start - base), 2 * KW), 1)[:, :KW]

    state_ref[...] = jnp.concatenate([head_part(0), sigmoid(head_part(1))], axis=1)
    keyvals = jnp.concatenate([head_part(2).T[:HDT], head_part(3).T[:HDT]], axis=0)
    tkv_ref[...] = keyvals.astype(bf16)
    last = [(state_ref, state_hbm)] + [(tkv_ref, tkv_hbm.at[k]) for k in range(tkv_hbm.shape[0])]
    for i, (source, target) in enumerate(last):
        stores.append(pltpu.make_async_copy(source, target, out_sems.at[2 + i]))
        stores[-1].start()
    for copy in stores:
        copy.wait()


def atom_attention(
    place, bands, shards, tokens, atom_gain, proj, exit_w, pool, single, gain, tproj, copies
):
    total = tokens.size
    atoms = total - 2 * HALO
    rows = single.shape[0]
    operands = (tokens, atom_gain, proj, exit_w, pool, single, gain)
    fetched = (*shards, tproj)
    out_shape = [
        jax.ShapeDtypeStruct((atoms, CA), bf16),
        jax.ShapeDtypeStruct((rows, CS), bf16),
        jax.ShapeDtypeStruct((rows, 2 * KW), f32),
        jax.ShapeDtypeStruct((copies, 2 * HDT, rows), bf16),
    ]
    return pl.pallas_call(
        atoms_body,
        grid=(1,),
        in_specs=[SMEM]
        + [full(array) for array in operands]
        + [VMEM] * len(bands)
        + [HBM] * len(fetched),
        out_specs=[HBM] * len(out_shape),
        out_shape=out_shape,
        scratch_shapes=[
            pltpu.VMEM((rows, HA * 3 * KW), bf16),
            pltpu.VMEM((total, CA + 3 * KW), bf16),
            pltpu.VMEM((rows, CS), f32),
            pltpu.VMEM((total, CA), bf16),
            pltpu.VMEM((total, CA), bf16),
            pltpu.VMEM((atoms, CA), bf16),
            pltpu.VMEM((atoms, CA), f32),
        ]
        + held(fetched)
        + [pltpu.VMEM(a.shape, a.dtype) for a in out_shape[:3]]
        + [pltpu.VMEM((2 * HDT, rows), bf16), pltpu.SemaphoreType.DMA((3 + copies,))],
        compiler_params=pltpu.CompilerParams(vmem_limit_bytes=52 * 2**20),
        cost_estimate=pl.CostEstimate(
            flops=10**10, bytes_accessed=2**24, transcendentals=2**22
        ),
        name="atoms",
    )(place, *operands, *bands, *fetched)


def tokens_body(
    place, strength, chain_ref, state_hbm, kv_hbm, bias_hbm, out_ref, state_ref, kv_ref, bias_ref, sems
):
    per = state_hbm.shape[0] // bias_hbm.shape[2]
    groups = kv_hbm.shape[0]
    bias_parts = [pl.ds(r * per, per) for r in range(groups)]
    copies = fetch(
        [state_hbm, kv_hbm] + [bias_hbm.at[part] for part in bias_parts],
        [state_ref, kv_ref] + [bias_ref.at[part] for part in bias_parts],
        sems,
    )
    col = place[1]
    rows = state_ref.shape[0]
    own = pl.multiple_of(place[0] * rows, rows)
    mine = chain_ref[:, pl.ds(own, rows)].astype(f32)
    mine = jnp.broadcast_to(mine, (KW, rows)).T
    mine = jnp.concatenate([mine] * (rows // KW), axis=1).astype(jnp.int32)
    copies[0].wait()
    copies[1].wait()
    query = state_ref[:, :HDT].astype(bf16)
    strong = strength[col]
    raws = [dot(query, kv_ref[r, :HDT, :]) * HDT ** (-0.5) for r in range(groups)]
    scores = []
    for r, raw in enumerate(raws):
        copies[2 + r].wait()
        bias = jnp.concatenate([bias_ref[r * per + k].astype(f32) for k in range(per)], axis=1)
        same = mine == chain_ref[:, r * rows : (r + 1) * rows]
        scores.append(raw + bias + jnp.where(same, strong, 0.0))
    top = scores[0]
    for part in scores[1:]:
        top = jnp.maximum(top, part)
    top = jnp.max(top, axis=-1, keepdims=True)
    exps = [jnp.exp(part - top) for part in scores]
    total = exps[0]
    for part in exps[1:]:
        total = total + part
    total = jnp.sum(total, axis=-1, keepdims=True)
    out = jnp.zeros((rows, HDT), f32)
    for r in range(kv_ref.shape[0]):
        out = out + dot_nt(exps[r].astype(bf16), kv_ref[r, HDT:, :])
    gated = out / total * state_ref[:, KW : KW + HDT]
    wide = jnp.concatenate([gated, jnp.zeros((rows, KW - HDT), f32)], axis=1)
    gated = wide.T[:HDT].astype(bf16)
    for k in range(out_ref.shape[0]):
        out_ref[k] = gated


def token_attention(place, state, kv, bias, chain, strength):
    rows = state.shape[0]
    out_shape = jax.ShapeDtypeStruct((bias.shape[0] // 2, HDT, rows), bf16)
    return pl.pallas_call(
        tokens_body,
        grid=(1,),
        in_specs=[SMEM] * 2 + [full(chain)] + [HBM] * 3,
        out_specs=full(out_shape),
        out_shape=out_shape,
        scratch_shapes=held((state, kv, bias))[:-1]
        + [pltpu.SemaphoreType.DMA((2 + kv.shape[0],))],
        compiler_params=pltpu.CompilerParams(vmem_limit_bytes=GRANT),
        cost_estimate=pl.CostEstimate(flops=10**9, bytes_accessed=2**22, transcendentals=2**19),
        name="tokens",
    )(place, strength, chain, state, kv, bias)


def update_body(
    place,
    tokens_ref,
    mine_ref,
    theirs_ref,
    exit_ref,
    tmid_ref,
    back_ref,
    mid_ref,
    tout_ref,
    aout_ref,
    gated_ref,
):
    even = lax.rem(place[1], 2) == 0
    for k in range(mine_ref.shape[0]):
        mine, theirs = mine_ref[k], theirs_ref[k]
        first = slice(2 * k * HDT, (2 * k + 1) * HDT)
        second = slice((2 * k + 1) * HDT, (2 * k + 2) * HDT)
        gated_ref[first, :] = jnp.where(even, mine, theirs)
        gated_ref[second, :] = jnp.where(even, theirs, mine)
    col = place[1]
    atoms, rows = aout_ref.shape[0], tmid_ref.shape[0]
    at = pl.multiple_of(col * atoms, atoms)
    added = dot_tn(gated_ref[...], exit_ref[...])
    update = (tmid_ref[...].astype(f32) + added).astype(bf16)
    tout_ref[...] = update
    sent = dot(update, back_ref[...]).astype(bf16)
    own = tokens_ref[...]
    onehot = (lax.broadcasted_iota(jnp.int32, (rows, atoms), 0) == own).astype(f32).astype(bf16)
    aout_ref[...] = (mid_ref[pl.ds(at, atoms), :].astype(f32) + dot_tn(onehot, sent)).astype(bf16)


def updates(place, gated, exit_w, tmid, back, mid, tokens, atoms):
    rows = tmid.shape[0]
    out_shape = [
        jax.ShapeDtypeStruct((rows, CS), bf16),
        jax.ShapeDtypeStruct((atoms, CA), bf16),
    ]
    return pl.pallas_call(
        update_body,
        grid=(1,),
        in_specs=[SMEM] + [VMEM] * 7,
        out_specs=[full(shape) for shape in out_shape],
        out_shape=out_shape,
        scratch_shapes=[pltpu.VMEM((CS, rows), bf16)],
        compiler_params=pltpu.CompilerParams(vmem_limit_bytes=16 * 2**20),
        name="updates",
    )(place, tokens, *gated, exit_w, tmid, back, mid)


def local(
    pair_tensor,
    token_single,
    atom_single,
    atom_token,
    chain_index,
    pair_up,
    pair_down,
    bias_heads,
    atom_gain,
    atom_proj,
    atom_exit,
    atom_pool,
    token_gain,
    token_proj,
    token_exit,
    chain_bias,
    token_back,
):
    rows, cols = pair_tensor.shape[:2]
    atom_rows = atom_single.shape[0]
    row_count = lax.axis_size("row")
    col_count = lax.axis_size("col")
    row = lax.axis_index("row")
    col = lax.axis_index("col")
    chips = col_count // 2
    row_atoms = atom_rows * col_count

    both = ("row", "col")
    at = lambda r, k, core: r * col_count + 2 * k + core
    last = col_count - 1

    last = col_count - 1
    halo = lax.ppermute(
        jnp.where(col == last, atom_single[-HALO:], atom_single[:HALO]),
        both,
        [(r * col_count + last, at(r + 1, r + 1, 0)) for r in range(row_count - 1)]
        + [((r + 1) * col_count, at(r, r, 1)) for r in range(row_count - 1)],
    )
    ext_tokens = lax.dynamic_slice_in_dim(
        jnp.pad(atom_token, (HALO, HALO)), row * row_atoms, row_atoms + 2 * HALO
    )
    ext_tokens = (ext_tokens - row * rows).reshape(-1, KW)
    own_tokens = lax.dynamic_slice_in_dim(
        atom_token, row * row_atoms + col * atom_rows, atom_rows
    )
    own_tokens = (own_tokens - row * rows)[None, :]

    flip = ((col == 2 * row + 1) | (col == 2 * row + 2)).astype(jnp.int32)
    place = jnp.stack([row, col, jnp.int32(row_count), flip]).astype(jnp.int32)
    center = jnp.asarray((np.eye(CZ) - 1.0 / CZ).astype(bf16))
    weights = (pair_up, pair_down, bias_heads.T, center)
    token_bias, band, edge = pair_rows(place, pair_tensor, weights, (), 0, PART, 2, True)
    halo, band, edge, token_bias, own_atoms = lax.optimization_barrier(
        (halo, band, edge, token_bias, atom_single)
    )

    here = col // 2 == row
    even = col % 2 == 0
    ring = chips // 2
    flat = lambda k, step: k // ring * ring + (k + step) % ring
    across = lambda k: (k + ring) % chips
    split = REACH - HALO
    band = jnp.where(even, band[:, :REACH], band[:, 2 * PART - REACH :])
    band = jnp.concatenate([band, halo.reshape(HA, HALO // HA, CA)], axis=1)
    none = jnp.zeros_like(band)
    place_in = lax.broadcasted_iota(jnp.int32, band.shape, 1)
    lane = lax.broadcasted_iota(jnp.int32, band.shape, 2)
    late = (place_in >= split) & (place_in < REACH) & (lane < HALO)
    early = (place_in < HALO) & (lane >= HALO)
    late_edge = jnp.concatenate([none[:, :split], edge, none[:, REACH:]], axis=1)
    early_edge = jnp.concatenate([edge, none[:, HALO:]], axis=1)
    band = jnp.where(jnp.where(even, late, early), none, band)
    edge = jnp.where(
        even, jnp.where(early, early_edge, none), jnp.where(late, late_edge, none)
    )
    band = jnp.where(here, band, edge)
    over_y = [
        (at(r, r, core), at(r, across(r), core)) for r in range(row_count) for core in range(2)
    ]
    beside = lambda to: [(at(r, r - 1, 1), at(r, to(r), 0)) for r in range(1, row_count)] + [
        (at(r, r + 1, 0), at(r, to(r), 1)) for r in range(row_count - 1)
    ]
    arrived = [
        lax.ppermute(band, both, over_y + beside(lambda r: r)),
        lax.ppermute(band, both, beside(across)),
    ]
    cores = [[at(0, k, core) for k in range(chips)] for core in range(2)]
    own_atoms = jnp.broadcast_to(own_atoms[None], (chips,) + own_atoms.shape)
    shards = lax.all_to_all(own_atoms, "col", 0, 0, axis_index_groups=cores)
    swap = [(i, i ^ 1) for i in range(col_count)]
    arrived = lax.optimization_barrier(arrived)
    band = jnp.where(here, band, none) + arrived[0] + arrived[1]
    band, token_bias = lax.optimization_barrier((band, token_bias))
    sent = [
        lax.ppermute(
            band,
            both,
            [
                (at(r, k, core), at(r, flat(k, step), core))
                for r in range(row_count)
                for k in (r, across(r))
                for core in range(2)
            ],
        )
        for step in range(1, ring)
    ]
    (token_bias,) = pair_rows(
        place, pair_tensor, weights, (token_bias,), 2 * PART, rows - 2 * PART, 1, False
    )
    theirs = lax.ppermute(shards, "col", swap)
    gain = token_gain.reshape(-1, KW)
    theirs, token_bias = lax.optimization_barrier((theirs, token_bias))
    head_bias = lax.all_to_all(token_bias, "col", 0, 0)
    sent, theirs, gain, ext_tokens = lax.optimization_barrier((sent, theirs, gain, ext_tokens))
    band = band + sent[0] + sent[1] + sent[2]
    other = lax.ppermute(band, "col", swap)

    atom_mid, token_mid, state, keyvals = atom_attention(
        place,
        (band, other),
        (shards, theirs),
        ext_tokens,
        atom_gain[None],
        atom_proj,
        atom_exit,
        atom_pool,
        token_single,
        gain,
        token_proj,
        row_count,
    )
    keyvals, head_bias = lax.optimization_barrier((keyvals, head_bias))
    keyvals = lax.all_to_all(keyvals, "row", 0, 0)
    gated = token_attention(place, state, keyvals, head_bias, chain_index[None], chain_bias)
    gated = lax.all_to_all(gated, "col", 0, 0, axis_index_groups=cores)
    gated = (gated, lax.ppermute(gated, "col", swap))
    return tuple(
        updates(
            place, gated, token_exit, token_mid, token_back, atom_mid, own_tokens, atom_rows
        )
    )


def solution(mesh):
    placed = (
        P("row", "col", None),
        P("row", None),
        P(("row", "col"), None),
    ) + (P(),) * 14
    return jax.shard_map(
        local,
        mesh=mesh,
        in_specs=placed,
        out_specs=(P("row", None), P(("row", "col"), None)),
        check_vma=False,
    )
```
